128 devices in a mesh: mesh: 16 (over y, x_hi, core), mode: 8 (over z, x_lo).
Axes of the slice: x: 4 (x_hi: 2, x_lo: 2; x = x_hi * 2 + x_lo), y: 4, z: 4, core: 2. Of those that a mesh axis runs over, the one named last changes fastest.
Arguments:
- mode_shapes: bfloat16 [4000, 3, 65536], P('mode', None, 'mesh'), may hold values from -0.09375 to 0.09375
- load_nodal: bfloat16 [3, 65536, 384], P(None, 'mesh'), may hold values from -0.125 to 0.125
- mode_freq: float32 [4000], P('mode'), may hold values from 1 to 4
- damping: float32 [4000], P('mode'), may hold values from 0.3 to 0.6
- drive_freq: float32 [4], replicated, may hold values from 1 to 4
- send_lists: int32 [2, 4096], P(None, 'mesh'), may hold values from 0 to 4095
- connectivity: int32 [8, 65536], P(None, ('mesh', 'mode')), may hold values from 0 to 4607
- shape_grads: float32 [3, 8, 65536], P(None, None, ('mesh', 'mode')), may hold values from -3 to 3
- modulus: float32 [65536], P(('mesh', 'mode')), may hold values from 0.7 to 1.4
Outputs:
- stress_spectra: float32 [4, 36, 65536], P(None, None, ('mesh', 'mode'))
The draws below stay inside these ranges and needn't reach their ends.
Inputs may be any that keep to these rules, and one draw needn't show every extreme that they name: `connectivity`: numbers below 4096 are the partition's own nodes, then 256 nodes received from the partition before, then 256 from the one after. `send_lists`: each entry is a node of the sending partition in its own numbering.
All inputs are finite; a program needn't handle non-finite values.
Results may differ from the reference program's by a relative error of at most 0.012.
Values may be sent and summed in bfloat16 or wider, within the bound.
No kernel may reach another device: no remote copies, remote signals or barrier semaphores. Data moves between devices by JAX's collectives and lax.ppermute only.
A program may use at most 128 MiB of HBM per device.

```python
import math
import jax
import jax.numpy as jnp
from jax import lax

NODE_DEV = 4096
MODE_DEV = 500
LOADS = 48
FREQS = 4
MODES = 4000
COLS = 384
BOUND = 256
ELEM_DEV = 512
NODES = 65536
ELEMS = 65536
N_MESH = 16
N_MODE = 8


def with_ends(result, key, least, largest):
    longest = result.shape.index(max(result.shape))
    spots = []
    for shift in (0, 1):
        where = [jax.random.randint(jax.random.fold_in(key, axis), (), 0, length) for axis, length in enumerate(result.shape)]
        where[longest] = (where[longest] + shift) % result.shape[longest]
        spots.append(tuple(where))
    return result.at[spots[0]].set(least).at[spots[1]].set(largest)


def levels(stream_key, shape, cuts, least, high):
    def one(axis_at, parts):
        heights = jax.random.uniform(jax.random.fold_in(jax.random.fold_in(stream_key, 6), axis_at), (parts,), jnp.float32, least / len(cuts), high / len(cuts))
        return jnp.repeat(jnp.exp(heights), shape[axis_at] // parts).reshape((-1,) + (1,) * (len(shape) - axis_at - 1))

    level = one(*cuts[0])
    for cut in cuts[1:]:
        level = level * one(*cut)
    return level


def normal_values(key, dims, scale, limit, cuts=(), kind=jnp.bfloat16):
    level = levels(key, dims, cuts, -0.22, 0.18) if cuts else 1.0
    array = jax.random.normal(key, dims, jnp.float32) * scale * level
    return jnp.minimum(jnp.maximum(array, -limit), limit).astype(kind)


def setup_inputs(seed: int = 0) -> dict:
    arg_keys = jax.random.split(jax.random.key(seed), 10)
    mode_shapes = normal_values(arg_keys[0], (MODES, 3, NODES), MODES ** -0.5, 0.09375, ((0, 8), (2, 16)))
    load_nodal = normal_values(arg_keys[1], (3, NODES, COLS), (3 * NODES * LOADS // MODES) ** -0.5, 0.125, ((1, 16),))
    mode_freq = jnp.clip(jnp.exp(math.log(4.0) - 1.3862944 * jax.random.uniform(arg_keys[2], (MODES,), jnp.float32) ** levels(arg_keys[2], (MODES,), ((0, 8),), -0.2, 0.2)), 1.0, 4.0)
    damping = jnp.clip(jnp.exp(math.log(0.6) - 0.6931472 * jax.random.uniform(arg_keys[3], (MODES,), jnp.float32) ** levels(arg_keys[3], (MODES,), ((0, 8),), -0.2, 0.2)), 0.3, 0.6)
    drive_freq = jnp.clip(jnp.exp(jax.random.uniform(arg_keys[4], (FREQS,), jnp.float32, math.log(1.0), math.log(4.0))), 1.0, 4.0)
    send_lists = with_ends(jax.random.randint(arg_keys[5], (2, BOUND * N_MESH), 0, NODE_DEV), jax.random.fold_in(arg_keys[5], 1), 0, NODE_DEV - 1).astype(jnp.int32)
    connectivity = with_ends(jax.random.randint(arg_keys[6], (8, ELEMS), 0, NODE_DEV + 2 * BOUND), jax.random.fold_in(arg_keys[6], 1), 0, (NODE_DEV + 2 * BOUND) - 1).astype(jnp.int32)
    shape_grads = normal_values(arg_keys[7], (3, 8, ELEMS), 0.5, 3.0, ((2, 128),), jnp.float32)
    modulus = jnp.clip(jnp.exp(math.log(1.4) - 0.6931472 * jax.random.uniform(arg_keys[8], (ELEMS,), jnp.float32) ** levels(arg_keys[8], (ELEMS,), ((0, 128),), -0.2, 0.2)), 0.7, 1.4)
    return dict(mode_shapes=mode_shapes, load_nodal=load_nodal, mode_freq=mode_freq, damping=damping, drive_freq=drive_freq, send_lists=send_lists, connectivity=connectivity, shape_grads=shape_grads, modulus=modulus)


POISSON = 0.3


def transfer_factor(mode_freq, damping, drive_freq):
    natural = mode_freq[:, None]
    forcing = drive_freq[None, :]
    real_gap = natural * natural - forcing * forcing
    loss_term = 2.0 * damping[:, None] * natural * forcing
    magnitude = real_gap * real_gap + loss_term * loss_term
    return real_gap / magnitude, -loss_term / magnitude


def apply_factor(load_pairs, factor_re, factor_im):
    load_re = load_pairs[..., 0]
    load_im = load_pairs[..., 1]
    out_re = factor_re * load_re - factor_im * load_im
    out_im = factor_re * load_im + factor_im * load_re
    return jnp.stack([out_re, out_im], axis=-1)


def element_spectra(local_nodes, connectivity, shape_grads, modulus, freq_count):
    corners, elem_count = connectivity.shape
    col_count = local_nodes.shape[2]
    picked = jnp.take(local_nodes, connectivity.reshape(-1), axis=1).reshape(3, corners, elem_count, col_count)
    disp_grad = jnp.einsum("caek,dae->cdek", picked.astype(jnp.float32), shape_grads, precision=lax.Precision.HIGHEST)
    lame_first = (modulus * (POISSON / ((1.0 + POISSON) * (1.0 - 2.0 * POISSON))))[:, None]
    shear_mod = (modulus * (1.0 / (2.0 * (1.0 + POISSON))))[:, None]
    volume_strain = disp_grad[0, 0] + disp_grad[1, 1] + disp_grad[2, 2]
    stress = jnp.stack([
        lame_first * volume_strain + 2.0 * shear_mod * disp_grad[0, 0],
        lame_first * volume_strain + 2.0 * shear_mod * disp_grad[1, 1],
        lame_first * volume_strain + 2.0 * shear_mod * disp_grad[2, 2],
        shear_mod * (disp_grad[1, 2] + disp_grad[2, 1]),
        shear_mod * (disp_grad[2, 0] + disp_grad[0, 2]),
        shear_mod * (disp_grad[0, 1] + disp_grad[1, 0]),
    ], axis=0)
    stress_parts = stress.reshape(6, elem_count, freq_count, col_count // (2 * freq_count), 2)
    real_part = stress_parts[..., 0]
    imag_part = stress_parts[..., 1]
    entries = []
    for row_index in range(6):
        for col_index in range(row_index, 6):
            entries.append(jnp.sum(real_part[row_index] * real_part[col_index] + imag_part[row_index] * imag_part[col_index], axis=-1))
    for row_index in range(6):
        for col_index in range(row_index + 1, 6):
            entries.append(jnp.sum(imag_part[row_index] * real_part[col_index] - real_part[row_index] * imag_part[col_index], axis=-1))
    return jnp.transpose(jnp.stack(entries, axis=0), (2, 0, 1))


def reference(mode_shapes, load_nodal, mode_freq, damping, drive_freq, send_lists, connectivity, shape_grads, modulus):
    modal_load = jnp.dot(mode_shapes.reshape(MODES, 3 * NODES), load_nodal.reshape(3 * NODES, COLS), preferred_element_type=jnp.float32)
    factor_re, factor_im = transfer_factor(mode_freq, damping, drive_freq)
    response = apply_factor(modal_load.reshape(MODES, FREQS, LOADS, 2), factor_re[:, :, None], factor_im[:, :, None])
    response = response.reshape(MODES, COLS).astype(jnp.bfloat16)
    total_disp = jnp.zeros((3 * NODES, COLS), jnp.float32)
    for block_index in range(N_MODE):
        shapes_block = mode_shapes[block_index * MODE_DEV:(block_index + 1) * MODE_DEV].reshape(MODE_DEV, 3 * NODES)
        partial_value = jnp.dot(shapes_block.T, response[block_index * MODE_DEV:(block_index + 1) * MODE_DEV], preferred_element_type=jnp.float32)
        rounded = lax.optimization_barrier(partial_value.astype(jnp.bfloat16))
        total_disp = total_disp + rounded.astype(jnp.float32)
    displacement = total_disp.astype(jnp.bfloat16).reshape(3, N_MESH, NODE_DEV, COLS)
    send_rows = send_lists.reshape(2, N_MESH, BOUND)

    def pick_sent(node_block, index_block):
        return jnp.take(node_block, index_block.reshape(-1), axis=1).reshape(3, 2, BOUND, COLS)

    outgoing = jax.vmap(pick_sent, in_axes=(1, 1))(displacement, send_rows)
    zero_rim = jnp.zeros((1, 3, BOUND, COLS), jnp.bfloat16)
    from_before = jnp.concatenate([zero_rim, outgoing[:-1, :, 1]], axis=0)
    from_after = jnp.concatenate([outgoing[1:, :, 0], zero_rim], axis=0)
    own_nodes = jnp.transpose(displacement, (1, 0, 2, 3))
    local_nodes = jnp.concatenate([own_nodes, from_before, from_after], axis=2)
    elem_part = ELEM_DEV * N_MODE
    conn_parts = jnp.transpose(connectivity.reshape(8, N_MESH, elem_part), (1, 0, 2))
    grad_parts = jnp.transpose(shape_grads.reshape(3, 8, N_MESH, elem_part), (2, 0, 1, 3))
    modulus_parts = modulus.reshape(N_MESH, elem_part)
    spectra = lax.map(lambda pieces: element_spectra(pieces[0], pieces[1], pieces[2], pieces[3], FREQS), (local_nodes, conn_parts, grad_parts, modulus_parts))
    return jnp.transpose(spectra, (1, 2, 0, 3)).reshape(FREQS, 36, ELEMS)
```

```python
import functools

import jax
import jax.numpy as jnp
from jax import lax
from jax.experimental import pallas as pl
from jax.experimental.pallas import tpu as pltpu
from jax.sharding import PartitionSpec as P

POISSON = 0.3
F32 = jnp.float32
BF16 = jnp.bfloat16
MIB = 1024 * 1024
Z, XLO = 4, 2
Y, XHI, CORE = 4, 2, 2
HALF = 256


def params(mib):
    return pltpu.CompilerParams(vmem_limit_bytes=mib * MIB)


def mode_index(z, x):
    return (z % Z) * XLO + x


def mesh_index(y, h, c):
    return ((y % Y) * XHI + h) * CORE + c


def mode_perm(dz, flip=0):
    return [(mode_index(z, x), mode_index(z + dz, x ^ flip)) for z in range(Z) for x in range(XLO)]


def mesh_perm(dy, flip_h=0, flip_c=0):
    return [
        (mesh_index(y, h, c), mesh_index(y + dy, h ^ flip_h, c ^ flip_c))
        for y in range(Y)
        for h in range(XHI)
        for c in range(CORE)
    ]


def loads_kernel(core_ref, shapes_ref, load_ref, mine_ref, theirs_ref, acc):
    step = pl.program_id(0)
    modes = shapes_ref.shape[1]

    @pl.when(step == 0)
    def _():
        acc[...] = jnp.zeros_like(acc)

    acc[:modes, :] += jnp.dot(shapes_ref[0], load_ref[0], preferred_element_type=F32)

    @pl.when(step == pl.num_programs(0) - 1)
    def _():
        core = core_ref[0]
        mine_ref[...] = acc[pl.ds(core * HALF, HALF), :]
        theirs_ref[...] = acc[pl.ds((1 - core) * HALF, HALF), :].astype(BF16)


def partial_loads(core, shapes, load):
    comps, modes, nodes = shapes.shape
    cols = load.shape[2]
    block = 1024
    per = nodes // block
    return pl.pallas_call(
        loads_kernel,
        out_shape=(
            jax.ShapeDtypeStruct((HALF, cols), F32),
            jax.ShapeDtypeStruct((HALF, cols), BF16),
        ),
        grid=(comps * per,),
        in_specs=[
            pl.BlockSpec(memory_space=pltpu.SMEM),
            pl.BlockSpec((1, modes, block), lambda i: (i // per, 0, i % per)),
            pl.BlockSpec((1, block, cols), lambda i: (i // per, i % per, 0)),
        ],
        out_specs=(
            pl.BlockSpec((HALF, cols), lambda i: (0, 0)),
            pl.BlockSpec((HALF, cols), lambda i: (0, 0)),
        ),
        scratch_shapes=[pltpu.VMEM((2 * HALF, cols), F32)],
        compiler_params=params(32),
        cost_estimate=pl.CostEstimate(
            flops=2 * modes * comps * nodes * cols,
            bytes_accessed=2 * comps * nodes * (modes + cols),
            transcendentals=0,
        ),
        name="modal_loads",
    )(core, shapes, load)


def response_kernel(a_ref, b_ref, c_ref, d_ref, direct_ref, cross_ref, out_ref):
    total = (
        a_ref[...].astype(F32)
        + b_ref[...].astype(F32)
        + c_ref[...].astype(F32)
        + d_ref[...].astype(F32)
    )
    cols = total.shape[1]
    even = lax.broadcasted_iota(jnp.int32, total.shape, 1) % 2 == 0
    other = jnp.where(even, pltpu.roll(total, cols - 1, 1), pltpu.roll(total, 1, 1))
    out_ref[...] = (direct_ref[...] * total + cross_ref[...] * other).astype(BF16)


def half_response(parts, direct, cross):
    return pl.pallas_call(
        response_kernel,
        out_shape=jax.ShapeDtypeStruct(direct.shape, BF16),
        compiler_params=params(32),
        name="modal_response",
    )(*parts, direct, cross)


def disp_kernel(core_ref, mine_ref, theirs_ref, order_ref, shapes_ref, out_ref, mark_ref, resp, resp_t):
    modes = shapes_ref.shape[1]

    @pl.when(pl.program_id(0) == 0)
    def _():
        core = core_ref[0]
        resp[pl.ds(core * HALF, HALF), :] = mine_ref[...]
        resp[pl.ds((1 - core) * HALF, HALF), :] = theirs_ref[...]
        turned = lax.dot_general(
            order_ref[...], resp[...], (((1,), (1,)), ((), ())), preferred_element_type=F32
        )
        resp_t[...] = turned[:, :modes].astype(BF16)
        mark_ref[...] = jnp.zeros_like(mark_ref)

    value = jnp.dot(resp_t[...], shapes_ref[0], preferred_element_type=F32)
    parts, _, rows, width = out_ref.shape
    out_ref[...] = value.astype(BF16).reshape(parts, 1, rows, width)


def partial_disp(core, mine, theirs, order, shapes, parts):
    comps, modes, nodes = shapes.shape
    cols = mine.shape[1]
    rows = cols // parts
    block = 1024
    per = nodes // block
    return pl.pallas_call(
        disp_kernel,
        out_shape=(
            jax.ShapeDtypeStruct((parts, comps, rows, nodes), BF16),
            jax.ShapeDtypeStruct((8, 128), F32),
        ),
        grid=(comps * per,),
        in_specs=[
            pl.BlockSpec(memory_space=pltpu.SMEM),
            pl.BlockSpec((HALF, cols), lambda i: (0, 0)),
            pl.BlockSpec((HALF, cols), lambda i: (0, 0)),
            pl.BlockSpec((cols, cols), lambda i: (0, 0)),
            pl.BlockSpec((1, modes, block), lambda i: (i // per, 0, i % per)),
        ],
        out_specs=(
            pl.BlockSpec((parts, 1, rows, block), lambda i: (0, i // per, 0, i % per)),
            pl.BlockSpec((8, 128), lambda i: (0, 0)),
        ),
        scratch_shapes=[pltpu.VMEM((2 * HALF, cols), BF16), pltpu.VMEM((cols, modes), BF16)],
        compiler_params=params(32),
        cost_estimate=pl.CostEstimate(
            flops=2 * modes * comps * nodes * cols,
            bytes_accessed=2 * comps * nodes * (modes + cols),
            transcendentals=0,
        ),
        name="mode_displacement",
    )(core, mine, theirs, order, shapes)


NODE_BLOCK = 256
ROWS = 16


def weights_kernel(mark_ref, conn_ref, grads_ref, out_ref):
    del mark_ref
    first = (pl.program_id(0) * NODE_BLOCK).astype(F32)
    corners, width = conn_ref.shape
    lanes = 128
    base = lax.broadcasted_iota(jnp.int32, (ROWS, lanes), 0).astype(F32).astype(BF16)
    for piece in range(width // lanes):
        cut = pl.ds(piece * lanes, lanes)
        keys = (conn_ref[:, cut] - first).astype(BF16)
        grads = grads_ref[:, cut].astype(BF16)
        key = [jnp.broadcast_to(keys[a : a + 1, :], (ROWS, lanes)) for a in range(corners)]
        grad = [jnp.broadcast_to(grads[i : i + 1, :], (ROWS, lanes)) for i in range(3 * corners)]
        zero = jnp.zeros((ROWS, lanes), BF16)
        for row in range(NODE_BLOCK // ROWS):
            node = base + BF16(row * ROWS)
            sums = [None] * 3
            for a in range(corners):
                hit = node == key[a]
                for d in range(3):
                    term = jnp.where(hit, grad[d * corners + a], zero)
                    sums[d] = term if a == 0 else sums[d] + term
            for d in range(3):
                out_ref[d, pl.ds(row * ROWS, ROWS), cut] = sums[d]


def element_weights(mark, conn, grads, nodes):
    corners, elems = conn.shape
    width = 512
    return pl.pallas_call(
        weights_kernel,
        out_shape=jax.ShapeDtypeStruct((3, nodes, elems), BF16),
        grid=(nodes // NODE_BLOCK, elems // width),
        in_specs=[
            pl.BlockSpec(memory_space=pl.ANY),
            pl.BlockSpec((corners, width), lambda i, j: (0, j)),
            pl.BlockSpec((3 * corners, width), lambda i, j: (0, j)),
        ],
        out_specs=pl.BlockSpec((3, NODE_BLOCK, width), lambda i, j: (0, i, j)),
        compiler_params=params(32),
        cost_estimate=pl.CostEstimate(
            flops=6 * corners * nodes * elems * 20,
            bytes_accessed=6 * nodes * elems,
            transcendentals=0,
        ),
        name="element_weights",
    )(mark, conn, grads)


def spectra_kernel(own_ref, oth_ref, own_rim_ref, oth_rim_ref, weights_ref, modulus_ref, out_ref):
    inner = own_ref.shape[1]
    rows = own_ref.shape[0] // 3
    half = rows // 2
    width = weights_ref.shape[2]
    lame = modulus_ref[...] * (POISSON / ((1.0 + POISSON) * (1.0 - 2.0 * POISSON)))
    shear = modulus_ref[...] * (1.0 / (2.0 * (1.0 + POISSON)))
    real = [[0.0] * 6 for _ in range(6)]
    imag = [[0.0] * 6 for _ in range(6)]
    for values, rim in ((own_ref, own_rim_ref), (oth_ref, oth_rim_ref)):
        grads = []
        for d in range(3):
            grads.append(
                jnp.dot(values[...], weights_ref[d, :inner, :], preferred_element_type=F32)
                + jnp.dot(rim[...], weights_ref[d, inner:, :], preferred_element_type=F32)
            )

        def at(c, d):
            return grads[d][c * rows : (c + 1) * rows, :]

        volume = lame * (at(0, 0) + at(1, 1) + at(2, 2))
        twice = 2.0 * shear
        stress = [
            volume + twice * at(0, 0),
            volume + twice * at(1, 1),
            volume + twice * at(2, 2),
            shear * (at(1, 2) + at(2, 1)),
            shear * (at(2, 0) + at(0, 2)),
            shear * (at(0, 1) + at(1, 0)),
        ]
        re = [s[:half, :] for s in stress]
        im = [s[half:, :] for s in stress]

        def fold(x):
            return sum(x[8 * i : 8 * i + 8, :] for i in range(half // 8))

        for i in range(6):
            for j in range(i, 6):
                real[i][j] = real[i][j] + fold(re[i] * re[j] + im[i] * im[j])
            for j in range(i + 1, 6):
                imag[i][j] = imag[i][j] + fold(im[i] * re[j] - re[i] * im[j])
    entry = 0
    for i in range(6):
        for j in range(i, 6):
            out_ref[0, entry : entry + 1, :] = jnp.sum(real[i][j], axis=0, keepdims=True)
            entry += 1
    for i in range(6):
        for j in range(i + 1, 6):
            out_ref[0, entry : entry + 1, :] = jnp.sum(imag[i][j], axis=0, keepdims=True)
            entry += 1


def element_spectra(own, oth, own_rim, oth_rim, weights, modulus, groups):
    rows, inner = own.shape
    rim = own_rim.shape[1]
    elems = weights.shape[2]
    width = 256
    per = elems // groups // width
    whole = lambda i: (0, 0)
    return pl.pallas_call(
        spectra_kernel,
        out_shape=jax.ShapeDtypeStruct((groups, 36, elems // groups), F32),
        grid=(elems // width,),
        in_specs=[
            pl.BlockSpec((rows, inner), whole),
            pl.BlockSpec((rows, inner), whole),
            pl.BlockSpec((rows, rim), whole),
            pl.BlockSpec((rows, rim), whole),
            pl.BlockSpec((3, inner + rim, width), lambda i: (0, 0, i)),
            pl.BlockSpec((1, width), lambda i: (0, i)),
        ],
        out_specs=pl.BlockSpec((1, 36, width), lambda i: (i // per, 0, i % per)),
        compiler_params=params(48),
        cost_estimate=pl.CostEstimate(
            flops=2 * 6 * rows * (inner + rim) * elems,
            bytes_accessed=6 * (inner + rim) * elems,
            transcendentals=0,
        ),
        name="element_spectra",
    )(own, oth, own_rim, oth_rim, weights, modulus)


def local(
    mode_shapes,
    load_nodal,
    mode_freq,
    damping,
    drive_freq,
    send_lists,
    connectivity,
    shape_grads,
    modulus,
):
    modes, comps, nodes = mode_shapes.shape
    cols = load_nodal.shape[2]
    bound = send_lists.shape[1]
    freqs = drive_freq.shape[0]
    parts = Z * XLO
    rows = cols // parts
    mesh_at = lax.axis_index("mesh")
    z_at = lax.axis_index("mode") // XLO
    core = (mesh_at % CORE).astype(jnp.int32)
    core_arg = core.reshape(1)
    shapes = jnp.transpose(mode_shapes, (1, 0, 2))

    mesh_data = jnp.concatenate(
        [
            connectivity.astype(F32),
            shape_grads.reshape(-1, shape_grads.shape[2]),
            modulus[None, :],
        ],
        axis=0,
    )
    near = [mesh_data] + [lax.ppermute(mesh_data, "mode", mode_perm(-j)) for j in range(1, Z)]
    mesh_all = jnp.concatenate(near, axis=1)

    pad = 2 * HALF - modes
    natural = jnp.pad(mode_freq, (0, pad), constant_values=1.0)[:, None]
    loss = jnp.pad(damping, (0, pad), constant_values=0.5)[:, None]
    natural = lax.dynamic_slice_in_dim(natural, core * HALF, HALF)
    loss = lax.dynamic_slice_in_dim(loss, core * HALF, HALF)
    forcing = jnp.repeat(drive_freq, cols // freqs)[None, :]
    gap = natural * natural - forcing * forcing
    damp = 2.0 * loss * natural * forcing
    size = gap * gap + damp * damp
    sign = jnp.where(jnp.arange(cols) % 2 == 0, 1.0, -1.0).astype(F32)[None, :]
    direct = gap / size
    cross = sign * (damp / size)

    mine, theirs = partial_loads(core_arg, shapes, load_nodal)
    got = lax.ppermute(theirs, "mesh", mesh_perm(0, 0, 1))
    chip = (mine + got.astype(F32)).astype(BF16)
    got = lax.ppermute(chip, "mesh", mesh_perm(0, 1, 0))
    pair = (chip.astype(F32) + got.astype(F32)).astype(BF16)
    ring = [pair] + [lax.ppermute(pair, "mesh", mesh_perm(dy)) for dy in range(1, Y)]
    resp_mine = half_response(ring, direct, cross)
    resp_theirs = lax.ppermute(resp_mine, "mesh", mesh_perm(0, 0, 1))

    spot = jnp.arange(cols)
    block, inside = spot // rows, spot % rows
    source = block * rows + 2 * (inside % (rows // 2)) + inside // (rows // 2)
    order = (source[:, None] == spot[None, :]).astype(BF16)

    terms, mark = partial_disp(core_arg, resp_mine, resp_theirs, order, shapes, parts)
    terms = lax.all_to_all(terms, "mode", 0, 0)

    weights = element_weights(mark, mesh_all[:8], mesh_all[8:32], nodes + 2 * bound)
    pick = (send_lists.reshape(1, -1) == jnp.arange(nodes)[:, None]).astype(BF16)

    own = jnp.sum(terms.astype(F32), axis=0).astype(BF16).reshape(comps * rows, nodes)
    oth = lax.ppermute(own, "mode", mode_perm(0, 1))
    rim = jnp.dot(own, pick, preferred_element_type=F32).astype(BF16)

    count = lax.axis_size("mesh")

    def beside(values, step, flip):
        perm = []
        for p in range(count):
            if 0 <= p + step < count:
                for z in range(Z):
                    for x in range(XLO):
                        perm.append(
                            (p * parts + mode_index(z, x), (p + step) * parts + mode_index(z, x ^ flip))
                        )
        return lax.ppermute(values, ("mesh", "mode"), perm)

    before, after = rim[:, bound:], rim[:, :bound]
    own_rim = jnp.concatenate([beside(before, 1, 0), beside(after, -1, 0)], axis=1)
    oth_rim = jnp.concatenate([beside(before, 1, 1), beside(after, -1, 1)], axis=1)

    spectra = element_spectra(own, oth, own_rim, oth_rim, weights, mesh_all[32:33], Z)
    back = [spectra[0]] + [lax.ppermute(spectra[j], "mode", mode_perm(j)) for j in range(1, Z)]
    back = jnp.stack(back)
    return jnp.take(back, (z_at - jnp.arange(Z)) % Z, axis=0)


def solution(mesh):
    in_specs = (
        P("mode", None, "mesh"),
        P(None, "mesh", None),
        P("mode"),
        P("mode"),
        P(),
        P(None, "mesh"),
        P(None, ("mesh", "mode")),
        P(None, None, ("mesh", "mode")),
        P(("mesh", "mode")),
    )
    out_specs = P(None, None, ("mesh", "mode"))
    return jax.shard_map(local, mesh=mesh, in_specs=in_specs, out_specs=out_specs, check_vma=False)
```

```python
import functools

import jax
import jax.numpy as jnp
from jax import lax
from jax.experimental import pallas as pl
from jax.experimental.pallas import tpu as pltpu
from jax.sharding import PartitionSpec as P

POISSON = 0.3
F32 = jnp.float32
BF16 = jnp.bfloat16
MIB = 1024 * 1024
Z, XLO = 4, 2
Y, XHI, CORE = 4, 2, 2
HALF = 256
CHUNK = 1024
ANY = pl.BlockSpec(memory_space=pl.ANY)
SMEM = pl.BlockSpec(memory_space=pltpu.SMEM)


def params(mib):
    return pltpu.CompilerParams(vmem_limit_bytes=mib * MIB)


def cost(flops, moved):
    return pl.CostEstimate(flops=int(flops), bytes_accessed=int(moved), transcendentals=0)


def shaped(shape, kind):
    return jax.ShapeDtypeStruct(shape, kind)


def mode_index(z, x):
    return (z % Z) * XLO + x


def mesh_index(y, h, c):
    return ((y % Y) * XHI + h) * CORE + c


def mode_perm(dz, flip=0):
    return [(mode_index(z, x), mode_index(z + dz, x ^ flip)) for z in range(Z) for x in range(XLO)]


def mesh_perm(dy, flip_h=0, flip_c=0):
    return [
        (mesh_index(y, h, c), mesh_index(y + dy, h ^ flip_h, c ^ flip_c))
        for y in range(Y)
        for h in range(XHI)
        for c in range(CORE)
    ]


def loads_kernel(core_ref, shapes_ref, load_ref, mine_ref, theirs_ref, acc):
    step = pl.program_id(0)
    modes = shapes_ref.shape[1]

    @pl.when(step == 0)
    def _():
        acc[...] = jnp.zeros_like(acc)

    acc[:modes, :] += jnp.dot(shapes_ref[0], load_ref[0], preferred_element_type=F32)

    @pl.when(step == pl.num_programs(0) - 1)
    def _():
        core = core_ref[0]
        mine_ref[...] = acc[pl.ds(core * HALF, HALF), :]
        theirs_ref[...] = acc[pl.ds((1 - core) * HALF, HALF), :].astype(BF16)


def partial_loads(core, shapes, load):
    comps, modes, nodes = shapes.shape
    cols = load.shape[2]
    block = 2048
    per = nodes // block
    return pl.pallas_call(
        loads_kernel,
        out_shape=(shaped((HALF, cols), F32), shaped((HALF, cols), BF16)),
        grid=(comps * per,),
        in_specs=[
            SMEM,
            pl.BlockSpec((1, modes, block), lambda i: (i // per, 0, i % per)),
            pl.BlockSpec((1, block, cols), lambda i: (i // per, i % per, 0)),
        ],
        out_specs=(
            pl.BlockSpec((HALF, cols), lambda i: (0, 0)),
            pl.BlockSpec((HALF, cols), lambda i: (0, 0)),
        ),
        scratch_shapes=[pltpu.VMEM((2 * HALF, cols), F32)],
        compiler_params=params(56),
        cost_estimate=cost(2 * modes * comps * nodes * cols, 2 * comps * nodes * (modes + cols)),
        name="modal_loads",
    )(core, shapes, load)


def response_kernel(a_ref, b_ref, c_ref, d_ref, direct_ref, cross_ref, out_ref):
    total = (
        a_ref[...].astype(F32)
        + b_ref[...].astype(F32)
        + c_ref[...].astype(F32)
        + d_ref[...].astype(F32)
    )
    cols = total.shape[1]
    even = lax.broadcasted_iota(jnp.int32, total.shape, 1) % 2 == 0
    other = jnp.where(even, pltpu.roll(total, cols - 1, 1), pltpu.roll(total, 1, 1))
    out_ref[...] = (direct_ref[...] * total + cross_ref[...] * other).astype(BF16)


def half_response(parts, direct, cross):
    return pl.pallas_call(
        response_kernel,
        out_shape=shaped(direct.shape, BF16),
        compiler_params=params(32),
        cost_estimate=cost(direct.size * 8, direct.size * 18),
        name="modal_response",
    )(*parts, direct, cross)


def element_data_kernel(mark_ref, conn_ref, grads_ref, modulus_ref, out_ref):
    del mark_ref
    corners, width = conn_ref.shape
    conn = conn_ref[...].astype(F32)
    out_ref[:corners, :] = conn
    for d in range(3):
        total = jnp.zeros((corners, width), F32)
        for a in range(corners):
            total = total + jnp.where(conn == conn[a : a + 1, :], grads_ref[d, a : a + 1, :], 0.0)
        out_ref[(d + 1) * corners : (d + 2) * corners, :] = total
    out_ref[4 * corners :, :] = jnp.broadcast_to(modulus_ref[...], (corners, width))


def element_data(mark, conn, grads, modulus):
    corners, elems = conn.shape
    vmem = pl.BlockSpec(memory_space=pltpu.VMEM)
    return pl.pallas_call(
        element_data_kernel,
        out_shape=shaped((5 * corners, elems), F32),
        in_specs=[ANY, vmem, vmem, vmem],
        out_specs=vmem,
        compiler_params=params(32),
        cost_estimate=cost(1000, elems * 4 * 80),
        name="element_data",
    )(mark, conn, grads, modulus[None, :])


def split_ways(blocks, plus_ref, minus_ref, up_ref, down_ref, own_ref):
    half = up_ref.shape[-1]
    low = [b[..., :half] for b in blocks]
    high = [b[..., half:] for b in blocks]
    plus_ref[0, 0] = low[2]
    plus_ref[1, 0] = high[1]
    minus_ref[0, 0] = high[2]
    minus_ref[1, 0] = low[3]
    up_ref[0] = low[1]
    down_ref[0] = high[3]
    own_ref[0] = blocks[0]


def way_shapes(comps, rows, width):
    half = width // 2
    shapes = (
        (2, comps, rows, half),
        (2, comps, rows, half),
        (comps, rows, half),
        (comps, rows, half),
        (comps, rows, width),
    )
    specs = tuple(
        pl.BlockSpec((2, 1) + s[2:], lambda i: (0, i, 0, 0))
        if len(s) == 4
        else pl.BlockSpec((1,) + s[1:], lambda i: (i, 0, 0))
        for s in shapes
    )
    return tuple(shaped(s, BF16) for s in shapes), specs


def z_first_kernel(mark_ref, resp_ref, shapes_ref, *out_refs):
    del mark_ref
    value = jnp.dot(resp_ref[...], shapes_ref[0], preferred_element_type=F32).astype(BF16)
    rows = value.shape[0] // Z
    split_ways([value[j * rows : (j + 1) * rows, :] for j in range(Z)], *out_refs)


def z_first_terms(mark, resp, shapes, chunk):
    comps, modes, _ = shapes.shape
    cols = resp.shape[0]
    out_shape, out_specs = way_shapes(comps, cols // Z, CHUNK)
    return pl.pallas_call(
        z_first_kernel,
        out_shape=out_shape,
        grid=(comps,),
        in_specs=[
            ANY,
            pl.BlockSpec((cols, modes), lambda i: (0, 0)),
            pl.BlockSpec((1, modes, CHUNK), lambda i: (i, 0, chunk)),
        ],
        out_specs=out_specs,
        compiler_params=params(52),
        cost_estimate=cost(2 * modes * comps * CHUNK * cols, 2 * comps * CHUNK * (modes + cols)),
        name="z_first_terms",
    )(mark, resp, shapes)


def x_first_kernel(core_ref, mine_ref, theirs_ref, order_ref, shapes_ref, away_ref, keep_ref, turned_ref, resp):
    modes = shapes_ref.shape[1]

    @pl.when(pl.program_id(0) == 0)
    def _():
        core = core_ref[0]
        resp[pl.ds(core * HALF, HALF), :] = mine_ref[...]
        resp[pl.ds((1 - core) * HALF, HALF), :] = theirs_ref[...]
        turned = lax.dot_general(
            order_ref[...], resp[...], (((1,), (1,)), ((), ())), preferred_element_type=F32
        )
        turned_ref[...] = turned[:, :modes].astype(BF16)

    value = jnp.dot(turned_ref[...], shapes_ref[0], preferred_element_type=F32).astype(BF16)
    rows = value.shape[0] // (Z * XLO)
    for j in range(Z):
        keep_ref[j, 0] = value[(2 * j) * rows : (2 * j + 1) * rows, :]
        away_ref[j, 0] = value[(2 * j + 1) * rows : (2 * j + 2) * rows, :]


def x_first_terms(core, mine, theirs, order, shapes, chunk):
    comps, modes, _ = shapes.shape
    cols = mine.shape[1]
    rows = cols // (Z * XLO)
    part = pl.BlockSpec((Z, 1, rows, CHUNK), lambda i: (0, i, 0, 0))
    whole = lambda i: (0, 0)
    return pl.pallas_call(
        x_first_kernel,
        out_shape=(
            shaped((Z, comps, rows, CHUNK), BF16),
            shaped((Z, comps, rows, CHUNK), BF16),
            shaped((cols, modes), BF16),
        ),
        grid=(comps,),
        in_specs=[
            SMEM,
            pl.BlockSpec((HALF, cols), whole),
            pl.BlockSpec((HALF, cols), whole),
            pl.BlockSpec((cols, cols), whole),
            pl.BlockSpec((1, modes, CHUNK), lambda i: (i, 0, chunk)),
        ],
        out_specs=(part, part, pl.BlockSpec((cols, modes), whole)),
        scratch_shapes=[pltpu.VMEM((2 * HALF, cols), BF16)],
        compiler_params=params(52),
        cost_estimate=cost(2 * modes * comps * CHUNK * cols, 2 * comps * CHUNK * (modes + cols)),
        name="x_first_terms",
    )(core, mine, theirs, order, shapes)


def x_sum_kernel(keep_ref, got_ref, *out_refs):
    blocks = [(keep_ref[j, 0].astype(F32) + got_ref[j, 0].astype(F32)).astype(BF16) for j in range(Z)]
    split_ways(blocks, *out_refs)


def x_sum(keep, got):
    _, comps, rows, width = keep.shape
    out_shape, out_specs = way_shapes(comps, rows, width)
    part = pl.BlockSpec((Z, 1, rows, width), lambda i: (0, i, 0, 0))
    return pl.pallas_call(
        x_sum_kernel,
        out_shape=out_shape,
        grid=(comps,),
        in_specs=[part, part],
        out_specs=out_specs,
        compiler_params=params(32),
        cost_estimate=cost(keep.size, keep.size * 6),
        name="x_sum",
    )(keep, got)


def pass_on_kernel(up_ref, down_ref, plus_ref, minus_ref, up_out, down_out):
    up_out[...] = (up_ref[...].astype(F32) + plus_ref[0].astype(F32)).astype(BF16)
    down_out[...] = (down_ref[...].astype(F32) + minus_ref[0].astype(F32)).astype(BF16)


def pass_on(up, down, plus, minus):
    comps, rows, half = up.shape
    one = pl.BlockSpec((1, rows, half), lambda i: (i, 0, 0))
    first = pl.BlockSpec((1, 1, rows, half), lambda i: (0, i, 0, 0))
    return pl.pallas_call(
        pass_on_kernel,
        out_shape=(shaped(up.shape, BF16), shaped(up.shape, BF16)),
        grid=(comps,),
        in_specs=[one, one, first, first],
        out_specs=(one, one),
        compiler_params=params(32),
        cost_estimate=cost(2 * up.size, up.size * 12),
        name="pass_on",
    )(up, down, plus, minus)


def ring_sum_kernel(own_ref, plus_ref, minus_ref, up_ref, down_ref, out_ref):
    half = up_ref.shape[2]
    low = own_ref[0, :, :half].astype(F32) + minus_ref[0, 0].astype(F32) + up_ref[0].astype(F32)
    high = own_ref[0, :, half:].astype(F32) + plus_ref[0, 0].astype(F32) + down_ref[0].astype(F32)
    out_ref[0, :, :half] = low.astype(BF16)
    out_ref[0, :, half:] = high.astype(BF16)


def ring_sum(own, plus, minus, up, down):
    comps, rows, width = own.shape
    one = lambda n: pl.BlockSpec((1, rows, n), lambda i: (i, 0, 0))
    second = pl.BlockSpec((1, 1, rows, width // 2), lambda i: (1, i, 0, 0))
    return pl.pallas_call(
        ring_sum_kernel,
        out_shape=shaped(own.shape, BF16),
        grid=(comps,),
        in_specs=[one(width), second, second, one(width // 2), one(width // 2)],
        out_specs=one(width),
        compiler_params=params(32),
        cost_estimate=cost(2 * own.size, own.size * 8),
        name="ring_sum",
    )(own, plus, minus, up, down)


def gather_rows_kernel(first, lists_ref, own_ref, got_ref, rim_in_ref, out_ref, rim_ref):
    rows = own_ref.shape[1]
    width = own_ref.shape[2]
    if rows == out_ref.shape[1]:
        half = rows // 2
        own = own_ref[0].astype(F32)
        got = got_ref[0].astype(F32)
        out_ref[0, :half, :] = (own[:half] + got[half:]).astype(BF16)
        out_ref[0, half:, :] = (own[half:] + got[:half]).astype(BF16)
    else:
        out_ref[0, :rows, :] = own_ref[0]
        out_ref[0, rows:, :] = got_ref[0]
    node = lax.broadcasted_iota(jnp.int32, (width, lists_ref.shape[1]), 0)
    pick = jnp.where(node == lists_ref[...] - first, 1.0, 0.0).astype(BF16)
    rim = jnp.dot(out_ref[0], pick, preferred_element_type=F32)
    if rim_in_ref is not None:
        rim = rim + rim_in_ref[0].astype(F32)
    rim_ref[0] = rim.astype(BF16)


def gather_rows(lists, own, got, rim, chunk):
    comps, rows, width = own.shape
    full = rows if rim is not None else 2 * rows
    count = lists.shape[1]
    one = lambda r, n: pl.BlockSpec((1, r, n), lambda i: (i, 0, 0))
    kernel = functools.partial(gather_rows_kernel, chunk * width)
    if rim is None:
        kernel = lambda l, a, b, o, r: gather_rows_kernel(chunk * width, l, a, b, None, o, r)
    specs = [pl.BlockSpec((1, count), lambda i: (0, 0)), one(rows, width), one(rows, width)]
    args = [lists, own, got]
    if rim is not None:
        specs.append(one(full, count))
        args.append(rim)
    return pl.pallas_call(
        kernel,
        out_shape=(shaped((comps, full, width), BF16), shaped((comps, full, count), BF16)),
        grid=(comps,),
        in_specs=specs,
        out_specs=(one(full, width), one(full, count)),
        compiler_params=params(32),
        cost_estimate=cost(2 * comps * full * width * count, comps * full * width * 6),
        name="gather_rows",
    )(*args)


NODE_BLOCK = 256
ROWS = 16
LANES = 128


def write_weights(first, conn_ref, grads_ref, out_ref, nodes, start, width):
    corners = conn_ref.shape[0]
    base = lax.broadcasted_iota(jnp.int32, (ROWS, LANES), 0).astype(F32).astype(BF16)
    zero = jnp.zeros((ROWS, LANES), BF16)
    for piece in range(width // LANES):
        cut = pl.ds(start + piece * LANES, LANES)
        grads = grads_ref[:, cut].astype(BF16)
        grad = [jnp.broadcast_to(grads[i : i + 1, :], (ROWS, LANES)) for i in range(3 * corners)]
        for part in range(nodes // NODE_BLOCK):
            keys = (conn_ref[:, cut] - (first + part * NODE_BLOCK)).astype(BF16)
            key = [jnp.broadcast_to(keys[a : a + 1, :], (ROWS, LANES)) for a in range(corners)]
            for row in range(NODE_BLOCK // ROWS):
                node = base + BF16(row * ROWS)
                sums = [zero] * 3
                for a in range(corners):
                    hit = node == key[a]
                    for d in range(3):
                        sums[d] = jnp.where(hit, grad[d * corners + a], sums[d])
                for d in range(3):
                    out_ref[d, pl.ds(part * NODE_BLOCK + row * ROWS, ROWS), pl.ds(piece * LANES, LANES)] = sums[d]


def weights_kernel(first, mark_ref, conn_ref, grads_ref, out_ref):
    del mark_ref
    _, nodes, width = out_ref.shape
    start = first + (pl.program_id(1) * nodes).astype(F32)
    write_weights(start, conn_ref, grads_ref, out_ref, nodes, 0, width)


def element_weights(mark, data, first, nodes):
    elems = data.shape[1]
    width = 512
    block = 512
    return pl.pallas_call(
        functools.partial(weights_kernel, first),
        out_shape=shaped((3, nodes, elems), BF16),
        grid=(elems // width, nodes // block),
        in_specs=[
            ANY,
            pl.BlockSpec((8, width), lambda j, i: (0, j)),
            pl.BlockSpec((24, width), lambda j, i: (0, j)),
        ],
        out_specs=pl.BlockSpec((3, block, width), lambda j, i: (0, i, j)),
        compiler_params=params(32),
        cost_estimate=cost(nodes * elems * 1500, 6 * nodes * elems),
        name="element_weights",
    )(mark, data[:8], data[8:32])


def build_multiply_kernel(first, values_ref, conn_ref, grads_ref, *refs):
    acc_ref, out_ref, weights = refs if len(refs) == 3 else (None,) + refs
    width = out_ref.shape[2]
    nodes = weights.shape[2]
    comps, rows, _ = values_ref.shape
    values = values_ref[...].reshape(comps * rows, nodes)
    piece = weights.shape[3]
    for at in range(width // piece):
        slot = at % weights.shape[0]
        cut = pl.ds(at * piece, piece)
        write_weights(first, conn_ref, grads_ref, weights.at[slot], nodes, at * piece, piece)
        for d in range(3):
            term = jnp.dot(values, weights[slot, d], preferred_element_type=F32)
            if acc_ref is not None:
                term = term + acc_ref[d, :, cut]
            out_ref[d, :, cut] = term


def build_multiply(values, data, acc, first):
    comps, rows, nodes = values.shape
    elems = data.shape[1]
    width = 512
    total = comps * rows
    block = pl.BlockSpec((3, total, width), lambda j: (0, 0, j))
    specs = [
        pl.BlockSpec((comps, rows, nodes), lambda j: (0, 0, 0)),
        pl.BlockSpec((8, width), lambda j: (0, j)),
        pl.BlockSpec((24, width), lambda j: (0, j)),
    ]
    args = [values, data[:8], data[8:32]]
    if acc is not None:
        specs.append(block)
        args.append(acc)
    return pl.pallas_call(
        functools.partial(build_multiply_kernel, float(first)),
        out_shape=shaped((3, total, elems), F32),
        grid=(elems // width,),
        in_specs=specs,
        out_specs=block,
        scratch_shapes=[pltpu.VMEM((2, 3, nodes, 256), BF16)],
        input_output_aliases={} if acc is None else {3: 0},
        compiler_params=params(40),
        cost_estimate=cost(nodes * elems * 1500, 24 * total * elems),
        name="build_multiply",
    )(*args)


def multiply_kernel(values_ref, weights_ref, acc_ref, out_ref):
    comps, rows, nodes = values_ref.shape
    values = values_ref[...].reshape(comps * rows, nodes)
    for d in range(3):
        out_ref[d] = acc_ref[d] + jnp.dot(values, weights_ref[d], preferred_element_type=F32)


def multiply(values, weights, acc):
    comps, rows, nodes = values.shape
    elems = weights.shape[2]
    width = 512
    block = pl.BlockSpec((3, comps * rows, width), lambda j: (0, 0, j))
    return pl.pallas_call(
        multiply_kernel,
        out_shape=shaped(acc.shape, F32),
        grid=(elems // width,),
        in_specs=[
            pl.BlockSpec((comps, rows, nodes), lambda j: (0, 0, 0)),
            pl.BlockSpec((3, nodes, width), lambda j: (0, 0, j)),
            block,
        ],
        out_specs=block,
        input_output_aliases={2: 0},
        compiler_params=params(40),
        cost_estimate=cost(6 * comps * rows * nodes * elems, 6 * nodes * elems),
        name="multiply",
    )(values, weights, acc)


def spectra_kernel(before_ref, after_ref, weights_ref, acc_ref, modulus_ref, out_ref):
    comps, rows, rim = before_ref.shape
    width = out_ref.shape[2]
    half = rows // 4
    before = before_ref[...].reshape(comps * rows, rim)
    after = after_ref[...].reshape(comps * rows, rim)
    modulus = modulus_ref[:1, :]
    lame = modulus * (POISSON / ((1.0 + POISSON) * (1.0 - 2.0 * POISSON)))
    shear = modulus * (1.0 / (2.0 * (1.0 + POISSON)))
    grads = []
    for d in range(3):
        grads.append(
            acc_ref[d]
            + jnp.dot(before, weights_ref[d, :rim, :], preferred_element_type=F32)
            + jnp.dot(after, weights_ref[d, rim:, :], preferred_element_type=F32)
        )
    real = [[None] * 6 for _ in range(6)]
    imag = [[None] * 6 for _ in range(6)]

    def add(store, i, j, value):
        store[i][j] = value if store[i][j] is None else store[i][j] + value

    def stress(top):
        def at(c, d):
            return grads[d][c * rows + top : c * rows + top + 8, :]

        volume = lame * (at(0, 0) + at(1, 1) + at(2, 2))
        twice = 2.0 * shear
        return [
            volume + twice * at(0, 0),
            volume + twice * at(1, 1),
            volume + twice * at(2, 2),
            shear * (at(1, 2) + at(2, 1)),
            shear * (at(2, 0) + at(0, 2)),
            shear * (at(0, 1) + at(1, 0)),
        ]

    for side in range(2):
        for part in range(half // 8):
            re = stress(side * 2 * half + part * 8)
            im = stress(side * 2 * half + half + part * 8)
            for i in range(6):
                for j in range(i, 6):
                    add(real, i, j, re[i] * re[j] + im[i] * im[j])
                for j in range(i + 1, 6):
                    add(imag, i, j, im[i] * re[j] - re[i] * im[j])
    entry = 0
    for i in range(6):
        for j in range(i, 6):
            out_ref[0, entry : entry + 1, :] = jnp.sum(real[i][j], axis=0, keepdims=True)
            entry += 1
    for i in range(6):
        for j in range(i + 1, 6):
            out_ref[0, entry : entry + 1, :] = jnp.sum(imag[i][j], axis=0, keepdims=True)
            entry += 1


def element_spectra(before, after, weights, acc, modulus):
    comps, rows, rim = before.shape
    elems = weights.shape[2]
    width = 256
    per = elems // Z // width
    whole = lambda i: (0, 0, 0)
    return pl.pallas_call(
        spectra_kernel,
        out_shape=shaped((Z, 36, elems // Z), F32),
        grid=(elems // width,),
        in_specs=[
            pl.BlockSpec((comps, rows, rim), whole),
            pl.BlockSpec((comps, rows, rim), whole),
            pl.BlockSpec((3, 2 * rim, width), lambda i: (0, 0, i)),
            pl.BlockSpec((3, comps * rows, width), lambda i: (0, 0, i)),
            pl.BlockSpec((8, width), lambda i: (0, i)),
        ],
        out_specs=pl.BlockSpec((1, 36, width), lambda i: (i // per, 0, i % per)),
        compiler_params=params(40),
        cost_estimate=cost(12 * comps * rows * rim * elems, 24 * comps * rows * elems),
        name="element_spectra",
    )(before, after, weights, acc, modulus)


def local(
    mode_shapes,
    load_nodal,
    mode_freq,
    damping,
    drive_freq,
    send_lists,
    connectivity,
    shape_grads,
    modulus,
):
    modes, _, nodes = mode_shapes.shape
    cols = load_nodal.shape[2]
    bound = send_lists.shape[1]
    freqs = drive_freq.shape[0]
    rows = cols // (Z * XLO)
    mode_at = lax.axis_index("mode")
    z_at, x_at = mode_at // XLO, mode_at % XLO
    core = (lax.axis_index("mesh") % CORE).astype(jnp.int32)
    core_arg = core.reshape(1)
    shapes = jnp.transpose(mode_shapes, (1, 0, 2))
    lists = send_lists.reshape(1, -1)

    pad = 2 * HALF - modes
    natural = jnp.pad(mode_freq, (0, pad), constant_values=1.0)[:, None]
    loss = jnp.pad(damping, (0, pad), constant_values=0.5)[:, None]
    natural = lax.dynamic_slice_in_dim(natural, core * HALF, HALF)
    loss = lax.dynamic_slice_in_dim(loss, core * HALF, HALF)
    forcing = jnp.repeat(drive_freq, cols // freqs)[None, :]
    gap = natural * natural - forcing * forcing
    damp = 2.0 * loss * natural * forcing
    size = gap * gap + damp * damp
    sign = jnp.where(jnp.arange(cols) % 2 == 0, 1.0, -1.0).astype(F32)[None, :]
    direct = gap / size
    cross = sign * (damp / size)

    spot = jnp.arange(cols)
    block, inside = spot // rows, spot % rows
    block = mode_index(z_at + block // XLO, x_at ^ (block % XLO))
    source = block * rows + 2 * (inside % (rows // 2)) + inside // (rows // 2)
    order = (source[:, None] == spot[None, :]).astype(BF16)

    mine, theirs = partial_loads(core_arg, shapes, load_nodal)
    got = lax.ppermute(theirs, "mesh", mesh_perm(0, 0, 1))
    chip = (mine + got.astype(F32)).astype(BF16)
    got = lax.ppermute(chip, "mesh", mesh_perm(0, 1, 0))
    pair = (chip.astype(F32) + got.astype(F32)).astype(BF16)
    ring = [pair] + [lax.ppermute(pair, "mesh", mesh_perm(dy)) for dy in range(1, Y)]

    data = element_data(theirs, connectivity, shape_grads, modulus)
    data = jnp.concatenate(
        [data] + [lax.ppermute(data, "mode", mode_perm(-j)) for j in range(1, Z)], axis=1
    )
    rim_weights = element_weights(pair, data, float(nodes), 2 * bound)

    resp_mine = half_response(ring, direct, cross)
    resp_theirs = lax.ppermute(resp_mine, "mesh", mesh_perm(0, 0, 1))

    chunks = nodes // CHUNK
    up_perm, down_perm, side_perm = mode_perm(1), mode_perm(-1), mode_perm(0, 1)
    away, keep, resp = x_first_terms(core_arg, resp_mine, resp_theirs, order, shapes, 0)
    got = lax.ppermute(away, "mode", side_perm)

    def first_hop(ways):
        return lax.ppermute(ways[0], "mode", up_perm), lax.ppermute(ways[1], "mode", down_perm)

    def second_hop(ways, plus, minus):
        up, down = pass_on(ways[2], ways[3], plus, minus)
        return up, lax.ppermute(up, "mode", up_perm), lax.ppermute(down, "mode", down_perm)

    ways_1 = z_first_terms(resp, resp, shapes, 1)
    plus_1, minus_1 = first_hop(ways_1)
    ways_2 = z_first_terms(ways_1[2], resp, shapes, 2)
    plus_2, minus_2 = first_hop(ways_2)
    last_weights = element_weights(ways_2[2], data, float((chunks - 1) * CHUNK), CHUNK)
    sent_1, up_1, down_1 = second_hop(ways_1, plus_1, minus_1)
    ways_0 = x_sum(keep, got)
    plus_0, minus_0 = first_hop(ways_0)
    ways_3 = z_first_terms(sent_1, resp, shapes, 3)
    own_1 = ring_sum(ways_1[4], plus_1, minus_1, up_1, down_1)
    side_1 = lax.ppermute(own_1, "mode", side_perm)
    _, up_2, down_2 = second_hop(ways_2, plus_2, minus_2)
    plus_3, minus_3 = first_hop(ways_3)
    own_2 = ring_sum(ways_2[4], plus_2, minus_2, up_2, down_2)
    side_2 = lax.ppermute(own_2, "mode", side_perm)
    _, up_0, down_0 = second_hop(ways_0, plus_0, minus_0)
    own_0 = ring_sum(ways_0[4], plus_0, minus_0, up_0, down_0)
    side_0 = lax.ppermute(own_0, "mode", side_perm)
    _, up_3, down_3 = second_hop(ways_3, plus_3, minus_3)
    own_3 = ring_sum(ways_3[4], plus_3, minus_3, up_3, down_3)
    side_3 = lax.ppermute(own_3, "mode", side_perm)

    values_0, rim = gather_rows(lists, own_0, side_0, None, 0)
    values_1, rim = gather_rows(lists, own_1, side_1, rim, 1)
    values_2, rim = gather_rows(lists, own_2, side_2, rim, 2)
    acc = build_multiply(values_1, data, None, CHUNK)
    acc = build_multiply(values_2, data, acc, 2 * CHUNK)
    acc = build_multiply(values_0, data, acc, 0)
    values_3, rim = gather_rows(lists, own_3, side_3, rim, 3)

    count = lax.axis_size("mesh")
    before = lax.ppermute(rim[..., bound:], "mesh", [(p, p + 1) for p in range(count - 1)])
    after = lax.ppermute(rim[..., :bound], "mesh", [(p + 1, p) for p in range(count - 1)])
    acc = multiply(values_3, last_weights, acc)
    spectra = element_spectra(before, after, rim_weights, acc, data[32:40])
    back = [spectra[0]] + [lax.ppermute(spectra[j], "mode", mode_perm(j)) for j in range(1, Z)]
    back = jnp.stack(back)
    return jnp.take(back, (z_at - jnp.arange(Z)) % Z, axis=0)


def solution(mesh):
    in_specs = (
        P("mode", None, "mesh"),
        P(None, "mesh", None),
        P("mode"),
        P("mode"),
        P(),
        P(None, "mesh"),
        P(None, ("mesh", "mode")),
        P(None, None, ("mesh", "mode")),
        P(("mesh", "mode")),
    )
    out_specs = P(None, None, ("mesh", "mode"))
    return jax.shard_map(local, mesh=mesh, in_specs=in_specs, out_specs=out_specs, check_vma=False)
```

```python
import functools

import jax
import jax.numpy as jnp
from jax import lax
from jax.experimental import pallas as pl
from jax.experimental.pallas import tpu as pltpu
from jax.sharding import PartitionSpec as P

POISSON = 0.3
F32 = jnp.float32
BF16 = jnp.bfloat16
MIB = 1024 * 1024
Z, XLO = 4, 2
Y, XHI, CORE = 4, 2, 2
HALF = 256
ANY = pl.BlockSpec(memory_space=pl.ANY)
VMEM = pl.BlockSpec(memory_space=pltpu.VMEM)
SMEM = pl.BlockSpec(memory_space=pltpu.SMEM)


def params(mib):
    return pltpu.CompilerParams(vmem_limit_bytes=mib * MIB)


def cost(flops, moved):
    return pl.CostEstimate(flops=int(flops), bytes_accessed=int(moved), transcendentals=0)


def shaped(shape, kind):
    return jax.ShapeDtypeStruct(shape, kind)


def mode_index(z, x):
    return (z % Z) * XLO + x


def mesh_index(y, h, c):
    return ((y % Y) * XHI + h) * CORE + c


def mode_perm(dz, flip=0):
    return [(mode_index(z, x), mode_index(z + dz, x ^ flip)) for z in range(Z) for x in range(XLO)]


def mesh_perm(dy, flip_h=0, flip_c=0):
    return [
        (mesh_index(y, h, c), mesh_index(y + dy, h ^ flip_h, c ^ flip_c))
        for y in range(Y)
        for h in range(XHI)
        for c in range(CORE)
    ]


def loads_kernel(cuts, core_ref, shapes_ref, load_ref, mine_ref, theirs_ref, shapes, load, acc, shape_sems, load_sems):
    modes = shapes.shape[1]

    def copies(i):
        c, at, width = cuts[i]
        cut = pl.ds(at, width)
        return (
            pltpu.make_async_copy(shapes_ref.at[c, :, cut], shapes.at[c, :, cut], shape_sems.at[i]),
            pltpu.make_async_copy(load_ref.at[c, cut, :], load.at[c, cut, :], load_sems.at[i]),
        )

    for i in range(len(cuts)):
        for copy in copies(i):
            copy.start()
    acc[modes:, :] = jnp.zeros((acc.shape[0] - modes, acc.shape[1]), F32)
    for i, (c, at, width) in enumerate(cuts):
        for copy in copies(i):
            copy.wait()
        cut = pl.ds(at, width)
        term = jnp.dot(shapes[c, :, cut], load[c, cut, :], preferred_element_type=F32)
        acc[:modes, :] = term if i == 0 else acc[:modes, :] + term
    core = core_ref[0]
    mine_ref[...] = acc[pl.ds(core * HALF, HALF), :]
    theirs_ref[...] = acc[pl.ds((1 - core) * HALF, HALF), :].astype(BF16)


def partial_loads(core, shapes, load):
    comps, modes, nodes = shapes.shape
    cols = load.shape[2]
    block = 1024
    cuts = [(c, at, block) for c in range(comps) for at in range(0, nodes, block)]
    vmem = pl.BlockSpec(memory_space=pltpu.VMEM)
    return pl.pallas_call(
        functools.partial(loads_kernel, cuts),
        out_shape=(shaped((HALF, cols), F32), shaped((HALF, cols), BF16)),
        in_specs=[SMEM, ANY, ANY],
        out_specs=(vmem, vmem),
        scratch_shapes=[
            pltpu.VMEM(shapes.shape, BF16),
            pltpu.VMEM(load.shape, BF16),
            pltpu.VMEM((2 * HALF, cols), F32),
            pltpu.SemaphoreType.DMA((len(cuts),)),
            pltpu.SemaphoreType.DMA((len(cuts),)),
        ],
        compiler_params=params(56),
        cost_estimate=cost(2 * modes * comps * nodes * cols, 2 * comps * nodes * (modes + cols)),
        name="modal_loads",
    )(core, shapes, load)


def response_kernel(mark_ref, a_ref, b_ref, c_ref, d_ref, direct_ref, cross_ref, out_ref):
    del mark_ref
    total = (
        a_ref[...].astype(F32)
        + b_ref[...].astype(F32)
        + c_ref[...].astype(F32)
        + d_ref[...].astype(F32)
    )
    cols = total.shape[1]
    even = lax.broadcasted_iota(jnp.int32, total.shape, 1) % 2 == 0
    other = jnp.where(even, pltpu.roll(total, cols - 1, 1), pltpu.roll(total, 1, 1))
    out_ref[...] = (direct_ref[...] * total + cross_ref[...] * other).astype(BF16)


def half_response(mark, parts, direct, cross):
    vmem = pl.BlockSpec(memory_space=pltpu.VMEM)
    return pl.pallas_call(
        response_kernel,
        out_shape=shaped(direct.shape, BF16),
        in_specs=[ANY] + [vmem] * 6,
        out_specs=vmem,
        compiler_params=params(16),
        cost_estimate=cost(direct.size * 8, direct.size * 18),
        name="modal_response",
    )(mark, *parts, direct, cross)


def element_data_kernel(mark_ref, conn_ref, grads_ref, modulus_ref, out_ref):
    del mark_ref
    corners, width = conn_ref.shape
    conn = conn_ref[...].astype(F32)
    out_ref[:corners, :] = conn
    for d in range(3):
        total = jnp.zeros((corners, width), F32)
        for a in range(corners):
            total = total + jnp.where(conn == conn[a : a + 1, :], grads_ref[d, a : a + 1, :], 0.0)
        out_ref[(d + 1) * corners : (d + 2) * corners, :] = total
    out_ref[4 * corners :, :] = jnp.broadcast_to(modulus_ref[...], (corners, width))


def element_data(mark, conn, grads, modulus):
    corners, elems = conn.shape
    vmem = pl.BlockSpec(memory_space=pltpu.VMEM)
    return pl.pallas_call(
        element_data_kernel,
        out_shape=shaped((5 * corners, elems), F32),
        in_specs=[ANY, vmem, vmem, vmem],
        out_specs=vmem,
        compiler_params=params(16),
        cost_estimate=cost(1000, elems * 4 * 80),
        name="element_data",
    )(mark, conn, grads, modulus[None, :])


def split_ways(blocks, plus_ref, minus_ref, up_ref, down_ref, own_ref):
    half = up_ref.shape[-1]
    low = [b[..., :half] for b in blocks]
    high = [b[..., half:] for b in blocks]
    plus_ref[0, 0] = low[2]
    plus_ref[1, 0] = high[1]
    minus_ref[0, 0] = high[2]
    minus_ref[1, 0] = low[3]
    up_ref[0] = low[1]
    down_ref[0] = high[3]
    own_ref[0] = blocks[0]


def way_shapes(comps, rows, width):
    half = width // 2
    shapes = (
        (2, comps, rows, half),
        (2, comps, rows, half),
        (comps, rows, half),
        (comps, rows, half),
        (comps, rows, width),
    )
    specs = tuple(
        pl.BlockSpec((2, 1) + s[2:], lambda i: (0, i, 0, 0))
        if len(s) == 4
        else pl.BlockSpec((1,) + s[1:], lambda i: (i, 0, 0))
        for s in shapes
    )
    return tuple(shaped(s, BF16) for s in shapes), specs


def fetch_shapes(first, shapes_ref, held, sems):
    step = pl.program_id(0)
    cut = pl.ds(first, held.shape[2])

    @pl.when(step == 0)
    def _():
        for c in range(held.shape[0]):
            pltpu.make_async_copy(shapes_ref.at[c, :, cut], held.at[c], sems.at[c]).start()

    pltpu.make_async_copy(shapes_ref.at[step, :, cut], held.at[step], sems.at[step]).wait()
    return held[step]


def fetch_scratch(shapes, width):
    comps, modes, _ = shapes.shape
    return [pltpu.VMEM((comps, modes, width), BF16), pltpu.SemaphoreType.DMA((comps,))]


def z_first_kernel(first, mark_ref, resp_ref, shapes_ref, *refs):
    del mark_ref
    out_refs, (held, sems) = refs[:5], refs[5:]
    part = fetch_shapes(first, shapes_ref, held, sems)
    value = jnp.dot(resp_ref[...], part, preferred_element_type=F32).astype(BF16)
    rows = value.shape[0] // Z
    split_ways([value[j * rows : (j + 1) * rows, :] for j in range(Z)], *out_refs)


def z_first_terms(mark, resp, shapes, chunk):
    first, width = chunk
    comps, modes, _ = shapes.shape
    cols = resp.shape[0]
    out_shape, out_specs = way_shapes(comps, cols // Z, width)
    return pl.pallas_call(
        functools.partial(z_first_kernel, first),
        out_shape=out_shape,
        grid=(comps,),
        in_specs=[ANY, pl.BlockSpec((cols, modes), lambda i: (0, 0)), ANY],
        out_specs=out_specs,
        scratch_shapes=fetch_scratch(shapes, width),
        compiler_params=params(24),
        cost_estimate=cost(2 * modes * comps * width * cols, 2 * comps * width * (modes + cols)),
        name="z_first_terms",
    )(mark, resp, shapes)


def x_first_kernel(
    first, core_ref, mine_ref, theirs_ref, order_ref, shapes_ref, away_ref, keep_ref, turned_ref, resp, held, sems
):
    modes = shapes_ref.shape[1]
    part = fetch_shapes(first, shapes_ref, held, sems)

    @pl.when(pl.program_id(0) == 0)
    def _():
        core = core_ref[0]
        resp[pl.ds(core * HALF, HALF), :] = mine_ref[...]
        resp[pl.ds((1 - core) * HALF, HALF), :] = theirs_ref[...]
        turned = lax.dot_general(
            order_ref[...], resp[...], (((1,), (1,)), ((), ())), preferred_element_type=F32
        )
        turned_ref[...] = turned[:, :modes].astype(BF16)

    value = jnp.dot(turned_ref[...], part, preferred_element_type=F32).astype(BF16)
    rows = value.shape[0] // (Z * XLO)
    for j in range(Z):
        keep_ref[j, 0] = value[(2 * j) * rows : (2 * j + 1) * rows, :]
        away_ref[j, 0] = value[(2 * j + 1) * rows : (2 * j + 2) * rows, :]


def x_first_terms(core, mine, theirs, order, shapes, chunk):
    first, width = chunk
    comps, modes, _ = shapes.shape
    cols = mine.shape[1]
    rows = cols // (Z * XLO)
    part = pl.BlockSpec((Z, 1, rows, width), lambda i: (0, i, 0, 0))
    whole = lambda i: (0, 0)
    return pl.pallas_call(
        functools.partial(x_first_kernel, first),
        out_shape=(
            shaped((Z, comps, rows, width), BF16),
            shaped((Z, comps, rows, width), BF16),
            shaped((cols, modes), BF16),
        ),
        grid=(comps,),
        in_specs=[
            SMEM,
            pl.BlockSpec((HALF, cols), whole),
            pl.BlockSpec((HALF, cols), whole),
            pl.BlockSpec((cols, cols), whole),
            ANY,
        ],
        out_specs=(part, part, pl.BlockSpec((cols, modes), whole)),
        scratch_shapes=[pltpu.VMEM((2 * HALF, cols), BF16)] + fetch_scratch(shapes, width),
        compiler_params=params(24),
        cost_estimate=cost(2 * modes * comps * width * cols, 2 * comps * width * (modes + cols)),
        name="x_first_terms",
    )(core, mine, theirs, order, shapes)


def x_sum_kernel(mark_ref, keep_ref, got_ref, *out_refs):
    del mark_ref
    blocks = [(keep_ref[j, 0].astype(F32) + got_ref[j, 0].astype(F32)).astype(BF16) for j in range(Z)]
    split_ways(blocks, *out_refs)


def x_sum(mark, keep, got):
    _, comps, rows, width = keep.shape
    out_shape, out_specs = way_shapes(comps, rows, width)
    part = pl.BlockSpec((Z, 1, rows, width), lambda i: (0, i, 0, 0))
    return pl.pallas_call(
        x_sum_kernel,
        out_shape=out_shape,
        grid=(comps,),
        in_specs=[ANY, part, part],
        out_specs=out_specs,
        compiler_params=params(16),
        cost_estimate=cost(keep.size, keep.size * 6),
        name="x_sum",
    )(mark, keep, got)


def pass_on_kernel(mark_ref, up_ref, down_ref, plus_ref, minus_ref, up_out, down_out):
    del mark_ref
    up_out[...] = (up_ref[...].astype(F32) + plus_ref[0].astype(F32)).astype(BF16)
    down_out[...] = (down_ref[...].astype(F32) + minus_ref[0].astype(F32)).astype(BF16)


def pass_on(mark, up, down, plus, minus):
    comps, rows, half = up.shape
    one = pl.BlockSpec((1, rows, half), lambda i: (i, 0, 0))
    first = pl.BlockSpec((1, 1, rows, half), lambda i: (0, i, 0, 0))
    return pl.pallas_call(
        pass_on_kernel,
        out_shape=(shaped(up.shape, BF16), shaped(up.shape, BF16)),
        grid=(comps,),
        in_specs=[ANY, one, one, first, first],
        out_specs=(one, one),
        compiler_params=params(16),
        cost_estimate=cost(2 * up.size, up.size * 12),
        name="pass_on",
    )(mark, up, down, plus, minus)


def ring_sum_kernel(mark_ref, own_ref, plus_ref, minus_ref, up_ref, down_ref, out_ref):
    del mark_ref
    half = up_ref.shape[2]
    low = own_ref[0, :, :half].astype(F32) + minus_ref[0, 0].astype(F32) + up_ref[0].astype(F32)
    high = own_ref[0, :, half:].astype(F32) + plus_ref[0, 0].astype(F32) + down_ref[0].astype(F32)
    out_ref[0, :, :half] = low.astype(BF16)
    out_ref[0, :, half:] = high.astype(BF16)


def ring_sum(mark, own, plus, minus, up, down):
    comps, rows, width = own.shape
    one = lambda n: pl.BlockSpec((1, rows, n), lambda i: (i, 0, 0))
    second = pl.BlockSpec((1, 1, rows, width // 2), lambda i: (1, i, 0, 0))
    return pl.pallas_call(
        ring_sum_kernel,
        out_shape=shaped(own.shape, BF16),
        grid=(comps,),
        in_specs=[ANY, one(width), second, second, one(width // 2), one(width // 2)],
        out_specs=one(width),
        compiler_params=params(16),
        cost_estimate=cost(2 * own.size, own.size * 8),
        name="ring_sum",
    )(mark, own, plus, minus, up, down)


def gather_rows_kernel(first, mark_ref, lists_ref, own_ref, got_ref, *refs):
    del mark_ref
    rim_in_ref, out_ref, rim_ref = refs if len(refs) == 3 else (None,) + refs
    rows = own_ref.shape[1]
    width = own_ref.shape[2]
    if rows == out_ref.shape[1]:
        half = rows // 2
        own = own_ref[0].astype(F32)
        got = got_ref[0].astype(F32)
        out_ref[0, :half, :] = (own[:half] + got[half:]).astype(BF16)
        out_ref[0, half:, :] = (own[half:] + got[:half]).astype(BF16)
    else:
        out_ref[0, :rows, :] = own_ref[0]
        out_ref[0, rows:, :] = got_ref[0]
    node = lax.broadcasted_iota(jnp.int32, (width, lists_ref.shape[1]), 0)
    pick = jnp.where(node == lists_ref[...] - first, 1.0, 0.0).astype(BF16)
    rim = jnp.dot(out_ref[0], pick, preferred_element_type=F32)
    if rim_in_ref is not None:
        rim = rim + rim_in_ref[0].astype(F32)
    rim_ref[0] = rim.astype(BF16)


def gather_rows(mark, lists, own, got, rim, first, full):
    comps, rows, width = own.shape
    count = lists.shape[1]
    one = lambda r, n: pl.BlockSpec((1, r, n), lambda i: (i, 0, 0))
    specs = [ANY, pl.BlockSpec((1, count), lambda i: (0, 0)), one(rows, width), one(rows, width)]
    args = [mark, lists, own, got]
    if rim is not None:
        specs.append(one(full, count))
        args.append(rim)
    return pl.pallas_call(
        functools.partial(gather_rows_kernel, first),
        out_shape=(shaped((comps, full, width), BF16), shaped((comps, full, count), BF16)),
        grid=(comps,),
        in_specs=specs,
        out_specs=(one(full, width), one(full, count)),
        compiler_params=params(16),
        cost_estimate=cost(2 * comps * full * width * count, comps * full * width * 6),
        name="gather_rows",
    )(*args)


NODE_BLOCK = 256
ROWS = 16
LANES = 128


def weights_kernel(first, mark_ref, conn_ref, grads_ref, out_ref):
    del mark_ref
    corners, elems = conn_ref.shape
    nodes = out_ref.shape[1]
    base = lax.broadcasted_iota(jnp.int32, (ROWS, LANES), 0).astype(F32).astype(BF16)
    zero = jnp.zeros((ROWS, LANES), BF16)

    def piece(step, carry):
        cut = pl.ds(pl.multiple_of(step * LANES, LANES), LANES)
        grads = grads_ref[:, cut].astype(BF16)
        grad = [jnp.broadcast_to(grads[i : i + 1, :], (ROWS, LANES)) for i in range(3 * corners)]
        for at in range(0, nodes, NODE_BLOCK):
            keys = (conn_ref[:, cut] - (first + at)).astype(BF16)
            key = [jnp.broadcast_to(keys[a : a + 1, :], (ROWS, LANES)) for a in range(corners)]
            for row in range(0, NODE_BLOCK, ROWS):
                node = base + BF16(row)
                sums = [zero] * 3
                for a in range(corners):
                    hit = node == key[a]
                    for d in range(3):
                        sums[d] = jnp.where(hit, grad[d * corners + a], sums[d])
                for d in range(3):
                    out_ref[d, pl.ds(at + row, ROWS), cut] = sums[d]
        return carry

    lax.fori_loop(0, elems // LANES, piece, 0)


def element_weights(mark, data, first, count):
    elems = data.shape[1]
    return pl.pallas_call(
        functools.partial(weights_kernel, float(first)),
        out_shape=shaped((3, count, elems), BF16),
        in_specs=[ANY, VMEM, VMEM],
        out_specs=VMEM,
        compiler_params=params(8),
        cost_estimate=cost(count * elems * 1500, 6 * count * elems),
        name="element_weights",
    )(mark, data[:8], data[8:32])


def multiply_kernel(pieces, mark_ref, values_ref, *refs):
    del mark_ref
    weights_refs, rest = refs[:pieces], refs[pieces:]
    acc_ref, out_ref = rest if len(rest) == 2 else (None,) + rest
    comps, rows, nodes = values_ref.shape
    values = values_ref[...].reshape(comps * rows, nodes)

    def piece(step, carry):
        cut = pl.ds(pl.multiple_of(step * WIDE, WIDE), WIDE)
        for d in range(3):
            total = None if acc_ref is None else acc_ref[d, :, cut]
            at = 0
            for ref in weights_refs:
                count = ref.shape[1]
                term = jnp.dot(values[:, at : at + count], ref[d, :, cut], preferred_element_type=F32)
                total = term if total is None else total + term
                at += count
            out_ref[d, :, cut] = total
        return carry

    lax.fori_loop(0, out_ref.shape[2] // WIDE, piece, 0)


WIDE = 256


def multiply(mark, values, weights, acc):
    comps, rows, nodes = values.shape
    elems = weights[0].shape[2]
    total = comps * rows
    args = [mark, values] + list(weights) + ([] if acc is None else [acc])
    return pl.pallas_call(
        functools.partial(multiply_kernel, len(weights)),
        out_shape=shaped((3, total, elems), F32),
        in_specs=[ANY] + [VMEM] * (len(args) - 1),
        out_specs=VMEM,
        input_output_aliases={} if acc is None else {len(args) - 1: 0},
        compiler_params=params(8),
        cost_estimate=cost(6 * total * nodes * elems, 6 * nodes * elems),
        name="multiply",
    )(*args)


def spectra_kernel(before_ref, after_ref, weights_ref, acc_ref, modulus_ref, out_ref, grads):
    comps, rows, rim = before_ref.shape
    half = rows // 4
    groups, _, count = out_ref.shape
    per = count // WIDE
    before = before_ref[...].reshape(comps * rows, rim)
    after = after_ref[...].reshape(comps * rows, rim)

    def finish(group, place, lanes_at, modulus):
        lame = modulus * (POISSON / ((1.0 + POISSON) * (1.0 - 2.0 * POISSON)))
        shear = modulus * (1.0 / (2.0 * (1.0 + POISSON)))
        twice = 2.0 * shear
        lanes = pl.ds(lanes_at, LANES)

        def stress(top):
            def at(c, d):
                return grads[d, c * rows + top : c * rows + top + 8, lanes]

            volume = lame * (at(0, 0) + at(1, 1) + at(2, 2))
            return [
                volume + twice * at(0, 0),
                volume + twice * at(1, 1),
                volume + twice * at(2, 2),
                shear * (at(1, 2) + at(2, 1)),
                shear * (at(2, 0) + at(0, 2)),
                shear * (at(0, 1) + at(1, 0)),
            ]

        pairs = [(i, j, 0) for i in range(6) for j in range(i, 6)]
        pairs += [(i, j, 1) for i in range(6) for j in range(i + 1, 6)]
        totals = [None] * len(pairs)
        for top in [s * 2 * half + p for s in range(2) for p in range(0, half, 8)]:
            re = stress(top)
            im = stress(top + half)
            for n, (i, j, turned) in enumerate(pairs):
                if turned:
                    term = im[i] * re[j] - re[i] * im[j]
                else:
                    term = re[i] * re[j] + im[i] * im[j]
                totals[n] = term if totals[n] is None else totals[n] + term
        for n in range(len(pairs)):
            out_ref[group, pl.ds(n, 1), pl.ds(place, LANES)] = jnp.sum(totals[n], axis=0, keepdims=True)

    def piece(step, carry):
        cut = pl.ds(pl.multiple_of(step * WIDE, WIDE), WIDE)
        for d in range(3):
            grads[d] = (
                acc_ref[d, :, cut]
                + jnp.dot(before, weights_ref[d, :rim, cut], preferred_element_type=F32)
                + jnp.dot(after, weights_ref[d, rim:, cut], preferred_element_type=F32)
            )
        group = step // per
        start = (step % per) * WIDE
        for at in range(0, WIDE, LANES):
            here = pl.ds(pl.multiple_of(step * WIDE + at, LANES), LANES)
            finish(group, pl.multiple_of(start + at, LANES), at, modulus_ref[:1, here])
        return carry

    lax.fori_loop(0, groups * per, piece, 0)


def element_spectra(before, after, weights, acc, modulus):
    comps, rows, rim = before.shape
    elems = weights.shape[2]
    return pl.pallas_call(
        spectra_kernel,
        out_shape=shaped((Z, 36, elems // Z), F32),
        in_specs=[VMEM] * 5,
        out_specs=VMEM,
        scratch_shapes=[pltpu.VMEM((3, comps * rows, WIDE), F32)],
        compiler_params=params(8),
        cost_estimate=cost(12 * comps * rows * rim * elems, 24 * comps * rows * elems),
        name="element_spectra",
    )(before, after, weights, acc, modulus)


def collect_kernel(place_ref, a_ref, b_ref, c_ref, d_ref, out_ref):
    for j, ref in enumerate((a_ref, b_ref, c_ref, d_ref)):
        out_ref[pl.ds((place_ref[0] + Z - j) % Z, 1)] = ref[...][None]


def collect(place, blocks):
    return pl.pallas_call(
        collect_kernel,
        out_shape=shaped((Z,) + blocks[0].shape, F32),
        in_specs=[SMEM] + [VMEM] * Z,
        out_specs=VMEM,
        compiler_params=params(8),
        cost_estimate=cost(1, 8 * Z * blocks[0].size),
        name="collect",
    )(place, *blocks)


def local(
    mode_shapes,
    load_nodal,
    mode_freq,
    damping,
    drive_freq,
    send_lists,
    connectivity,
    shape_grads,
    modulus,
):
    modes, _, nodes = mode_shapes.shape
    cols = load_nodal.shape[2]
    bound = send_lists.shape[1]
    freqs = drive_freq.shape[0]
    rows = cols // (Z * XLO)
    mode_at = lax.axis_index("mode")
    z_at, x_at = mode_at // XLO, mode_at % XLO
    core = (lax.axis_index("mesh") % CORE).astype(jnp.int32)
    core_arg = core.reshape(1)
    shapes = jnp.transpose(mode_shapes, (1, 0, 2))
    lists = send_lists.reshape(1, -1)

    pad = 2 * HALF - modes
    natural = jnp.pad(mode_freq, (0, pad), constant_values=1.0)[:, None]
    loss = jnp.pad(damping, (0, pad), constant_values=0.5)[:, None]
    natural = lax.dynamic_slice_in_dim(natural, core * HALF, HALF)
    loss = lax.dynamic_slice_in_dim(loss, core * HALF, HALF)
    forcing = jnp.repeat(drive_freq, cols // freqs)[None, :]
    gap = natural * natural - forcing * forcing
    damp = 2.0 * loss * natural * forcing
    size = gap * gap + damp * damp
    sign = jnp.where(jnp.arange(cols) % 2 == 0, 1.0, -1.0).astype(F32)[None, :]
    direct = gap / size
    cross = sign * (damp / size)

    spot = jnp.arange(cols)
    block, inside = spot // rows, spot % rows
    block = mode_index(z_at + block // XLO, x_at ^ (block % XLO))
    source = block * rows + 2 * (inside % (rows // 2)) + inside // (rows // 2)
    order = (source[:, None] == spot[None, :]).astype(BF16)

    mine, theirs = partial_loads(core_arg, shapes, load_nodal)
    got = lax.ppermute(theirs, "mesh", mesh_perm(0, 0, 1))
    chip = (mine + got.astype(F32)).astype(BF16)
    got = lax.ppermute(chip, "mesh", mesh_perm(0, 1, 0))
    pair = (chip.astype(F32) + got.astype(F32)).astype(BF16)
    ring = [pair] + [lax.ppermute(pair, "mesh", mesh_perm(dy)) for dy in range(1, Y)]

    data = element_data(theirs, connectivity, shape_grads, modulus)
    data = jnp.concatenate(
        [data] + [lax.ppermute(data, "mode", mode_perm(-j)) for j in range(1, Z)], axis=1
    )
    up_perm, down_perm, side_perm = mode_perm(1), mode_perm(-1), mode_perm(0, 1)
    up = lambda v: lax.ppermute(v, "mode", up_perm)
    down = lambda v: lax.ppermute(v, "mode", down_perm)
    side = lambda v: lax.ppermute(v, "mode", side_perm)
    full = 2 * rows

    w_1, w_0, w_2, w_3 = nodes * 5 // 16, nodes * 4 // 16, nodes * 5 // 16, nodes * 2 // 16
    c_1, c_0 = (0, w_1), (w_1, w_0)
    c_2, c_3 = (w_1 + w_0, w_2), (w_1 + w_0 + w_2, w_3)

    part = 2 * NODE_BLOCK
    early = w_2 - part
    build = lambda mark, first, count: element_weights(mark, data, first, count)
    weights_1 = [build(pair, 0, part)]
    resp_mine = half_response(weights_1[0], ring, direct, cross)
    resp_theirs = lax.ppermute(resp_mine, "mesh", mesh_perm(0, 0, 1))
    away, keep, resp = x_first_terms(core_arg, resp_mine, resp_theirs, order, shapes, c_0)
    got_0 = side(away)
    ways_1 = z_first_terms(keep, resp, shapes, c_1)
    plus_1, minus_1 = up(ways_1[0]), down(ways_1[1])
    ways_2 = z_first_terms(ways_1[2], resp, shapes, c_2)
    plus_2, minus_2 = up(ways_2[0]), down(ways_2[1])
    weights_1.append(build(ways_2[2], part, w_1 - part))
    on_1 = pass_on(weights_1[1], ways_1[2], ways_1[3], plus_1, minus_1)
    up_1, down_1 = up(on_1[0]), down(on_1[1])
    ways_3 = z_first_terms(on_1[0], resp, shapes, c_3)
    weights_0 = [build(ways_3[2], c_0[0], part)]
    ways_0 = x_sum(weights_0[0], keep, got_0)
    plus_0, minus_0 = up(ways_0[0]), down(ways_0[1])
    weights_0.append(build(ways_0[2], c_0[0] + part, w_0 - part))
    on_2 = pass_on(weights_0[1], ways_2[2], ways_2[3], plus_2, minus_2)
    up_2, down_2 = up(on_2[0]), down(on_2[1])
    plus_3, minus_3 = up(ways_3[0]), down(ways_3[1])
    weights_2 = [build(on_2[0], c_2[0], early)]
    own_1 = ring_sum(weights_2[0], ways_1[4], plus_1, minus_1, up_1, down_1)
    side_1 = side(own_1)
    on_0 = pass_on(own_1, ways_0[2], ways_0[3], plus_0, minus_0)
    up_0, down_0 = up(on_0[0]), down(on_0[1])
    own_2 = ring_sum(on_0[0], ways_2[4], plus_2, minus_2, up_2, down_2)
    side_2 = side(own_2)
    values_1, rim = gather_rows(own_2, lists, own_1, side_1, None, c_1[0], full)
    acc = multiply(rim, values_1, weights_1, None)
    on_3 = pass_on(acc, ways_3[2], ways_3[3], plus_3, minus_3)
    up_3, down_3 = up(on_3[0]), down(on_3[1])
    own_0 = ring_sum(on_3[0], ways_0[4], plus_0, minus_0, up_0, down_0)
    side_0 = side(own_0)
    weights_2.append(build(own_0, c_2[0] + early, w_2 - early))
    own_3 = ring_sum(weights_2[1], ways_3[4], plus_3, minus_3, up_3, down_3)
    side_3 = side(own_3)
    values_2, rim = gather_rows(own_3, lists, own_2, side_2, rim, c_2[0], full)
    acc = multiply(rim, values_2, weights_2, acc)
    weights_3 = [build(acc, nodes - w_3, w_3)]
    values_0, rim = gather_rows(weights_3[0], lists, own_0, side_0, rim, c_0[0], full)
    acc = multiply(rim, values_0, weights_0, acc)
    rim_weights = build(acc, nodes, 2 * bound)
    values_3, rim = gather_rows(rim_weights, lists, own_3, side_3, rim, c_3[0], full)

    count = lax.axis_size("mesh")
    before = lax.ppermute(rim[..., bound:], "mesh", [(p, p + 1) for p in range(count - 1)])
    after = lax.ppermute(rim[..., :bound], "mesh", [(p + 1, p) for p in range(count - 1)])
    acc = multiply(rim, values_3, weights_3, acc)
    spectra = element_spectra(before, after, rim_weights, acc, data[32:40])
    back = [spectra[0]] + [lax.ppermute(spectra[j], "mode", mode_perm(j)) for j in range(1, Z)]
    return collect(z_at.astype(jnp.int32).reshape(1), back)


def solution(mesh):
    in_specs = (
        P("mode", None, "mesh"),
        P(None, "mesh", None),
        P("mode"),
        P("mode"),
        P(),
        P(None, "mesh"),
        P(None, ("mesh", "mode")),
        P(None, None, ("mesh", "mode")),
        P(("mesh", "mode")),
    )
    out_specs = P(None, None, ("mesh", "mode"))
    return jax.shard_map(local, mesh=mesh, in_specs=in_specs, out_specs=out_specs, check_vma=False)
```

```python
import functools

import jax
import jax.numpy as jnp
from jax import lax
from jax.experimental import pallas as pl
from jax.experimental.pallas import tpu as pltpu
from jax.sharding import PartitionSpec as P

POISSON = 0.3
F32 = jnp.float32
BF16 = jnp.bfloat16
MIB = 1024 * 1024
Z, XLO = 4, 2
Y, XHI, CORE = 4, 2, 2
HALF = 256
ANY = pl.BlockSpec(memory_space=pl.ANY)
VMEM = pl.BlockSpec(memory_space=pltpu.VMEM)
HBM = pl.BlockSpec(memory_space=pltpu.HBM)
SMEM = pl.BlockSpec(memory_space=pltpu.SMEM)


def params(mib):
    return pltpu.CompilerParams(vmem_limit_bytes=mib * MIB)


def cost(flops=1, moved=1):
    return pl.CostEstimate(flops=flops, bytes_accessed=moved, transcendentals=0)


def shaped(shape, kind):
    return jax.ShapeDtypeStruct(shape, kind)


def mode_index(z, x):
    return (z % Z) * XLO + x


def mesh_index(y, h, c):
    return ((y % Y) * XHI + h) * CORE + c


def mode_perm(dz, flip=0):
    return [(mode_index(z, x), mode_index(z + dz, x ^ flip)) for z in range(Z) for x in range(XLO)]


def mesh_perm(dy, flip_h=0, flip_c=0):
    return [
        (mesh_index(y, h, c), mesh_index(y + dy, h ^ flip_h, c ^ flip_c))
        for y in range(Y)
        for h in range(XHI)
        for c in range(CORE)
    ]


def loads_kernel(cuts, core_ref, shapes_ref, load_ref, mine_ref, theirs_ref, shapes, load, acc, shape_sems, load_sems):
    modes = shapes.shape[1]

    def copies(i):
        c, at, width = cuts[i]
        cut = pl.ds(at, width)
        return (
            pltpu.make_async_copy(shapes_ref.at[c, :, cut], shapes.at[c, :, cut], shape_sems.at[i]),
            pltpu.make_async_copy(load_ref.at[c, cut, :], load.at[c, cut, :], load_sems.at[i]),
        )

    for i in range(len(cuts)):
        for copy in copies(i):
            copy.start()
    acc[modes:, :] = jnp.zeros((acc.shape[0] - modes, acc.shape[1]), F32)
    for i, (c, at, width) in enumerate(cuts):
        for copy in copies(i):
            copy.wait()
        cut = pl.ds(at, width)
        term = jnp.dot(shapes[c, :, cut], load[c, cut, :], preferred_element_type=F32)
        acc[:modes, :] = term if i == 0 else acc[:modes, :] + term
    core = core_ref[0]
    mine_ref[...] = acc[pl.ds(core * HALF, HALF), :]
    theirs_ref[...] = acc[pl.ds((1 - core) * HALF, HALF), :].astype(BF16)


def partial_loads(core, shapes, load):
    comps, modes, nodes = shapes.shape
    cols = load.shape[2]
    block = 1024
    cuts = [(c, at, block) for c in range(comps) for at in range(0, nodes, block)]
    vmem = pl.BlockSpec(memory_space=pltpu.VMEM)
    return pl.pallas_call(
        functools.partial(loads_kernel, cuts),
        out_shape=(shaped((HALF, cols), F32), shaped((HALF, cols), BF16)),
        in_specs=[SMEM, HBM, HBM],
        out_specs=(vmem, vmem),
        scratch_shapes=[
            pltpu.VMEM(shapes.shape, BF16),
            pltpu.VMEM(load.shape, BF16),
            pltpu.VMEM((2 * HALF, cols), F32),
            pltpu.SemaphoreType.DMA((len(cuts),)),
            pltpu.SemaphoreType.DMA((len(cuts),)),
        ],
        compiler_params=params(56),
        cost_estimate=cost(),
        name="modal_loads",
    )(core, shapes, load)


def response_kernel(mark_ref, a_ref, b_ref, c_ref, d_ref, direct_ref, cross_ref, out_ref):
    del mark_ref
    total = (
        a_ref[...].astype(F32)
        + b_ref[...].astype(F32)
        + c_ref[...].astype(F32)
        + d_ref[...].astype(F32)
    )
    cols = total.shape[1]
    even = lax.broadcasted_iota(jnp.int32, total.shape, 1) % 2 == 0
    other = jnp.where(even, pltpu.roll(total, cols - 1, 1), pltpu.roll(total, 1, 1))
    out_ref[...] = (direct_ref[...] * total + cross_ref[...] * other).astype(BF16)


def half_response(mark, parts, direct, cross):
    vmem = pl.BlockSpec(memory_space=pltpu.VMEM)
    return pl.pallas_call(
        response_kernel,
        out_shape=shaped(direct.shape, BF16),
        in_specs=[ANY] + [vmem] * 6,
        out_specs=vmem,
        compiler_params=params(8),
        cost_estimate=cost(),
        name="modal_response",
    )(mark, *parts, direct, cross)


def element_data_kernel(mark_ref, conn_ref, grads_ref, modulus_ref, out_ref):
    del mark_ref
    corners, width = conn_ref.shape
    conn = conn_ref[...].astype(F32)
    out_ref[:corners, :] = conn
    for d in range(3):
        total = jnp.zeros((corners, width), F32)
        for a in range(corners):
            total = total + jnp.where(conn == conn[a : a + 1, :], grads_ref[d, a : a + 1, :], 0.0)
        out_ref[(d + 1) * corners : (d + 2) * corners, :] = total
    out_ref[4 * corners :, :] = jnp.broadcast_to(modulus_ref[...], (corners, width))


def element_data(mark, conn, grads, modulus):
    corners, elems = conn.shape
    vmem = pl.BlockSpec(memory_space=pltpu.VMEM)
    return pl.pallas_call(
        element_data_kernel,
        out_shape=shaped((5 * corners, elems), F32),
        in_specs=[ANY, vmem, vmem, vmem],
        out_specs=vmem,
        compiler_params=params(8),
        cost_estimate=cost(),
        name="element_data",
    )(mark, conn, grads, modulus[None, :])


def split_ways(blocks, plus_ref, minus_ref, up_ref, down_ref, own_ref):
    half = up_ref.shape[-1]
    low = [b[..., :half] for b in blocks]
    high = [b[..., half:] for b in blocks]
    plus_ref[0, 0] = low[2]
    plus_ref[1, 0] = high[1]
    minus_ref[0, 0] = high[2]
    minus_ref[1, 0] = low[3]
    up_ref[0] = low[1]
    down_ref[0] = high[3]
    own_ref[0] = blocks[0]


def way_shapes(comps, rows, width):
    half = width // 2
    shapes = (
        (2, comps, rows, half),
        (2, comps, rows, half),
        (comps, rows, half),
        (comps, rows, half),
        (comps, rows, width),
    )
    specs = tuple(
        pl.BlockSpec((2, 1) + s[2:], lambda i: (0, i, 0, 0))
        if len(s) == 4
        else pl.BlockSpec((1,) + s[1:], lambda i: (i, 0, 0))
        for s in shapes
    )
    return tuple(shaped(s, BF16) for s in shapes), specs


def fetch_shapes(first, shapes_ref, held, sems):
    step = pl.program_id(0)
    cut = pl.ds(first, held.shape[2])

    @pl.when(step == 0)
    def _():
        for c in range(held.shape[0]):
            pltpu.make_async_copy(shapes_ref.at[c, :, cut], held.at[c], sems.at[c]).start()

    pltpu.make_async_copy(shapes_ref.at[step, :, cut], held.at[step], sems.at[step]).wait()
    return held[step]


def fetch_scratch(shapes, width):
    comps, modes, _ = shapes.shape
    return [pltpu.VMEM((comps, modes, width), BF16), pltpu.SemaphoreType.DMA((comps,))]


def z_first_kernel(first, mark_ref, resp_ref, shapes_ref, *refs):
    del mark_ref
    out_refs, (held, sems) = refs[:5], refs[5:]
    part = fetch_shapes(first, shapes_ref, held, sems)
    value = jnp.dot(resp_ref[...], part, preferred_element_type=F32).astype(BF16)
    rows = value.shape[0] // Z
    split_ways([value[j * rows : (j + 1) * rows, :] for j in range(Z)], *out_refs)


def z_first_terms(mark, resp, shapes, chunk, mib):
    first, width = chunk
    comps, modes, _ = shapes.shape
    cols = resp.shape[0]
    out_shape, out_specs = way_shapes(comps, cols // Z, width)
    return pl.pallas_call(
        functools.partial(z_first_kernel, first),
        out_shape=out_shape,
        grid=(comps,),
        in_specs=[ANY, pl.BlockSpec((cols, modes), lambda i: (0, 0)), HBM],
        out_specs=out_specs,
        scratch_shapes=fetch_scratch(shapes, width),
        compiler_params=params(mib),
        cost_estimate=cost(),
        name="z_first_terms",
    )(mark, resp, shapes)


def x_first_kernel(
    first, core_ref, mine_ref, theirs_ref, order_ref, shapes_ref, away_ref, keep_ref, turned_ref, resp, held, sems
):
    modes = shapes_ref.shape[1]
    part = fetch_shapes(first, shapes_ref, held, sems)

    @pl.when(pl.program_id(0) == 0)
    def _():
        core = core_ref[0]
        resp[pl.ds(core * HALF, HALF), :] = mine_ref[...]
        resp[pl.ds((1 - core) * HALF, HALF), :] = theirs_ref[...]
        turned = lax.dot_general(
            order_ref[...], resp[...], (((1,), (1,)), ((), ())), preferred_element_type=F32
        )
        turned_ref[...] = turned[:, :modes].astype(BF16)

    value = jnp.dot(turned_ref[...], part, preferred_element_type=F32).astype(BF16)
    rows = value.shape[0] // (Z * XLO)
    for j in range(Z):
        keep_ref[j, 0] = value[(2 * j) * rows : (2 * j + 1) * rows, :]
        away_ref[j, 0] = value[(2 * j + 1) * rows : (2 * j + 2) * rows, :]


def x_first_terms(core, mine, theirs, order, shapes, chunk, mib):
    first, width = chunk
    comps, modes, _ = shapes.shape
    cols = mine.shape[1]
    rows = cols // (Z * XLO)
    part = pl.BlockSpec((Z, 1, rows, width), lambda i: (0, i, 0, 0))
    whole = lambda i: (0, 0)
    return pl.pallas_call(
        functools.partial(x_first_kernel, first),
        out_shape=(
            shaped((Z, comps, rows, width), BF16),
            shaped((Z, comps, rows, width), BF16),
            shaped((cols, modes), BF16),
        ),
        grid=(comps,),
        in_specs=[
            SMEM,
            pl.BlockSpec((HALF, cols), whole),
            pl.BlockSpec((HALF, cols), whole),
            pl.BlockSpec((cols, cols), whole),
            HBM,
        ],
        out_specs=(part, part, pl.BlockSpec((cols, modes), whole)),
        scratch_shapes=[pltpu.VMEM((2 * HALF, cols), BF16)] + fetch_scratch(shapes, width),
        compiler_params=params(mib),
        cost_estimate=cost(),
        name="x_first_terms",
    )(core, mine, theirs, order, shapes)


def x_sum_kernel(mark_ref, keep_ref, got_ref, *out_refs):
    del mark_ref
    blocks = [(keep_ref[j, 0].astype(F32) + got_ref[j, 0].astype(F32)).astype(BF16) for j in range(Z)]
    split_ways(blocks, *out_refs)


def x_sum(mark, keep, got):
    _, comps, rows, width = keep.shape
    out_shape, out_specs = way_shapes(comps, rows, width)
    part = pl.BlockSpec((Z, 1, rows, width), lambda i: (0, i, 0, 0))
    return pl.pallas_call(
        x_sum_kernel,
        out_shape=out_shape,
        grid=(comps,),
        in_specs=[ANY, part, part],
        out_specs=out_specs,
        compiler_params=params(8),
        cost_estimate=cost(),
        name="x_sum",
    )(mark, keep, got)


def pass_on_kernel(mark_ref, up_ref, down_ref, plus_ref, minus_ref, up_out, down_out):
    del mark_ref
    up_out[...] = (up_ref[...].astype(F32) + plus_ref[0].astype(F32)).astype(BF16)
    down_out[...] = (down_ref[...].astype(F32) + minus_ref[0].astype(F32)).astype(BF16)


def pass_on(mark, up, down, plus, minus):
    comps, rows, half = up.shape
    one = pl.BlockSpec((1, rows, half), lambda i: (i, 0, 0))
    first = pl.BlockSpec((1, 1, rows, half), lambda i: (0, i, 0, 0))
    return pl.pallas_call(
        pass_on_kernel,
        out_shape=(shaped(up.shape, BF16), shaped(up.shape, BF16)),
        grid=(comps,),
        in_specs=[ANY, one, one, first, first],
        out_specs=(one, one),
        compiler_params=params(8),
        cost_estimate=cost(),
        name="pass_on",
    )(mark, up, down, plus, minus)


def ring_sum_kernel(mark_ref, own_ref, plus_ref, minus_ref, up_ref, down_ref, out_ref):
    del mark_ref
    half = up_ref.shape[2]
    low = own_ref[0, :, :half].astype(F32) + minus_ref[0, 0].astype(F32) + up_ref[0].astype(F32)
    high = own_ref[0, :, half:].astype(F32) + plus_ref[0, 0].astype(F32) + down_ref[0].astype(F32)
    out_ref[0, :, :half] = low.astype(BF16)
    out_ref[0, :, half:] = high.astype(BF16)


def ring_sum(mark, own, plus, minus, up, down):
    comps, rows, width = own.shape
    one = lambda n: pl.BlockSpec((1, rows, n), lambda i: (i, 0, 0))
    second = pl.BlockSpec((1, 1, rows, width // 2), lambda i: (1, i, 0, 0))
    return pl.pallas_call(
        ring_sum_kernel,
        out_shape=shaped(own.shape, BF16),
        grid=(comps,),
        in_specs=[ANY, one(width), second, second, one(width // 2), one(width // 2)],
        out_specs=one(width),
        compiler_params=params(8),
        cost_estimate=cost(),
        name="ring_sum",
    )(mark, own, plus, minus, up, down)


def half_sum_kernel(mark_ref, after_ref, own_ref, direct_ref, passed_ref, out_ref):
    del mark_ref, after_ref
    total = own_ref[...].astype(F32) + direct_ref[0].astype(F32) + passed_ref[...].astype(F32)
    out_ref[...] = total.astype(BF16)


def half_sum(mark, after, side, own, direct, passed):
    comps, rows, half = passed.shape
    one = pl.BlockSpec((1, rows, half), lambda i: (i, 0, 0))
    return pl.pallas_call(
        half_sum_kernel,
        out_shape=shaped(passed.shape, BF16),
        grid=(comps,),
        in_specs=[
            ANY,
            ANY,
            pl.BlockSpec((1, rows, half), lambda i: (i, 0, side)),
            pl.BlockSpec((1, 1, rows, half), lambda i: (1, i, 0, 0)),
            one,
        ],
        out_specs=one,
        compiler_params=params(8),
        cost_estimate=cost(),
        name="half_sum",
    )(mark, after, own, direct, passed)


def gather_rows_kernel(first, mark_ref, lists_ref, own_ref, got_ref, *refs):
    del mark_ref
    rim_in_ref, out_ref, rim_ref = refs if len(refs) == 3 else (None,) + refs
    rows = own_ref.shape[1]
    width = own_ref.shape[2]
    if rows == out_ref.shape[1]:
        half = rows // 2
        own = own_ref[0].astype(F32)
        got = got_ref[0].astype(F32)
        out_ref[0, :half, :] = (own[:half] + got[half:]).astype(BF16)
        out_ref[0, half:, :] = (own[half:] + got[:half]).astype(BF16)
    else:
        out_ref[0, :rows, :] = own_ref[0]
        out_ref[0, rows:, :] = got_ref[0]
    node = lax.broadcasted_iota(jnp.int32, (width, lists_ref.shape[1]), 0)
    pick = jnp.where(node == lists_ref[...] - first, 1.0, 0.0).astype(BF16)
    rim = jnp.dot(out_ref[0], pick, preferred_element_type=F32)
    if rim_in_ref is not None:
        rim = rim + rim_in_ref[0].astype(F32)
    rim_ref[0] = rim.astype(BF16)


def gather_rows(mark, lists, own, got, rim, first, full):
    comps, rows, width = own.shape
    count = lists.shape[1]
    one = lambda r, n: pl.BlockSpec((1, r, n), lambda i: (i, 0, 0))
    specs = [ANY, pl.BlockSpec((1, count), lambda i: (0, 0)), one(rows, width), one(rows, width)]
    args = [mark, lists, own, got]
    if rim is not None:
        specs.append(one(full, count))
        args.append(rim)
    return pl.pallas_call(
        functools.partial(gather_rows_kernel, first),
        out_shape=(shaped((comps, full, width), BF16), shaped((comps, full, count), BF16)),
        grid=(comps,),
        in_specs=specs,
        out_specs=(one(full, width), one(full, count)),
        compiler_params=params(8),
        cost_estimate=cost(),
        name="gather_rows",
    )(*args)


NODE_BLOCK = 256
WIDE = 256
ROWS = 16
LANES = 128


def build_tiles(first, nodes, conn, grads, store):
    corners = conn.shape[0]
    base = lax.broadcasted_iota(jnp.int32, (ROWS, LANES), 0).astype(F32).astype(BF16)
    zero = jnp.zeros((ROWS, LANES), BF16)
    grads = grads.astype(BF16)
    grad = [jnp.broadcast_to(grads[i : i + 1, :], (ROWS, LANES)) for i in range(3 * corners)]
    for at in range(0, nodes, NODE_BLOCK):
        keys = (conn - (first + at)).astype(BF16)
        key = [jnp.broadcast_to(keys[a : a + 1, :], (ROWS, LANES)) for a in range(corners)]
        for row in range(0, NODE_BLOCK, ROWS):
            node = base + BF16(row)
            sums = [zero] * 3
            for a in range(corners):
                hit = node == key[a]
                for d in range(3):
                    sums[d] = jnp.where(hit, grad[d * corners + a], sums[d])
            for d in range(3):
                store(d, at + row, sums[d])


def weights_kernel(first, mark_ref, conn_ref, grads_ref, out_ref):
    del mark_ref

    def piece(step, carry):
        cut = pl.ds(pl.multiple_of(step * LANES, LANES), LANES)

        def store(d, row, value):
            out_ref[d, pl.ds(row, ROWS), cut] = value

        build_tiles(first, out_ref.shape[1], conn_ref[:, cut], grads_ref[:, cut], store)
        return carry

    lax.fori_loop(0, conn_ref.shape[1] // LANES, piece, 0)


def all_weights_kernel(mark_ref, conn_ref, grads_ref, out_ref, made, sems):
    del mark_ref
    blocks, _, nodes, _ = out_ref.shape
    _, _, count, wide = made.shape
    parts = nodes // count

    def copy(step, slot):
        rows = pl.ds(pl.multiple_of((step % parts) * count, count), count)
        return pltpu.make_async_copy(made.at[slot], out_ref.at[step // parts, :, rows, :], sems.at[slot])

    def pair(twice, carry):
        for slot in range(2):
            step = twice * 2 + slot

            @pl.when(twice > 0)
            def _():
                copy(step - 2, slot).wait()

            first = ((step % parts) * count).astype(F32)
            for lane in range(0, wide, LANES):
                cut = pl.ds(pl.multiple_of((step // parts) * wide + lane, LANES), LANES)

                def store(d, row, value):
                    made[slot, d, pl.ds(row, ROWS), pl.ds(lane, LANES)] = value

                build_tiles(first, count, conn_ref[:, cut], grads_ref[:, cut], store)
            copy(step, slot).start()
        return carry

    steps = blocks * parts
    lax.fori_loop(0, steps // 2, pair, 0)
    for slot in range(2):
        copy(steps - 2 + slot, slot).wait()


def all_weights(mark, data, nodes):
    elems = data.shape[1]
    count = nodes // 4
    return pl.pallas_call(
        all_weights_kernel,
        out_shape=shaped((elems // WIDE, 3, nodes, WIDE), BF16),
        in_specs=[ANY, VMEM, VMEM],
        out_specs=ANY,
        scratch_shapes=[pltpu.VMEM((2, 3, count, WIDE), BF16), pltpu.SemaphoreType.DMA((2,))],
        compiler_params=params(12),
        cost_estimate=cost(),
        name="all_weights",
    )(mark, data[:8], data[8:32])


def element_weights(mark, data, first, count):
    elems = data.shape[1]
    return pl.pallas_call(
        functools.partial(weights_kernel, float(first)),
        out_shape=shaped((3, count, elems), BF16),
        in_specs=[ANY, VMEM, VMEM],
        out_specs=VMEM,
        compiler_params=params(8),
        cost_estimate=cost(),
        name="element_weights",
    )(mark, data[:8], data[8:32])


def multiply_kernel(first, mark_ref, values_ref, weights_ref, *refs):
    del mark_ref
    acc_ref, out_ref, held, sems = refs if len(refs) == 4 else (None,) + refs
    comps, rows, nodes = values_ref.shape
    values = values_ref[...].reshape(comps * rows, nodes)
    blocks = weights_ref.shape[0]

    def copy(block, slot):
        return pltpu.make_async_copy(
            weights_ref.at[block, :, pl.ds(first, nodes), :], held.at[slot], sems.at[slot]
        )

    for slot in range(2):
        copy(slot, slot).start()

    def pair(twice, carry):
        for slot in range(2):
            block = twice * 2 + slot
            copy(block, slot).wait()
            cut = pl.ds(pl.multiple_of(block * WIDE, WIDE), WIDE)
            for d in range(3):
                term = jnp.dot(values, held[slot, d], preferred_element_type=F32)
                out_ref[d, :, cut] = term if acc_ref is None else term + acc_ref[d, :, cut]

            @pl.when(twice < blocks // 2 - 1)
            def _():
                copy(block + 2, slot).start()

        return carry

    lax.fori_loop(0, blocks // 2, pair, 0)


def multiply(mark, values, weights, first, acc):
    comps, rows, nodes = values.shape
    elems = weights.shape[0] * WIDE
    args = [mark, values, weights] + ([] if acc is None else [acc])
    return pl.pallas_call(
        functools.partial(multiply_kernel, first),
        out_shape=shaped((3, comps * rows, elems), F32),
        in_specs=[ANY, VMEM, ANY] + [VMEM] * (len(args) - 3),
        out_specs=VMEM,
        input_output_aliases={} if acc is None else {3: 0},
        scratch_shapes=[pltpu.VMEM((2, 3, nodes, WIDE), BF16), pltpu.SemaphoreType.DMA((2,))],
        compiler_params=params(20),
        cost_estimate=cost(),
        name="multiply",
    )(*args)


def spectra_kernel(before_ref, after_ref, weights_ref, acc_ref, modulus_ref, out_ref, grads):
    comps, rows, rim = before_ref.shape
    half = rows // 4
    groups, _, count = out_ref.shape
    per = count // WIDE
    before = before_ref[...].reshape(comps * rows, rim)
    after = after_ref[...].reshape(comps * rows, rim)

    def finish(group, place, lanes_at, modulus):
        lame = modulus * (POISSON / ((1.0 + POISSON) * (1.0 - 2.0 * POISSON)))
        shear = modulus * (1.0 / (2.0 * (1.0 + POISSON)))
        twice = 2.0 * shear
        lanes = pl.ds(lanes_at, LANES)

        def stress(top):
            def at(c, d):
                return grads[d, c * rows + top : c * rows + top + 8, lanes]

            volume = lame * (at(0, 0) + at(1, 1) + at(2, 2))
            return [
                volume + twice * at(0, 0),
                volume + twice * at(1, 1),
                volume + twice * at(2, 2),
                shear * (at(1, 2) + at(2, 1)),
                shear * (at(2, 0) + at(0, 2)),
                shear * (at(0, 1) + at(1, 0)),
            ]

        pairs = [(i, j, 0) for i in range(6) for j in range(i, 6)]
        pairs += [(i, j, 1) for i in range(6) for j in range(i + 1, 6)]
        totals = [None] * len(pairs)
        for top in [s * 2 * half + p for s in range(2) for p in range(0, half, 8)]:
            re = stress(top)
            im = stress(top + half)
            for n, (i, j, turned) in enumerate(pairs):
                if turned:
                    term = im[i] * re[j] - re[i] * im[j]
                else:
                    term = re[i] * re[j] + im[i] * im[j]
                totals[n] = term if totals[n] is None else totals[n] + term
        for n in range(len(pairs)):
            out_ref[group, pl.ds(n, 1), pl.ds(place, LANES)] = jnp.sum(totals[n], axis=0, keepdims=True)

    def piece(step, carry):
        cut = pl.ds(pl.multiple_of(step * WIDE, WIDE), WIDE)
        for d in range(3):
            grads[d] = (
                acc_ref[d, :, cut]
                + jnp.dot(before, weights_ref[d, :rim, cut], preferred_element_type=F32)
                + jnp.dot(after, weights_ref[d, rim:, cut], preferred_element_type=F32)
            )
        group = step // per
        start = (step % per) * WIDE
        for at in range(0, WIDE, LANES):
            here = pl.ds(pl.multiple_of(step * WIDE + at, LANES), LANES)
            finish(group, pl.multiple_of(start + at, LANES), at, modulus_ref[:1, here])
        return carry

    lax.fori_loop(0, groups * per, piece, 0)


def element_spectra(before, after, weights, acc, modulus):
    comps, rows, rim = before.shape
    elems = weights.shape[2]
    return pl.pallas_call(
        spectra_kernel,
        out_shape=shaped((Z, 36, elems // Z), F32),
        in_specs=[VMEM] * 5,
        out_specs=VMEM,
        scratch_shapes=[pltpu.VMEM((3, comps * rows, WIDE), F32)],
        compiler_params=params(8),
        cost_estimate=cost(),
        name="element_spectra",
    )(before, after, weights, acc, modulus)


def collect_kernel(place_ref, a_ref, b_ref, c_ref, d_ref, out_ref):
    for j, ref in enumerate((a_ref, b_ref, c_ref, d_ref)):
        out_ref[pl.ds((place_ref[0] + Z - j) % Z, 1)] = ref[...][None]


def collect(place, blocks):
    return pl.pallas_call(
        collect_kernel,
        out_shape=shaped((Z,) + blocks[0].shape, F32),
        in_specs=[SMEM] + [VMEM] * Z,
        out_specs=VMEM,
        compiler_params=params(8),
        cost_estimate=cost(),
        name="collect",
    )(place, *blocks)


def local(
    mode_shapes,
    load_nodal,
    mode_freq,
    damping,
    drive_freq,
    send_lists,
    connectivity,
    shape_grads,
    modulus,
):
    modes, _, nodes = mode_shapes.shape
    cols = load_nodal.shape[2]
    bound = send_lists.shape[1]
    freqs = drive_freq.shape[0]
    rows = cols // (Z * XLO)
    mode_at = lax.axis_index("mode")
    z_at, x_at = mode_at // XLO, mode_at % XLO
    core = (lax.axis_index("mesh") % CORE).astype(jnp.int32)
    core_arg = core.reshape(1)
    shapes = jnp.transpose(mode_shapes, (1, 0, 2))
    lists = send_lists.reshape(1, -1)

    pad = 2 * HALF - modes
    natural = jnp.pad(mode_freq, (0, pad), constant_values=1.0)[:, None]
    loss = jnp.pad(damping, (0, pad), constant_values=0.5)[:, None]
    natural = lax.dynamic_slice_in_dim(natural, core * HALF, HALF)
    loss = lax.dynamic_slice_in_dim(loss, core * HALF, HALF)
    forcing = jnp.repeat(drive_freq, cols // freqs)[None, :]
    gap = natural * natural - forcing * forcing
    damp = 2.0 * loss * natural * forcing
    size = gap * gap + damp * damp
    sign = jnp.where(jnp.arange(cols) % 2 == 0, 1.0, -1.0).astype(F32)[None, :]
    direct = gap / size
    cross = sign * (damp / size)

    spot = jnp.arange(cols)
    block, inside = spot // rows, spot % rows
    block = mode_index(z_at + block // XLO, x_at ^ (block % XLO))
    source = block * rows + 2 * (inside % (rows // 2)) + inside // (rows // 2)
    order = (source[:, None] == spot[None, :]).astype(BF16)

    mine, theirs = partial_loads(core_arg, shapes, load_nodal)
    got = lax.ppermute(theirs, "mesh", mesh_perm(0, 0, 1))
    chip = (mine + got.astype(F32)).astype(BF16)
    got = lax.ppermute(chip, "mesh", mesh_perm(0, 1, 0))
    pair = (chip.astype(F32) + got.astype(F32)).astype(BF16)
    ring = [pair] + [lax.ppermute(pair, "mesh", mesh_perm(dy)) for dy in range(1, Y)]

    data = element_data(chip, connectivity, shape_grads, modulus)
    data = jnp.concatenate(
        [data] + [lax.ppermute(data, "mode", mode_perm(-j)) for j in range(1, Z)], axis=1
    )
    up_perm, down_perm, side_perm = mode_perm(1), mode_perm(-1), mode_perm(0, 1)
    up = lambda v: lax.ppermute(v, "mode", up_perm)
    down = lambda v: lax.ppermute(v, "mode", down_perm)
    side = lambda v: lax.ppermute(v, "mode", side_perm)
    full = 2 * rows

    w_0 = nodes * 7 // 16
    w_1 = nodes - w_0
    c_0, c_1 = (0, w_0), (w_0, w_1)
    middle = w_0 + w_1 // 2

    resp_mine = half_response(data, ring, direct, cross)
    resp_theirs = lax.ppermute(resp_mine, "mesh", mesh_perm(0, 0, 1))
    away, keep, resp = x_first_terms(core_arg, resp_mine, resp_theirs, order, shapes, c_0, 43)
    got_0 = side(away)
    ways_1 = z_first_terms(keep, resp, shapes, c_1, 43)
    plus_1, minus_1 = up(ways_1[0]), down(ways_1[1])
    weights = all_weights(ways_1[2], data, nodes)
    rim_weights = element_weights(weights, data, nodes, 2 * bound)
    on_1 = pass_on(rim_weights, ways_1[2], ways_1[3], plus_1, minus_1)
    up_1, down_1 = up(on_1[0]), down(on_1[1])
    ways_0 = x_sum(on_1[0], keep, got_0)
    plus_0, minus_0 = up(ways_0[0]), down(ways_0[1])
    low_1 = half_sum(ways_0[2], ways_0[2], 0, ways_1[4], minus_1, up_1)
    side_low = side(low_1)
    high_1 = half_sum(low_1, low_1, 1, ways_1[4], plus_1, down_1)
    side_high = side(high_1)
    on_0 = pass_on(high_1, ways_0[2], ways_0[3], plus_0, minus_0)
    up_0, down_0 = up(on_0[0]), down(on_0[1])
    values_low, rim = gather_rows(on_0[0], lists, low_1, side_low, None, w_0, full)
    acc = multiply(rim, values_low, weights, w_0, None)
    own_0 = ring_sum(acc, ways_0[4], plus_0, minus_0, up_0, down_0)
    side_0 = side(own_0)
    values_high, rim = gather_rows(own_0, lists, high_1, side_high, rim, middle, full)
    acc = multiply(rim, values_high, weights, middle, acc)
    values_0, rim = gather_rows(acc, lists, own_0, side_0, rim, 0, full)

    count = lax.axis_size("mesh")
    before = lax.ppermute(rim[..., bound:], "mesh", [(p, p + 1) for p in range(count - 1)])
    after = lax.ppermute(rim[..., :bound], "mesh", [(p + 1, p) for p in range(count - 1)])
    acc = multiply(rim, values_0, weights, 0, acc)
    spectra = element_spectra(before, after, rim_weights, acc, data[32:40])
    back = [spectra[0]] + [lax.ppermute(spectra[j], "mode", mode_perm(j)) for j in range(1, Z)]
    return collect(z_at.astype(jnp.int32).reshape(1), back)


def solution(mesh):
    in_specs = (
        P("mode", None, "mesh"),
        P(None, "mesh", None),
        P("mode"),
        P("mode"),
        P(),
        P(None, "mesh"),
        P(None, ("mesh", "mode")),
        P(None, None, ("mesh", "mode")),
        P(("mesh", "mode")),
    )
    out_specs = P(None, None, ("mesh", "mode"))
    return jax.shard_map(local, mesh=mesh, in_specs=in_specs, out_specs=out_specs, check_vma=False)
```

```python
import functools

import jax
import jax.numpy as jnp
from jax import lax
from jax.experimental import pallas as pl
from jax.experimental.pallas import tpu as pltpu
from jax.sharding import PartitionSpec as P

POISSON = 0.3
F32 = jnp.float32
BF16 = jnp.bfloat16
MIB = 1024 * 1024
Z, XLO = 4, 2
Y, XHI, CORE = 4, 2, 2
HALF = 256
ANY = pl.BlockSpec(memory_space=pl.ANY)
VMEM = pl.BlockSpec(memory_space=pltpu.VMEM)
HBM = pl.BlockSpec(memory_space=pltpu.HBM)
SMEM = pl.BlockSpec(memory_space=pltpu.SMEM)


def params(mib):
    return pltpu.CompilerParams(vmem_limit_bytes=mib * MIB)


def cost(flops=1, moved=1):
    return pl.CostEstimate(flops=flops, bytes_accessed=moved, transcendentals=0)


def shaped(shape, kind):
    return jax.ShapeDtypeStruct(shape, kind)


def mode_index(z, x):
    return (z % Z) * XLO + x


def mesh_index(y, h, c):
    return ((y % Y) * XHI + h) * CORE + c


def mode_perm(dz, flip=0):
    return [(mode_index(z, x), mode_index(z + dz, x ^ flip)) for z in range(Z) for x in range(XLO)]


def mesh_perm(dy, flip_h=0, flip_c=0):
    return [
        (mesh_index(y, h, c), mesh_index(y + dy, h ^ flip_h, c ^ flip_c))
        for y in range(Y)
        for h in range(XHI)
        for c in range(CORE)
    ]


def loads_kernel(cuts, core_ref, shapes_ref, load_ref, mine_ref, theirs_ref, shapes, load, acc, shape_sems, load_sems):
    modes = shapes.shape[1]

    def copies(i):
        c, at, width = cuts[i]
        cut = pl.ds(at, width)
        return (
            pltpu.make_async_copy(shapes_ref.at[c, :, cut], shapes.at[c, :, cut], shape_sems.at[i]),
            pltpu.make_async_copy(load_ref.at[c, cut, :], load.at[c, cut, :], load_sems.at[i]),
        )

    for i in range(len(cuts)):
        for copy in copies(i):
            copy.start()
    acc[modes:, :] = jnp.zeros((acc.shape[0] - modes, acc.shape[1]), F32)
    for i, (c, at, width) in enumerate(cuts):
        for copy in copies(i):
            copy.wait()
        cut = pl.ds(at, width)
        term = jnp.dot(shapes[c, :, cut], load[c, cut, :], preferred_element_type=F32)
        acc[:modes, :] = term if i == 0 else acc[:modes, :] + term
    core = core_ref[0]
    mine_ref[...] = acc[pl.ds(core * HALF, HALF), :]
    theirs_ref[...] = acc[pl.ds((1 - core) * HALF, HALF), :].astype(BF16)


def partial_loads(core, shapes, load):
    comps, modes, nodes = shapes.shape
    cols = load.shape[2]
    block = 1024
    cuts = [(c, at, block) for c in range(comps) for at in range(0, nodes, block)]
    vmem = pl.BlockSpec(memory_space=pltpu.VMEM)
    return pl.pallas_call(
        functools.partial(loads_kernel, cuts),
        out_shape=(shaped((HALF, cols), F32), shaped((HALF, cols), BF16)),
        in_specs=[SMEM, HBM, HBM],
        out_specs=(vmem, vmem),
        scratch_shapes=[
            pltpu.VMEM(shapes.shape, BF16),
            pltpu.VMEM(load.shape, BF16),
            pltpu.VMEM((2 * HALF, cols), F32),
            pltpu.SemaphoreType.DMA((len(cuts),)),
            pltpu.SemaphoreType.DMA((len(cuts),)),
        ],
        compiler_params=params(56),
        cost_estimate=cost(),
        name="modal_loads",
    )(core, shapes, load)


def response_kernel(mark_ref, a_ref, b_ref, c_ref, d_ref, direct_ref, cross_ref, out_ref):
    del mark_ref
    total = (
        a_ref[...].astype(F32)
        + b_ref[...].astype(F32)
        + c_ref[...].astype(F32)
        + d_ref[...].astype(F32)
    )
    cols = total.shape[1]
    even = lax.broadcasted_iota(jnp.int32, total.shape, 1) % 2 == 0
    other = jnp.where(even, pltpu.roll(total, cols - 1, 1), pltpu.roll(total, 1, 1))
    out_ref[...] = (direct_ref[...] * total + cross_ref[...] * other).astype(BF16)


def half_response(mark, parts, direct, cross):
    vmem = pl.BlockSpec(memory_space=pltpu.VMEM)
    return pl.pallas_call(
        response_kernel,
        out_shape=shaped(direct.shape, BF16),
        in_specs=[ANY] + [vmem] * 6,
        out_specs=vmem,
        compiler_params=params(8),
        cost_estimate=cost(),
        name="modal_response",
    )(mark, *parts, direct, cross)


def element_data_kernel(mark_ref, conn_ref, grads_ref, modulus_ref, out_ref):
    del mark_ref
    corners, width = conn_ref.shape
    conn = conn_ref[...].astype(F32)
    out_ref[:corners, :] = conn
    for d in range(3):
        total = jnp.zeros((corners, width), F32)
        for a in range(corners):
            total = total + jnp.where(conn == conn[a : a + 1, :], grads_ref[d, a : a + 1, :], 0.0)
        out_ref[(d + 1) * corners : (d + 2) * corners, :] = total
    out_ref[4 * corners :, :] = jnp.broadcast_to(modulus_ref[...], (corners, width))


def element_data(mark, conn, grads, modulus):
    corners, elems = conn.shape
    vmem = pl.BlockSpec(memory_space=pltpu.VMEM)
    return pl.pallas_call(
        element_data_kernel,
        out_shape=shaped((5 * corners, elems), F32),
        in_specs=[ANY, vmem, vmem, vmem],
        out_specs=vmem,
        compiler_params=params(8),
        cost_estimate=cost(),
        name="element_data",
    )(mark, conn, grads, modulus[None, :])


def split_ways(blocks, plus_ref, minus_ref, up_ref, down_ref, own_ref):
    half = up_ref.shape[-1]
    low = [b[..., :half] for b in blocks]
    high = [b[..., half:] for b in blocks]
    plus_ref[0, 0] = low[2]
    plus_ref[1, 0] = high[1]
    minus_ref[0, 0] = high[2]
    minus_ref[1, 0] = low[3]
    up_ref[0] = low[1]
    down_ref[0] = high[3]
    own_ref[0] = blocks[0]


def way_shapes(comps, rows, width):
    half = width // 2
    shapes = (
        (2, comps, rows, half),
        (2, comps, rows, half),
        (comps, rows, half),
        (comps, rows, half),
        (comps, rows, width),
    )
    specs = tuple(
        pl.BlockSpec((2, 1) + s[2:], lambda i: (0, i, 0, 0))
        if len(s) == 4
        else pl.BlockSpec((1,) + s[1:], lambda i: (i, 0, 0))
        for s in shapes
    )
    return tuple(shaped(s, BF16) for s in shapes), specs


def fetch_shapes(first, shapes_ref, held, sems):
    step = pl.program_id(0)
    cut = pl.ds(first, held.shape[2])

    @pl.when(step == 0)
    def _():
        for c in range(held.shape[0]):
            pltpu.make_async_copy(shapes_ref.at[c, :, cut], held.at[c], sems.at[c]).start()

    pltpu.make_async_copy(shapes_ref.at[step, :, cut], held.at[step], sems.at[step]).wait()
    return held[step]


def fetch_scratch(shapes, width):
    comps, modes, _ = shapes.shape
    return [pltpu.VMEM((comps, modes, width), BF16), pltpu.SemaphoreType.DMA((comps,))]


def z_first_kernel(first, mark_ref, resp_ref, shapes_ref, *refs):
    del mark_ref
    out_refs, (held, sems) = refs[:5], refs[5:]
    part = fetch_shapes(first, shapes_ref, held, sems)
    value = jnp.dot(resp_ref[...], part, preferred_element_type=F32).astype(BF16)
    rows = value.shape[0] // Z
    split_ways([value[j * rows : (j + 1) * rows, :] for j in range(Z)], *out_refs)


def z_first_terms(mark, resp, shapes, chunk, mib):
    first, width = chunk
    comps, modes, _ = shapes.shape
    cols = resp.shape[0]
    out_shape, out_specs = way_shapes(comps, cols // Z, width)
    return pl.pallas_call(
        functools.partial(z_first_kernel, first),
        out_shape=out_shape,
        grid=(comps,),
        in_specs=[ANY, pl.BlockSpec((cols, modes), lambda i: (0, 0)), HBM],
        out_specs=out_specs,
        scratch_shapes=fetch_scratch(shapes, width),
        compiler_params=params(mib),
        cost_estimate=cost(),
        name="z_first_terms",
    )(mark, resp, shapes)


def x_first_kernel(
    first, core_ref, mine_ref, theirs_ref, order_ref, shapes_ref, away_ref, keep_ref, turned_ref, resp, held, sems
):
    modes = shapes_ref.shape[1]
    part = fetch_shapes(first, shapes_ref, held, sems)

    @pl.when(pl.program_id(0) == 0)
    def _():
        core = core_ref[0]
        resp[pl.ds(core * HALF, HALF), :] = mine_ref[...]
        resp[pl.ds((1 - core) * HALF, HALF), :] = theirs_ref[...]
        turned = lax.dot_general(
            order_ref[...], resp[...], (((1,), (1,)), ((), ())), preferred_element_type=F32
        )
        turned_ref[...] = turned[:, :modes].astype(BF16)

    value = jnp.dot(turned_ref[...], part, preferred_element_type=F32).astype(BF16)
    rows = value.shape[0] // (Z * XLO)
    for j in range(Z):
        keep_ref[j, 0] = value[(2 * j) * rows : (2 * j + 1) * rows, :]
        away_ref[j, 0] = value[(2 * j + 1) * rows : (2 * j + 2) * rows, :]


def x_first_terms(core, mine, theirs, order, shapes, chunk, mib):
    first, width = chunk
    comps, modes, _ = shapes.shape
    cols = mine.shape[1]
    rows = cols // (Z * XLO)
    part = pl.BlockSpec((Z, 1, rows, width), lambda i: (0, i, 0, 0))
    whole = lambda i: (0, 0)
    return pl.pallas_call(
        functools.partial(x_first_kernel, first),
        out_shape=(
            shaped((Z, comps, rows, width), BF16),
            shaped((Z, comps, rows, width), BF16),
            shaped((cols, modes), BF16),
        ),
        grid=(comps,),
        in_specs=[
            SMEM,
            pl.BlockSpec((HALF, cols), whole),
            pl.BlockSpec((HALF, cols), whole),
            pl.BlockSpec((cols, cols), whole),
            HBM,
        ],
        out_specs=(part, part, pl.BlockSpec((cols, modes), whole)),
        scratch_shapes=[pltpu.VMEM((2 * HALF, cols), BF16)] + fetch_scratch(shapes, width),
        compiler_params=params(mib),
        cost_estimate=cost(),
        name="x_first_terms",
    )(core, mine, theirs, order, shapes)


def x_sum_kernel(mark_ref, keep_ref, got_ref, *out_refs):
    del mark_ref
    blocks = [(keep_ref[j, 0].astype(F32) + got_ref[j, 0].astype(F32)).astype(BF16) for j in range(Z)]
    split_ways(blocks, *out_refs)


def x_sum(mark, keep, got):
    _, comps, rows, width = keep.shape
    out_shape, out_specs = way_shapes(comps, rows, width)
    part = pl.BlockSpec((Z, 1, rows, width), lambda i: (0, i, 0, 0))
    return pl.pallas_call(
        x_sum_kernel,
        out_shape=out_shape,
        grid=(comps,),
        in_specs=[ANY, part, part],
        out_specs=out_specs,
        compiler_params=params(8),
        cost_estimate=cost(),
        name="x_sum",
    )(mark, keep, got)


def pass_on_kernel(mark_ref, up_ref, down_ref, plus_ref, minus_ref, up_out, down_out):
    del mark_ref
    up_out[...] = (up_ref[...].astype(F32) + plus_ref[0].astype(F32)).astype(BF16)
    down_out[...] = (down_ref[...].astype(F32) + minus_ref[0].astype(F32)).astype(BF16)


def pass_on(mark, up, down, plus, minus):
    comps, rows, half = up.shape
    one = pl.BlockSpec((1, rows, half), lambda i: (i, 0, 0))
    first = pl.BlockSpec((1, 1, rows, half), lambda i: (0, i, 0, 0))
    return pl.pallas_call(
        pass_on_kernel,
        out_shape=(shaped(up.shape, BF16), shaped(up.shape, BF16)),
        grid=(comps,),
        in_specs=[ANY, one, one, first, first],
        out_specs=(one, one),
        compiler_params=params(8),
        cost_estimate=cost(),
        name="pass_on",
    )(mark, up, down, plus, minus)


def ring_sum_kernel(mark_ref, own_ref, plus_ref, minus_ref, up_ref, down_ref, out_ref):
    del mark_ref
    half = up_ref.shape[2]
    low = own_ref[0, :, :half].astype(F32) + minus_ref[0, 0].astype(F32) + up_ref[0].astype(F32)
    high = own_ref[0, :, half:].astype(F32) + plus_ref[0, 0].astype(F32) + down_ref[0].astype(F32)
    out_ref[0, :, :half] = low.astype(BF16)
    out_ref[0, :, half:] = high.astype(BF16)


def ring_sum(mark, own, plus, minus, up, down):
    comps, rows, width = own.shape
    one = lambda n: pl.BlockSpec((1, rows, n), lambda i: (i, 0, 0))
    second = pl.BlockSpec((1, 1, rows, width // 2), lambda i: (1, i, 0, 0))
    return pl.pallas_call(
        ring_sum_kernel,
        out_shape=shaped(own.shape, BF16),
        grid=(comps,),
        in_specs=[ANY, one(width), second, second, one(width // 2), one(width // 2)],
        out_specs=one(width),
        compiler_params=params(8),
        cost_estimate=cost(),
        name="ring_sum",
    )(mark, own, plus, minus, up, down)


def half_sum_kernel(mark_ref, after_ref, own_ref, direct_ref, passed_ref, out_ref):
    del mark_ref, after_ref
    total = own_ref[...].astype(F32) + direct_ref[0].astype(F32) + passed_ref[...].astype(F32)
    out_ref[...] = total.astype(BF16)


def half_sum(mark, after, side, own, direct, passed):
    comps, rows, half = passed.shape
    one = pl.BlockSpec((1, rows, half), lambda i: (i, 0, 0))
    return pl.pallas_call(
        half_sum_kernel,
        out_shape=shaped(passed.shape, BF16),
        grid=(comps,),
        in_specs=[
            ANY,
            ANY,
            pl.BlockSpec((1, rows, half), lambda i: (i, 0, side)),
            pl.BlockSpec((1, 1, rows, half), lambda i: (1, i, 0, 0)),
            one,
        ],
        out_specs=one,
        compiler_params=params(8),
        cost_estimate=cost(),
        name="half_sum",
    )(mark, after, own, direct, passed)


def gather_rows_kernel(first, mark_ref, lists_ref, own_ref, got_ref, *refs):
    del mark_ref
    rim_in_ref, out_ref, rim_ref = refs if len(refs) == 3 else (None,) + refs
    rows = own_ref.shape[1]
    width = own_ref.shape[2]
    if rows == out_ref.shape[1]:
        half = rows // 2
        own = own_ref[0].astype(F32)
        got = got_ref[0].astype(F32)
        out_ref[0, :half, :] = (own[:half] + got[half:]).astype(BF16)
        out_ref[0, half:, :] = (own[half:] + got[:half]).astype(BF16)
    else:
        out_ref[0, :rows, :] = own_ref[0]
        out_ref[0, rows:, :] = got_ref[0]
    node = lax.broadcasted_iota(jnp.int32, (width, lists_ref.shape[1]), 0)
    pick = jnp.where(node == lists_ref[...] - first, 1.0, 0.0).astype(BF16)
    rim = jnp.dot(out_ref[0], pick, preferred_element_type=F32)
    if rim_in_ref is not None:
        rim = rim + rim_in_ref[0].astype(F32)
    rim_ref[0] = rim.astype(BF16)


def gather_rows(mark, lists, own, got, rim, first, full):
    comps, rows, width = own.shape
    count = lists.shape[1]
    one = lambda r, n: pl.BlockSpec((1, r, n), lambda i: (i, 0, 0))
    specs = [ANY, pl.BlockSpec((1, count), lambda i: (0, 0)), one(rows, width), one(rows, width)]
    args = [mark, lists, own, got]
    if rim is not None:
        specs.append(one(full, count))
        args.append(rim)
    return pl.pallas_call(
        functools.partial(gather_rows_kernel, first),
        out_shape=(shaped((comps, full, width), BF16), shaped((comps, full, count), BF16)),
        grid=(comps,),
        in_specs=specs,
        out_specs=(one(full, width), one(full, count)),
        compiler_params=params(8),
        cost_estimate=cost(),
        name="gather_rows",
    )(*args)


NODE_BLOCK = 256
WIDE = 256
ROWS = 16
LANES = 128


def build_tiles(first, nodes, conn, grads, store):
    corners = conn.shape[0]
    base = lax.broadcasted_iota(jnp.int32, (ROWS, LANES), 0).astype(F32).astype(BF16)
    zero = jnp.zeros((ROWS, LANES), BF16)
    grads = grads.astype(BF16)
    grad = [jnp.broadcast_to(grads[i : i + 1, :], (ROWS, LANES)) for i in range(3 * corners)]
    for at in range(0, nodes, NODE_BLOCK):
        keys = (conn - (first + at)).astype(BF16)
        key = [jnp.broadcast_to(keys[a : a + 1, :], (ROWS, LANES)) for a in range(corners)]
        for row in range(0, NODE_BLOCK, ROWS):
            node = base + BF16(row)
            sums = [zero] * 3
            for a in range(corners):
                hit = node == key[a]
                for d in range(3):
                    sums[d] = jnp.where(hit, grad[d * corners + a], sums[d])
            for d in range(3):
                store(d, at + row, sums[d])


def weights_kernel(first, mark_ref, conn_ref, grads_ref, out_ref):
    del mark_ref

    def piece(step, carry):
        cut = pl.ds(pl.multiple_of(step * LANES, LANES), LANES)

        def store(d, row, value):
            out_ref[d, pl.ds(row, ROWS), cut] = value

        build_tiles(first, out_ref.shape[1], conn_ref[:, cut], grads_ref[:, cut], store)
        return carry

    lax.fori_loop(0, conn_ref.shape[1] // LANES, piece, 0)


def all_weights_kernel(mark_ref, conn_ref, grads_ref, out_ref, made, sems):
    del mark_ref
    blocks, _, nodes, _ = out_ref.shape
    slots, _, count, wide = made.shape
    parts = nodes // count

    def copies(block, part, slot):
        rows = pl.ds(part * count, count)
        return [
            pltpu.make_async_copy(made.at[slot, d], out_ref.at[block, d, rows, :], sems.at[slot, d])
            for d in range(3)
        ]

    def block_of_elements(block, carry):
        for part in range(parts):
            slot = part % slots

            @pl.when(block > 0)
            def _():
                for copy in copies(block - 1, part, slot):
                    copy.wait()

            for lane in range(0, wide, LANES):
                cut = pl.ds(pl.multiple_of(block * wide + lane, LANES), LANES)

                def store(d, row, value):
                    made[slot, d, pl.ds(row, ROWS), pl.ds(lane, LANES)] = value

                build_tiles(float(part * count), count, conn_ref[:, cut], grads_ref[:, cut], store)
            for copy in copies(block, part, slot):
                copy.start()
        return carry

    lax.fori_loop(0, blocks, block_of_elements, 0)
    for part in range(parts):
        for copy in copies(blocks - 1, part, part):
            copy.wait()


def all_weights(mark, data, nodes):
    elems = data.shape[1]
    slots = 4
    count = nodes // slots
    return pl.pallas_call(
        all_weights_kernel,
        out_shape=shaped((elems // WIDE, 3, nodes, WIDE), BF16),
        in_specs=[ANY, VMEM, VMEM],
        out_specs=ANY,
        scratch_shapes=[pltpu.VMEM((slots, 3, count, WIDE), BF16), pltpu.SemaphoreType.DMA((slots, 3))],
        compiler_params=params(16),
        cost_estimate=cost(),
        name="all_weights",
    )(mark, data[:8], data[8:32])


def element_weights(mark, data, first, count):
    elems = data.shape[1]
    return pl.pallas_call(
        functools.partial(weights_kernel, float(first)),
        out_shape=shaped((3, count, elems), BF16),
        in_specs=[ANY, VMEM, VMEM],
        out_specs=VMEM,
        compiler_params=params(8),
        cost_estimate=cost(),
        name="element_weights",
    )(mark, data[:8], data[8:32])


SLOTS = 4


def multiply_kernel(first, mark_ref, values_ref, weights_ref, *refs):
    del mark_ref
    acc_ref, out_ref, held, sems = refs if len(refs) == 4 else (None,) + refs
    comps, rows, nodes = values_ref.shape
    values = values_ref[...].reshape(comps * rows, nodes)
    blocks = weights_ref.shape[0]

    def copy(block, slot, d):
        return pltpu.make_async_copy(
            weights_ref.at[block, d, pl.ds(first, nodes), :], held.at[slot, d], sems.at[slot, d]
        )

    for slot in range(SLOTS):
        for d in range(3):
            copy(slot, slot, d).start()

    def turn(step, carry):
        for slot in range(SLOTS):
            block = step * SLOTS + slot
            cut = pl.ds(pl.multiple_of(block * WIDE, WIDE), WIDE)
            for d in range(3):
                copy(block, slot, d).wait()
                term = jnp.dot(values, held[slot, d], preferred_element_type=F32)
                out_ref[d, :, cut] = term if acc_ref is None else term + acc_ref[d, :, cut]

                @pl.when(step < blocks // SLOTS - 1)
                def _():
                    copy(block + SLOTS, slot, d).start()

        return carry

    lax.fori_loop(0, blocks // SLOTS, turn, 0)


def multiply(mark, values, weights, first, acc):
    comps, rows, nodes = values.shape
    elems = weights.shape[0] * WIDE
    args = [mark, values, weights] + ([] if acc is None else [acc])
    return pl.pallas_call(
        functools.partial(multiply_kernel, first),
        out_shape=shaped((3, comps * rows, elems), F32),
        in_specs=[ANY, VMEM, ANY] + [VMEM] * (len(args) - 3),
        out_specs=VMEM,
        input_output_aliases={} if acc is None else {3: 0},
        scratch_shapes=[pltpu.VMEM((SLOTS, 3, nodes, WIDE), BF16), pltpu.SemaphoreType.DMA((SLOTS, 3))],
        compiler_params=params(24),
        cost_estimate=cost(),
        name="multiply",
    )(*args)


def spectra_kernel(before_ref, after_ref, weights_ref, acc_ref, modulus_ref, out_ref, grads):
    comps, rows, rim = before_ref.shape
    half = rows // 4
    groups, _, count = out_ref.shape
    per = count // WIDE
    before = before_ref[...].reshape(comps * rows, rim)
    after = after_ref[...].reshape(comps * rows, rim)

    def finish(group, place, lanes_at, modulus):
        lame = modulus * (POISSON / ((1.0 + POISSON) * (1.0 - 2.0 * POISSON)))
        shear = modulus * (1.0 / (2.0 * (1.0 + POISSON)))
        twice = 2.0 * shear
        lanes = pl.ds(lanes_at, LANES)

        def stress(top):
            def at(c, d):
                return grads[d, c * rows + top : c * rows + top + 8, lanes]

            volume = lame * (at(0, 0) + at(1, 1) + at(2, 2))
            return [
                volume + twice * at(0, 0),
                volume + twice * at(1, 1),
                volume + twice * at(2, 2),
                shear * (at(1, 2) + at(2, 1)),
                shear * (at(2, 0) + at(0, 2)),
                shear * (at(0, 1) + at(1, 0)),
            ]

        pairs = [(i, j, 0) for i in range(6) for j in range(i, 6)]
        pairs += [(i, j, 1) for i in range(6) for j in range(i + 1, 6)]
        totals = [None] * len(pairs)
        for top in [s * 2 * half + p for s in range(2) for p in range(0, half, 8)]:
            re = stress(top)
            im = stress(top + half)
            for n, (i, j, turned) in enumerate(pairs):
                if turned:
                    term = im[i] * re[j] - re[i] * im[j]
                else:
                    term = re[i] * re[j] + im[i] * im[j]
                totals[n] = term if totals[n] is None else totals[n] + term
        for n in range(len(pairs)):
            out_ref[group, pl.ds(n, 1), pl.ds(place, LANES)] = jnp.sum(totals[n], axis=0, keepdims=True)

    def piece(step, carry):
        cut = pl.ds(pl.multiple_of(step * WIDE, WIDE), WIDE)
        for d in range(3):
            grads[d] = (
                acc_ref[d, :, cut]
                + jnp.dot(before, weights_ref[d, :rim, cut], preferred_element_type=F32)
                + jnp.dot(after, weights_ref[d, rim:, cut], preferred_element_type=F32)
            )
        group = step // per
        start = (step % per) * WIDE
        for at in range(0, WIDE, LANES):
            here = pl.ds(pl.multiple_of(step * WIDE + at, LANES), LANES)
            finish(group, pl.multiple_of(start + at, LANES), at, modulus_ref[:1, here])
        return carry

    lax.fori_loop(0, groups * per, piece, 0)


def element_spectra(before, after, weights, acc, modulus):
    comps, rows, rim = before.shape
    elems = weights.shape[2]
    return pl.pallas_call(
        spectra_kernel,
        out_shape=shaped((Z, 36, elems // Z), F32),
        in_specs=[VMEM] * 5,
        out_specs=VMEM,
        scratch_shapes=[pltpu.VMEM((3, comps * rows, WIDE), F32)],
        compiler_params=params(8),
        cost_estimate=cost(),
        name="element_spectra",
    )(before, after, weights, acc, modulus)


def collect_kernel(place_ref, a_ref, b_ref, c_ref, d_ref, out_ref):
    for j, ref in enumerate((a_ref, b_ref, c_ref, d_ref)):
        out_ref[pl.ds((place_ref[0] + Z - j) % Z, 1)] = ref[...][None]


def collect(place, blocks):
    return pl.pallas_call(
        collect_kernel,
        out_shape=shaped((Z,) + blocks[0].shape, F32),
        in_specs=[SMEM] + [VMEM] * Z,
        out_specs=VMEM,
        compiler_params=params(8),
        cost_estimate=cost(),
        name="collect",
    )(place, *blocks)


def local(
    mode_shapes,
    load_nodal,
    mode_freq,
    damping,
    drive_freq,
    send_lists,
    connectivity,
    shape_grads,
    modulus,
):
    modes, _, nodes = mode_shapes.shape
    cols = load_nodal.shape[2]
    bound = send_lists.shape[1]
    freqs = drive_freq.shape[0]
    rows = cols // (Z * XLO)
    mode_at = lax.axis_index("mode")
    z_at, x_at = mode_at // XLO, mode_at % XLO
    core = (lax.axis_index("mesh") % CORE).astype(jnp.int32)
    core_arg = core.reshape(1)
    shapes = jnp.transpose(mode_shapes, (1, 0, 2))
    lists = send_lists.reshape(1, -1)

    pad = 2 * HALF - modes
    natural = jnp.pad(mode_freq, (0, pad), constant_values=1.0)[:, None]
    loss = jnp.pad(damping, (0, pad), constant_values=0.5)[:, None]
    natural = lax.dynamic_slice_in_dim(natural, core * HALF, HALF)
    loss = lax.dynamic_slice_in_dim(loss, core * HALF, HALF)
    forcing = jnp.repeat(drive_freq, cols // freqs)[None, :]
    gap = natural * natural - forcing * forcing
    damp = 2.0 * loss * natural * forcing
    size = gap * gap + damp * damp
    sign = jnp.where(jnp.arange(cols) % 2 == 0, 1.0, -1.0).astype(F32)[None, :]
    direct = gap / size
    cross = sign * (damp / size)

    spot = jnp.arange(cols)
    block, inside = spot // rows, spot % rows
    block = mode_index(z_at + block // XLO, x_at ^ (block % XLO))
    source = block * rows + 2 * (inside % (rows // 2)) + inside // (rows // 2)
    order = (source[:, None] == spot[None, :]).astype(BF16)

    mine, theirs = partial_loads(core_arg, shapes, load_nodal)
    got = lax.ppermute(theirs, "mesh", mesh_perm(0, 0, 1))
    chip = (mine + got.astype(F32)).astype(BF16)
    got = lax.ppermute(chip, "mesh", mesh_perm(0, 1, 0))
    pair = (chip.astype(F32) + got.astype(F32)).astype(BF16)
    ring = [pair] + [lax.ppermute(pair, "mesh", mesh_perm(dy)) for dy in range(1, Y)]

    data = element_data(chip, connectivity, shape_grads, modulus)
    data = jnp.concatenate(
        [data] + [lax.ppermute(data, "mode", mode_perm(-j)) for j in range(1, Z)], axis=1
    )
    up_perm, down_perm, side_perm = mode_perm(1), mode_perm(-1), mode_perm(0, 1)
    up = lambda v: lax.ppermute(v, "mode", up_perm)
    down = lambda v: lax.ppermute(v, "mode", down_perm)
    side = lambda v: lax.ppermute(v, "mode", side_perm)
    full = 2 * rows

    w_0 = nodes * 7 // 16
    w_1 = nodes - w_0
    c_0, c_1 = (0, w_0), (w_0, w_1)
    middle = w_0 + w_1 // 2

    resp_mine = half_response(data, ring, direct, cross)
    resp_theirs = lax.ppermute(resp_mine, "mesh", mesh_perm(0, 0, 1))
    away, keep, resp = x_first_terms(core_arg, resp_mine, resp_theirs, order, shapes, c_0, 43)
    got_0 = side(away)
    ways_1 = z_first_terms(keep, resp, shapes, c_1, 43)
    plus_1, minus_1 = up(ways_1[0]), down(ways_1[1])
    weights = all_weights(ways_1[2], data, nodes)
    rim_weights = element_weights(weights, data, nodes, 2 * bound)
    on_1 = pass_on(rim_weights, ways_1[2], ways_1[3], plus_1, minus_1)
    up_1, down_1 = up(on_1[0]), down(on_1[1])
    ways_0 = x_sum(on_1[0], keep, got_0)
    plus_0, minus_0 = up(ways_0[0]), down(ways_0[1])
    low_1 = half_sum(ways_0[2], ways_0[2], 0, ways_1[4], minus_1, up_1)
    side_low = side(low_1)
    high_1 = half_sum(low_1, low_1, 1, ways_1[4], plus_1, down_1)
    side_high = side(high_1)
    on_0 = pass_on(high_1, ways_0[2], ways_0[3], plus_0, minus_0)
    up_0, down_0 = up(on_0[0]), down(on_0[1])
    values_low, rim = gather_rows(on_0[0], lists, low_1, side_low, None, w_0, full)
    acc = multiply(rim, values_low, weights, w_0, None)
    own_0 = ring_sum(acc, ways_0[4], plus_0, minus_0, up_0, down_0)
    side_0 = side(own_0)
    values_high, rim = gather_rows(own_0, lists, high_1, side_high, rim, middle, full)
    acc = multiply(rim, values_high, weights, middle, acc)
    values_0, rim = gather_rows(acc, lists, own_0, side_0, rim, 0, full)

    count = lax.axis_size("mesh")
    before = lax.ppermute(rim[..., bound:], "mesh", [(p, p + 1) for p in range(count - 1)])
    after = lax.ppermute(rim[..., :bound], "mesh", [(p + 1, p) for p in range(count - 1)])
    acc = multiply(rim, values_0, weights, 0, acc)
    spectra = element_spectra(before, after, rim_weights, acc, data[32:40])
    back = [spectra[0]] + [lax.ppermute(spectra[j], "mode", mode_perm(j)) for j in range(1, Z)]
    return collect(z_at.astype(jnp.int32).reshape(1), back)


def solution(mesh):
    in_specs = (
        P("mode", None, "mesh"),
        P(None, "mesh", None),
        P("mode"),
        P("mode"),
        P(),
        P(None, "mesh"),
        P(None, ("mesh", "mode")),
        P(None, None, ("mesh", "mode")),
        P(("mesh", "mode")),
    )
    out_specs = P(None, None, ("mesh", "mode"))
    return jax.shard_map(local, mesh=mesh, in_specs=in_specs, out_specs=out_specs, check_vma=False)
```

```python
import functools

import jax
import jax.numpy as jnp
from jax import lax
from jax.experimental import pallas as pl
from jax.experimental.pallas import tpu as pltpu
from jax.sharding import PartitionSpec as P

POISSON = 0.3
F32 = jnp.float32
BF16 = jnp.bfloat16
MIB = 1024 * 1024
Z, XLO = 4, 2
Y, XHI, CORE = 4, 2, 2
HALF = 256
ANY = pl.BlockSpec(memory_space=pl.ANY)
VMEM = pl.BlockSpec(memory_space=pltpu.VMEM)
HBM = pl.BlockSpec(memory_space=pltpu.HBM)
SMEM = pl.BlockSpec(memory_space=pltpu.SMEM)


def params(mib):
    return pltpu.CompilerParams(vmem_limit_bytes=mib * MIB)


def cost(flops=1, moved=1):
    return pl.CostEstimate(flops=flops, bytes_accessed=moved, transcendentals=0)


def shaped(shape, kind):
    return jax.ShapeDtypeStruct(shape, kind)


def mode_index(z, x):
    return (z % Z) * XLO + x


def mesh_index(y, h, c):
    return ((y % Y) * XHI + h) * CORE + c


def mode_perm(dz, flip=0):
    return [(mode_index(z, x), mode_index(z + dz, x ^ flip)) for z in range(Z) for x in range(XLO)]


def mesh_perm(dy, flip_h=0, flip_c=0):
    return [
        (mesh_index(y, h, c), mesh_index(y + dy, h ^ flip_h, c ^ flip_c))
        for y in range(Y)
        for h in range(XHI)
        for c in range(CORE)
    ]


def loads_kernel(cuts, core_ref, shapes_ref, load_ref, mine_ref, theirs_ref, shapes, load, acc, shape_sems, load_sems):
    modes = shapes.shape[1]

    def copies(i):
        c, at, width = cuts[i]
        cut = pl.ds(at, width)
        return (
            pltpu.make_async_copy(shapes_ref.at[c, :, cut], shapes.at[c, :, cut], shape_sems.at[i]),
            pltpu.make_async_copy(load_ref.at[c, cut, :], load.at[c, cut, :], load_sems.at[i]),
        )

    for i in range(len(cuts)):
        for copy in copies(i):
            copy.start()
    acc[modes:, :] = jnp.zeros((acc.shape[0] - modes, acc.shape[1]), F32)
    for i, (c, at, width) in enumerate(cuts):
        for copy in copies(i):
            copy.wait()
        cut = pl.ds(at, width)
        term = jnp.dot(shapes[c, :, cut], load[c, cut, :], preferred_element_type=F32)
        acc[:modes, :] = term if i == 0 else acc[:modes, :] + term
    core = core_ref[0]
    mine_ref[...] = acc[pl.ds(core * HALF, HALF), :]
    theirs_ref[...] = acc[pl.ds((1 - core) * HALF, HALF), :].astype(BF16)


def partial_loads(core, shapes, load):
    comps, modes, nodes = shapes.shape
    cols = load.shape[2]
    block = 1024
    cuts = [(c, at, block) for c in range(comps) for at in range(0, nodes, block)]
    vmem = pl.BlockSpec(memory_space=pltpu.VMEM)
    return pl.pallas_call(
        functools.partial(loads_kernel, cuts),
        out_shape=(shaped((HALF, cols), F32), shaped((HALF, cols), BF16)),
        in_specs=[SMEM, HBM, HBM],
        out_specs=(vmem, vmem),
        scratch_shapes=[
            pltpu.VMEM(shapes.shape, BF16),
            pltpu.VMEM(load.shape, BF16),
            pltpu.VMEM((2 * HALF, cols), F32),
            pltpu.SemaphoreType.DMA((len(cuts),)),
            pltpu.SemaphoreType.DMA((len(cuts),)),
        ],
        compiler_params=params(56),
        cost_estimate=cost(),
        name="modal_loads",
    )(core, shapes, load)


def response_kernel(mark_ref, a_ref, b_ref, c_ref, d_ref, direct_ref, cross_ref, out_ref):
    del mark_ref
    total = (
        a_ref[...].astype(F32)
        + b_ref[...].astype(F32)
        + c_ref[...].astype(F32)
        + d_ref[...].astype(F32)
    )
    cols = total.shape[1]
    even = lax.broadcasted_iota(jnp.int32, total.shape, 1) % 2 == 0
    other = jnp.where(even, pltpu.roll(total, cols - 1, 1), pltpu.roll(total, 1, 1))
    out_ref[...] = (direct_ref[...] * total + cross_ref[...] * other).astype(BF16)


def half_response(mark, parts, direct, cross):
    vmem = pl.BlockSpec(memory_space=pltpu.VMEM)
    return pl.pallas_call(
        response_kernel,
        out_shape=shaped(direct.shape, BF16),
        in_specs=[ANY] + [vmem] * 6,
        out_specs=vmem,
        compiler_params=params(8),
        cost_estimate=cost(),
        name="modal_response",
    )(mark, *parts, direct, cross)


def element_data_kernel(mark_ref, conn_ref, grads_ref, modulus_ref, out_ref):
    del mark_ref
    corners, width = conn_ref.shape
    conn = conn_ref[...].astype(F32)
    out_ref[:corners, :] = conn
    for d in range(3):
        total = jnp.zeros((corners, width), F32)
        for a in range(corners):
            total = total + jnp.where(conn == conn[a : a + 1, :], grads_ref[d, a : a + 1, :], 0.0)
        out_ref[(d + 1) * corners : (d + 2) * corners, :] = total
    out_ref[4 * corners :, :] = jnp.broadcast_to(modulus_ref[...], (corners, width))


def element_data(mark, conn, grads, modulus):
    corners, elems = conn.shape
    vmem = pl.BlockSpec(memory_space=pltpu.VMEM)
    return pl.pallas_call(
        element_data_kernel,
        out_shape=shaped((5 * corners, elems), F32),
        in_specs=[ANY, vmem, vmem, vmem],
        out_specs=vmem,
        compiler_params=params(8),
        cost_estimate=cost(),
        name="element_data",
    )(mark, conn, grads, modulus[None, :])


def split_ways(blocks, plus_ref, minus_ref, up_ref, down_ref, own_ref):
    half = up_ref.shape[-1]
    low = [b[..., :half] for b in blocks]
    high = [b[..., half:] for b in blocks]
    plus_ref[0, 0] = low[2]
    plus_ref[1, 0] = high[1]
    minus_ref[0, 0] = high[2]
    minus_ref[1, 0] = low[3]
    up_ref[0] = low[1]
    down_ref[0] = high[3]
    own_ref[0] = blocks[0]


def way_shapes(comps, rows, width):
    half = width // 2
    shapes = (
        (2, comps, rows, half),
        (2, comps, rows, half),
        (comps, rows, half),
        (comps, rows, half),
        (comps, rows, width),
    )
    specs = tuple(
        pl.BlockSpec((2, 1) + s[2:], lambda i: (0, i, 0, 0))
        if len(s) == 4
        else pl.BlockSpec((1,) + s[1:], lambda i: (i, 0, 0))
        for s in shapes
    )
    return tuple(shaped(s, BF16) for s in shapes), specs


def fetch_shapes(first, shapes_ref, held, sems):
    step = pl.program_id(0)
    cut = pl.ds(first, held.shape[2])

    @pl.when(step == 0)
    def _():
        for c in range(held.shape[0]):
            pltpu.make_async_copy(shapes_ref.at[c, :, cut], held.at[c], sems.at[c]).start()

    pltpu.make_async_copy(shapes_ref.at[step, :, cut], held.at[step], sems.at[step]).wait()
    return held[step]


def fetch_scratch(shapes, width):
    comps, modes, _ = shapes.shape
    return [pltpu.VMEM((comps, modes, width), BF16), pltpu.SemaphoreType.DMA((comps,))]


def z_first_kernel(first, mark_ref, resp_ref, shapes_ref, *refs):
    del mark_ref
    out_refs, (held, sems) = refs[:5], refs[5:]
    part = fetch_shapes(first, shapes_ref, held, sems)
    value = jnp.dot(resp_ref[...], part, preferred_element_type=F32).astype(BF16)
    rows = value.shape[0] // Z
    split_ways([value[j * rows : (j + 1) * rows, :] for j in range(Z)], *out_refs)


def z_first_terms(mark, resp, shapes, chunk, mib):
    first, width = chunk
    comps, modes, _ = shapes.shape
    cols = resp.shape[0]
    out_shape, out_specs = way_shapes(comps, cols // Z, width)
    return pl.pallas_call(
        functools.partial(z_first_kernel, first),
        out_shape=out_shape,
        grid=(comps,),
        in_specs=[ANY, pl.BlockSpec((cols, modes), lambda i: (0, 0)), HBM],
        out_specs=out_specs,
        scratch_shapes=fetch_scratch(shapes, width),
        compiler_params=params(mib),
        cost_estimate=cost(),
        name="z_first_terms",
    )(mark, resp, shapes)


def x_first_kernel(
    first, core_ref, mine_ref, theirs_ref, order_ref, shapes_ref, away_ref, keep_ref, turned_ref, resp, held, sems
):
    modes = shapes_ref.shape[1]
    part = fetch_shapes(first, shapes_ref, held, sems)

    @pl.when(pl.program_id(0) == 0)
    def _():
        core = core_ref[0]
        resp[pl.ds(core * HALF, HALF), :] = mine_ref[...]
        resp[pl.ds((1 - core) * HALF, HALF), :] = theirs_ref[...]
        turned = lax.dot_general(
            order_ref[...], resp[...], (((1,), (1,)), ((), ())), preferred_element_type=F32
        )
        turned_ref[...] = turned[:, :modes].astype(BF16)

    value = jnp.dot(turned_ref[...], part, preferred_element_type=F32).astype(BF16)
    rows = value.shape[0] // (Z * XLO)
    for j in range(Z):
        keep_ref[j, 0] = value[(2 * j) * rows : (2 * j + 1) * rows, :]
        away_ref[j, 0] = value[(2 * j + 1) * rows : (2 * j + 2) * rows, :]


def x_first_terms(core, mine, theirs, order, shapes, chunk, mib):
    first, width = chunk
    comps, modes, _ = shapes.shape
    cols = mine.shape[1]
    rows = cols // (Z * XLO)
    part = pl.BlockSpec((Z, 1, rows, width), lambda i: (0, i, 0, 0))
    whole = lambda i: (0, 0)
    return pl.pallas_call(
        functools.partial(x_first_kernel, first),
        out_shape=(
            shaped((Z, comps, rows, width), BF16),
            shaped((Z, comps, rows, width), BF16),
            shaped((cols, modes), BF16),
        ),
        grid=(comps,),
        in_specs=[
            SMEM,
            pl.BlockSpec((HALF, cols), whole),
            pl.BlockSpec((HALF, cols), whole),
            pl.BlockSpec((cols, cols), whole),
            HBM,
        ],
        out_specs=(part, part, pl.BlockSpec((cols, modes), whole)),
        scratch_shapes=[pltpu.VMEM((2 * HALF, cols), BF16)] + fetch_scratch(shapes, width),
        compiler_params=params(mib),
        cost_estimate=cost(),
        name="x_first_terms",
    )(core, mine, theirs, order, shapes)


def x_sum_kernel(mark_ref, keep_ref, got_ref, *out_refs):
    del mark_ref
    blocks = [(keep_ref[j, 0].astype(F32) + got_ref[j, 0].astype(F32)).astype(BF16) for j in range(Z)]
    split_ways(blocks, *out_refs)


def x_sum(mark, keep, got):
    _, comps, rows, width = keep.shape
    out_shape, out_specs = way_shapes(comps, rows, width)
    part = pl.BlockSpec((Z, 1, rows, width), lambda i: (0, i, 0, 0))
    return pl.pallas_call(
        x_sum_kernel,
        out_shape=out_shape,
        grid=(comps,),
        in_specs=[ANY, part, part],
        out_specs=out_specs,
        compiler_params=params(8),
        cost_estimate=cost(),
        name="x_sum",
    )(mark, keep, got)


def pass_on_kernel(mark_ref, up_ref, down_ref, plus_ref, minus_ref, up_out, down_out):
    del mark_ref
    up_out[...] = (up_ref[...].astype(F32) + plus_ref[0].astype(F32)).astype(BF16)
    down_out[...] = (down_ref[...].astype(F32) + minus_ref[0].astype(F32)).astype(BF16)


def pass_on(mark, up, down, plus, minus):
    comps, rows, half = up.shape
    one = pl.BlockSpec((1, rows, half), lambda i: (i, 0, 0))
    first = pl.BlockSpec((1, 1, rows, half), lambda i: (0, i, 0, 0))
    return pl.pallas_call(
        pass_on_kernel,
        out_shape=(shaped(up.shape, BF16), shaped(up.shape, BF16)),
        grid=(comps,),
        in_specs=[ANY, one, one, first, first],
        out_specs=(one, one),
        compiler_params=params(8),
        cost_estimate=cost(),
        name="pass_on",
    )(mark, up, down, plus, minus)


def ring_sum_kernel(mark_ref, own_ref, plus_ref, minus_ref, up_ref, down_ref, out_ref):
    del mark_ref
    half = up_ref.shape[2]
    low = own_ref[0, :, :half].astype(F32) + minus_ref[0, 0].astype(F32) + up_ref[0].astype(F32)
    high = own_ref[0, :, half:].astype(F32) + plus_ref[0, 0].astype(F32) + down_ref[0].astype(F32)
    out_ref[0, :, :half] = low.astype(BF16)
    out_ref[0, :, half:] = high.astype(BF16)


def ring_sum(mark, own, plus, minus, up, down):
    comps, rows, width = own.shape
    one = lambda n: pl.BlockSpec((1, rows, n), lambda i: (i, 0, 0))
    second = pl.BlockSpec((1, 1, rows, width // 2), lambda i: (1, i, 0, 0))
    return pl.pallas_call(
        ring_sum_kernel,
        out_shape=shaped(own.shape, BF16),
        grid=(comps,),
        in_specs=[ANY, one(width), second, second, one(width // 2), one(width // 2)],
        out_specs=one(width),
        compiler_params=params(8),
        cost_estimate=cost(),
        name="ring_sum",
    )(mark, own, plus, minus, up, down)


def half_sum_kernel(mark_ref, after_ref, own_ref, direct_ref, passed_ref, out_ref):
    del mark_ref, after_ref
    total = own_ref[...].astype(F32) + direct_ref[0].astype(F32) + passed_ref[...].astype(F32)
    out_ref[...] = total.astype(BF16)


def half_sum(mark, after, side, own, direct, passed):
    comps, rows, half = passed.shape
    one = pl.BlockSpec((1, rows, half), lambda i: (i, 0, 0))
    return pl.pallas_call(
        half_sum_kernel,
        out_shape=shaped(passed.shape, BF16),
        grid=(comps,),
        in_specs=[
            ANY,
            ANY,
            pl.BlockSpec((1, rows, half), lambda i: (i, 0, side)),
            pl.BlockSpec((1, 1, rows, half), lambda i: (1, i, 0, 0)),
            one,
        ],
        out_specs=one,
        compiler_params=params(8),
        cost_estimate=cost(),
        name="half_sum",
    )(mark, after, own, direct, passed)


def gather_rows_kernel(first, mark_ref, lists_ref, own_ref, got_ref, *refs):
    del mark_ref
    rim_in_ref, out_ref, rim_ref = refs if len(refs) == 3 else (None,) + refs
    rows = own_ref.shape[1]
    width = own_ref.shape[2]
    if rows == out_ref.shape[1]:
        half = rows // 2
        own = own_ref[0].astype(F32)
        got = got_ref[0].astype(F32)
        out_ref[0, :half, :] = (own[:half] + got[half:]).astype(BF16)
        out_ref[0, half:, :] = (own[half:] + got[:half]).astype(BF16)
    else:
        out_ref[0, :rows, :] = own_ref[0]
        out_ref[0, rows:, :] = got_ref[0]
    node = lax.broadcasted_iota(jnp.int32, (width, lists_ref.shape[1]), 0)
    pick = jnp.where(node == lists_ref[...] - first, 1.0, 0.0).astype(BF16)
    rim = jnp.dot(out_ref[0], pick, preferred_element_type=F32)
    if rim_in_ref is not None:
        rim = rim + rim_in_ref[0].astype(F32)
    rim_ref[0] = rim.astype(BF16)


def gather_rows(mark, lists, own, got, rim, first, full):
    comps, rows, width = own.shape
    count = lists.shape[1]
    one = lambda r, n: pl.BlockSpec((1, r, n), lambda i: (i, 0, 0))
    specs = [ANY, pl.BlockSpec((1, count), lambda i: (0, 0)), one(rows, width), one(rows, width)]
    args = [mark, lists, own, got]
    if rim is not None:
        specs.append(one(full, count))
        args.append(rim)
    return pl.pallas_call(
        functools.partial(gather_rows_kernel, first),
        out_shape=(shaped((comps, full, width), BF16), shaped((comps, full, count), BF16)),
        grid=(comps,),
        in_specs=specs,
        out_specs=(one(full, width), one(full, count)),
        compiler_params=params(8),
        cost_estimate=cost(),
        name="gather_rows",
    )(*args)


NODE_BLOCK = 256
WIDE = 256
ROWS = 16
LANES = 128


def build_tiles(first, nodes, conn, grads, store):
    corners = conn.shape[0]
    base = lax.broadcasted_iota(jnp.int32, (ROWS, LANES), 0).astype(F32).astype(BF16)
    zero = jnp.zeros((ROWS, LANES), BF16)
    grads = grads.astype(BF16)
    grad = [jnp.broadcast_to(grads[i : i + 1, :], (ROWS, LANES)) for i in range(3 * corners)]
    for at in range(0, nodes, NODE_BLOCK):
        keys = (conn - (first + at)).astype(BF16)
        key = [jnp.broadcast_to(keys[a : a + 1, :], (ROWS, LANES)) for a in range(corners)]
        for row in range(0, NODE_BLOCK, ROWS):
            node = base + BF16(row)
            sums = [zero] * 3
            for a in range(corners):
                hit = node == key[a]
                for d in range(3):
                    sums[d] = jnp.where(hit, grad[d * corners + a], sums[d])
            for d in range(3):
                store(d, at + row, sums[d])


def weights_kernel(first, mark_ref, conn_ref, grads_ref, out_ref):
    del mark_ref

    def piece(step, carry):
        cut = pl.ds(pl.multiple_of(step * LANES, LANES), LANES)

        def store(d, row, value):
            out_ref[d, pl.ds(row, ROWS), cut] = value

        build_tiles(first, out_ref.shape[1], conn_ref[:, cut], grads_ref[:, cut], store)
        return carry

    lax.fori_loop(0, conn_ref.shape[1] // LANES, piece, 0)


def all_weights_kernel(mark_ref, conn_ref, grads_ref, out_ref, made, sems):
    del mark_ref
    blocks, _, nodes, _ = out_ref.shape
    slots, _, count, wide = made.shape
    parts = nodes // count

    def copies(block, part, slot):
        rows = pl.ds(part * count, count)
        return [
            pltpu.make_async_copy(made.at[slot, d], out_ref.at[block, d, rows, :], sems.at[slot, d])
            for d in range(3)
        ]

    def block_of_elements(block, carry):
        for part in range(parts):
            slot = part % slots

            @pl.when(block > 0)
            def _():
                for copy in copies(block - 1, part, slot):
                    copy.wait()

            for lane in range(0, wide, LANES):
                cut = pl.ds(pl.multiple_of(block * wide + lane, LANES), LANES)

                def store(d, row, value):
                    made[slot, d, pl.ds(row, ROWS), pl.ds(lane, LANES)] = value

                build_tiles(float(part * count), count, conn_ref[:, cut], grads_ref[:, cut], store)
            for copy in copies(block, part, slot):
                copy.start()
        return carry

    lax.fori_loop(0, blocks, block_of_elements, 0)
    for part in range(parts):
        for copy in copies(blocks - 1, part, part):
            copy.wait()


def all_weights(mark, data, nodes):
    elems = data.shape[1]
    slots = 4
    count = nodes // slots
    return pl.pallas_call(
        all_weights_kernel,
        out_shape=shaped((elems // WIDE, 3, nodes, WIDE), BF16),
        in_specs=[ANY, VMEM, VMEM],
        out_specs=ANY,
        scratch_shapes=[pltpu.VMEM((slots, 3, count, WIDE), BF16), pltpu.SemaphoreType.DMA((slots, 3))],
        compiler_params=params(16),
        cost_estimate=cost(),
        name="all_weights",
    )(mark, data[:8], data[8:32])


def element_weights(mark, data, first, count):
    elems = data.shape[1]
    return pl.pallas_call(
        functools.partial(weights_kernel, float(first)),
        out_shape=shaped((3, count, elems), BF16),
        in_specs=[ANY, VMEM, VMEM],
        out_specs=VMEM,
        compiler_params=params(8),
        cost_estimate=cost(),
        name="element_weights",
    )(mark, data[:8], data[8:32])


SLOTS = 4


def multiply_kernel(first, mark_ref, values_ref, weights_ref, *refs):
    del mark_ref
    acc_ref, out_ref, held, sems = refs if len(refs) == 4 else (None,) + refs
    comps, rows, nodes = values_ref.shape
    values = values_ref[...].reshape(comps * rows, nodes)
    blocks = weights_ref.shape[0]

    def copy(block, slot, d):
        return pltpu.make_async_copy(
            weights_ref.at[block, d, pl.ds(first, nodes), :], held.at[slot, d], sems.at[slot, d]
        )

    for slot in range(SLOTS):
        for d in range(3):
            copy(slot, slot, d).start()

    def turn(block, carry):
        slot = block % SLOTS
        cut = pl.ds(pl.multiple_of(block * WIDE, WIDE), WIDE)
        for d in range(3):
            copy(block, slot, d).wait()
            term = jnp.dot(values, held[slot, d], preferred_element_type=F32)
            out_ref[d, :, cut] = term if acc_ref is None else term + acc_ref[d, :, cut]

        @pl.when(block < blocks - SLOTS)
        def _():
            for d in range(3):
                copy(block + SLOTS, slot, d).start()

        return carry

    lax.fori_loop(0, blocks, turn, 0)


def multiply(mark, values, weights, first, acc):
    comps, rows, nodes = values.shape
    elems = weights.shape[0] * WIDE
    args = [mark, values, weights] + ([] if acc is None else [acc])
    return pl.pallas_call(
        functools.partial(multiply_kernel, first),
        out_shape=shaped((3, comps * rows, elems), F32),
        in_specs=[ANY, VMEM, ANY] + [VMEM] * (len(args) - 3),
        out_specs=VMEM,
        input_output_aliases={} if acc is None else {3: 0},
        scratch_shapes=[pltpu.VMEM((SLOTS, 3, nodes, WIDE), BF16), pltpu.SemaphoreType.DMA((SLOTS, 3))],
        compiler_params=params(24),
        cost_estimate=cost(),
        name="multiply",
    )(*args)


def spectra_kernel(before_ref, after_ref, weights_ref, acc_ref, modulus_ref, out_ref, grads):
    comps, rows, rim = before_ref.shape
    half = rows // 4
    groups, _, count = out_ref.shape
    per = count // WIDE
    before = before_ref[...].reshape(comps * rows, rim)
    after = after_ref[...].reshape(comps * rows, rim)

    def finish(group, place, lanes_at, modulus):
        lame = modulus * (POISSON / ((1.0 + POISSON) * (1.0 - 2.0 * POISSON)))
        shear = modulus * (1.0 / (2.0 * (1.0 + POISSON)))
        twice = 2.0 * shear
        lanes = pl.ds(lanes_at, LANES)

        def stress(top):
            def at(c, d):
                return grads[d, c * rows + top : c * rows + top + 8, lanes]

            volume = lame * (at(0, 0) + at(1, 1) + at(2, 2))
            return [
                volume + twice * at(0, 0),
                volume + twice * at(1, 1),
                volume + twice * at(2, 2),
                shear * (at(1, 2) + at(2, 1)),
                shear * (at(2, 0) + at(0, 2)),
                shear * (at(0, 1) + at(1, 0)),
            ]

        pairs = [(i, j, 0) for i in range(6) for j in range(i, 6)]
        pairs += [(i, j, 1) for i in range(6) for j in range(i + 1, 6)]
        totals = [None] * len(pairs)
        for top in [s * 2 * half + p for s in range(2) for p in range(0, half, 8)]:
            re = stress(top)
            im = stress(top + half)
            for n, (i, j, turned) in enumerate(pairs):
                if turned:
                    term = im[i] * re[j] - re[i] * im[j]
                else:
                    term = re[i] * re[j] + im[i] * im[j]
                totals[n] = term if totals[n] is None else totals[n] + term
        for n in range(len(pairs)):
            out_ref[group, pl.ds(n, 1), pl.ds(place, LANES)] = jnp.sum(totals[n], axis=0, keepdims=True)

    def piece(step, carry):
        cut = pl.ds(pl.multiple_of(step * WIDE, WIDE), WIDE)
        for d in range(3):
            grads[d] = (
                acc_ref[d, :, cut]
                + jnp.dot(before, weights_ref[d, :rim, cut], preferred_element_type=F32)
                + jnp.dot(after, weights_ref[d, rim:, cut], preferred_element_type=F32)
            )
        group = step // per
        start = (step % per) * WIDE
        for at in range(0, WIDE, LANES):
            here = pl.ds(pl.multiple_of(step * WIDE + at, LANES), LANES)
            finish(group, pl.multiple_of(start + at, LANES), at, modulus_ref[:1, here])
        return carry

    lax.fori_loop(0, groups * per, piece, 0)


def element_spectra(before, after, weights, acc, modulus):
    comps, rows, rim = before.shape
    elems = weights.shape[2]
    return pl.pallas_call(
        spectra_kernel,
        out_shape=shaped((Z, 36, elems // Z), F32),
        in_specs=[VMEM] * 5,
        out_specs=VMEM,
        scratch_shapes=[pltpu.VMEM((3, comps * rows, WIDE), F32)],
        compiler_params=params(8),
        cost_estimate=cost(),
        name="element_spectra",
    )(before, after, weights, acc, modulus)


def collect_kernel(place_ref, a_ref, b_ref, c_ref, d_ref, out_ref):
    for j, ref in enumerate((a_ref, b_ref, c_ref, d_ref)):
        out_ref[pl.ds((place_ref[0] + Z - j) % Z, 1)] = ref[...][None]


def collect(place, blocks):
    return pl.pallas_call(
        collect_kernel,
        out_shape=shaped((Z,) + blocks[0].shape, F32),
        in_specs=[SMEM] + [VMEM] * Z,
        out_specs=VMEM,
        compiler_params=params(8),
        cost_estimate=cost(),
        name="collect",
    )(place, *blocks)


def local(
    mode_shapes,
    load_nodal,
    mode_freq,
    damping,
    drive_freq,
    send_lists,
    connectivity,
    shape_grads,
    modulus,
):
    modes, _, nodes = mode_shapes.shape
    cols = load_nodal.shape[2]
    bound = send_lists.shape[1]
    freqs = drive_freq.shape[0]
    rows = cols // (Z * XLO)
    mode_at = lax.axis_index("mode")
    z_at, x_at = mode_at // XLO, mode_at % XLO
    core = (lax.axis_index("mesh") % CORE).astype(jnp.int32)
    core_arg = core.reshape(1)
    shapes = jnp.transpose(mode_shapes, (1, 0, 2))
    lists = send_lists.reshape(1, -1)

    pad = 2 * HALF - modes
    natural = jnp.pad(mode_freq, (0, pad), constant_values=1.0)[:, None]
    loss = jnp.pad(damping, (0, pad), constant_values=0.5)[:, None]
    natural = lax.dynamic_slice_in_dim(natural, core * HALF, HALF)
    loss = lax.dynamic_slice_in_dim(loss, core * HALF, HALF)
    forcing = jnp.repeat(drive_freq, cols // freqs)[None, :]
    gap = natural * natural - forcing * forcing
    damp = 2.0 * loss * natural * forcing
    size = gap * gap + damp * damp
    sign = jnp.where(jnp.arange(cols) % 2 == 0, 1.0, -1.0).astype(F32)[None, :]
    direct = gap / size
    cross = sign * (damp / size)

    spot = jnp.arange(cols)
    block, inside = spot // rows, spot % rows
    block = mode_index(z_at + block // XLO, x_at ^ (block % XLO))
    source = block * rows + 2 * (inside % (rows // 2)) + inside // (rows // 2)
    order = (source[:, None] == spot[None, :]).astype(BF16)

    mine, theirs = partial_loads(core_arg, shapes, load_nodal)
    got = lax.ppermute(theirs, "mesh", mesh_perm(0, 0, 1))
    chip = (mine + got.astype(F32)).astype(BF16)
    got = lax.ppermute(chip, "mesh", mesh_perm(0, 1, 0))
    pair = (chip.astype(F32) + got.astype(F32)).astype(BF16)
    ring = [pair] + [lax.ppermute(pair, "mesh", mesh_perm(dy)) for dy in range(1, Y)]

    data = element_data(chip, connectivity, shape_grads, modulus)
    data = jnp.concatenate(
        [data] + [lax.ppermute(data, "mode", mode_perm(-j)) for j in range(1, Z)], axis=1
    )
    up_perm, down_perm, side_perm = mode_perm(1), mode_perm(-1), mode_perm(0, 1)
    up = lambda v: lax.ppermute(v, "mode", up_perm)
    down = lambda v: lax.ppermute(v, "mode", down_perm)
    side = lambda v: lax.ppermute(v, "mode", side_perm)
    full = 2 * rows

    w_0 = nodes * 7 // 16
    w_1 = nodes - w_0
    c_0, c_1 = (0, w_0), (w_0, w_1)
    middle = w_0 + w_1 // 2

    resp_mine = half_response(data, ring, direct, cross)
    resp_theirs = lax.ppermute(resp_mine, "mesh", mesh_perm(0, 0, 1))
    away, keep, resp = x_first_terms(core_arg, resp_mine, resp_theirs, order, shapes, c_0, 43)
    got_0 = side(away)
    ways_1 = z_first_terms(keep, resp, shapes, c_1, 43)
    plus_1, minus_1 = up(ways_1[0]), down(ways_1[1])
    weights = all_weights(ways_1[2], data, nodes)
    rim_weights = element_weights(weights, data, nodes, 2 * bound)
    on_1 = pass_on(rim_weights, ways_1[2], ways_1[3], plus_1, minus_1)
    up_1, down_1 = up(on_1[0]), down(on_1[1])
    ways_0 = x_sum(on_1[0], keep, got_0)
    plus_0, minus_0 = up(ways_0[0]), down(ways_0[1])
    low_1 = half_sum(ways_0[2], ways_0[2], 0, ways_1[4], minus_1, up_1)
    side_low = side(low_1)
    high_1 = half_sum(low_1, low_1, 1, ways_1[4], plus_1, down_1)
    side_high = side(high_1)
    on_0 = pass_on(high_1, ways_0[2], ways_0[3], plus_0, minus_0)
    up_0, down_0 = up(on_0[0]), down(on_0[1])
    values_low, rim = gather_rows(on_0[0], lists, low_1, side_low, None, w_0, full)
    acc = multiply(rim, values_low, weights, w_0, None)
    own_0 = ring_sum(acc, ways_0[4], plus_0, minus_0, up_0, down_0)
    side_0 = side(own_0)
    values_high, rim = gather_rows(own_0, lists, high_1, side_high, rim, middle, full)
    acc = multiply(rim, values_high, weights, middle, acc)
    values_0, rim = gather_rows(acc, lists, own_0, side_0, rim, 0, full)

    count = lax.axis_size("mesh")
    before = lax.ppermute(rim[..., bound:], "mesh", [(p, p + 1) for p in range(count - 1)])
    after = lax.ppermute(rim[..., :bound], "mesh", [(p + 1, p) for p in range(count - 1)])
    acc = multiply(rim, values_0, weights, 0, acc)
    spectra = element_spectra(before, after, rim_weights, acc, data[32:40])
    back = [spectra[0]] + [lax.ppermute(spectra[j], "mode", mode_perm(j)) for j in range(1, Z)]
    return collect(z_at.astype(jnp.int32).reshape(1), back)


def solution(mesh):
    in_specs = (
        P("mode", None, "mesh"),
        P(None, "mesh", None),
        P("mode"),
        P("mode"),
        P(),
        P(None, "mesh"),
        P(None, ("mesh", "mode")),
        P(None, None, ("mesh", "mode")),
        P(("mesh", "mode")),
    )
    out_specs = P(None, None, ("mesh", "mode"))
    return jax.shard_map(local, mesh=mesh, in_specs=in_specs, out_specs=out_specs, check_vma=False)
```

```python
import functools

import jax
import jax.numpy as jnp
from jax import lax
from jax.experimental import pallas as pl
from jax.experimental.pallas import tpu as pltpu
from jax.sharding import PartitionSpec as P

POISSON = 0.3
F32 = jnp.float32
BF16 = jnp.bfloat16
MIB = 1024 * 1024
Z, XLO = 4, 2
Y, XHI, CORE = 4, 2, 2
HALF = 256
ANY = pl.BlockSpec(memory_space=pl.ANY)
VMEM = pl.BlockSpec(memory_space=pltpu.VMEM)
HBM = pl.BlockSpec(memory_space=pltpu.HBM)
SMEM = pl.BlockSpec(memory_space=pltpu.SMEM)


def params(mib):
    return pltpu.CompilerParams(vmem_limit_bytes=mib * MIB)


def cost(flops=1, moved=1):
    return pl.CostEstimate(flops=flops, bytes_accessed=moved, transcendentals=0)


def shaped(shape, kind):
    return jax.ShapeDtypeStruct(shape, kind)


def mode_index(z, x):
    return (z % Z) * XLO + x


def mesh_index(y, h, c):
    return ((y % Y) * XHI + h) * CORE + c


def mode_perm(dz, flip=0):
    return [(mode_index(z, x), mode_index(z + dz, x ^ flip)) for z in range(Z) for x in range(XLO)]


def mesh_perm(dy, flip_h=0, flip_c=0):
    return [
        (mesh_index(y, h, c), mesh_index(y + dy, h ^ flip_h, c ^ flip_c))
        for y in range(Y)
        for h in range(XHI)
        for c in range(CORE)
    ]


def loads_kernel(cuts, core_ref, shapes_ref, load_ref, mine_ref, theirs_ref, shapes, load, acc, shape_sems, load_sems):
    modes = shapes.shape[1]

    def copies(i):
        c, at, width = cuts[i]
        cut = pl.ds(at, width)
        return (
            pltpu.make_async_copy(shapes_ref.at[c, :, cut], shapes.at[c, :, cut], shape_sems.at[i]),
            pltpu.make_async_copy(load_ref.at[c, cut, :], load.at[c, cut, :], load_sems.at[i]),
        )

    for i in range(len(cuts)):
        for copy in copies(i):
            copy.start()
    acc[modes:, :] = jnp.zeros((acc.shape[0] - modes, acc.shape[1]), F32)
    for i, (c, at, width) in enumerate(cuts):
        for copy in copies(i):
            copy.wait()
        cut = pl.ds(at, width)
        term = jnp.dot(shapes[c, :, cut], load[c, cut, :], preferred_element_type=F32)
        acc[:modes, :] = term if i == 0 else acc[:modes, :] + term
    core = core_ref[0]
    mine_ref[...] = acc[pl.ds(core * HALF, HALF), :]
    theirs_ref[...] = acc[pl.ds((1 - core) * HALF, HALF), :].astype(BF16)


def partial_loads(core, shapes, load):
    comps, modes, nodes = shapes.shape
    cols = load.shape[2]
    block = 1024
    cuts = [(c, at, block) for c in range(comps) for at in range(0, nodes, block)]
    vmem = pl.BlockSpec(memory_space=pltpu.VMEM)
    return pl.pallas_call(
        functools.partial(loads_kernel, cuts),
        out_shape=(shaped((HALF, cols), F32), shaped((HALF, cols), BF16)),
        in_specs=[SMEM, HBM, HBM],
        out_specs=(vmem, vmem),
        scratch_shapes=[
            pltpu.VMEM(shapes.shape, BF16),
            pltpu.VMEM(load.shape, BF16),
            pltpu.VMEM((2 * HALF, cols), F32),
            pltpu.SemaphoreType.DMA((len(cuts),)),
            pltpu.SemaphoreType.DMA((len(cuts),)),
        ],
        compiler_params=params(56),
        cost_estimate=cost(),
        name="modal_loads",
    )(core, shapes, load)


def response_kernel(mark_ref, a_ref, b_ref, c_ref, d_ref, direct_ref, cross_ref, out_ref):
    del mark_ref
    total = (
        a_ref[...].astype(F32)
        + b_ref[...].astype(F32)
        + c_ref[...].astype(F32)
        + d_ref[...].astype(F32)
    )
    cols = total.shape[1]
    even = lax.broadcasted_iota(jnp.int32, total.shape, 1) % 2 == 0
    other = jnp.where(even, pltpu.roll(total, cols - 1, 1), pltpu.roll(total, 1, 1))
    out_ref[...] = (direct_ref[...] * total + cross_ref[...] * other).astype(BF16)


def half_response(mark, parts, direct, cross):
    vmem = pl.BlockSpec(memory_space=pltpu.VMEM)
    return pl.pallas_call(
        response_kernel,
        out_shape=shaped(direct.shape, BF16),
        in_specs=[ANY] + [vmem] * 6,
        out_specs=vmem,
        compiler_params=params(8),
        cost_estimate=cost(),
        name="modal_response",
    )(mark, *parts, direct, cross)


def element_data_kernel(mark_ref, conn_ref, grads_ref, modulus_ref, out_ref):
    del mark_ref
    corners, width = conn_ref.shape
    conn = conn_ref[...].astype(F32)
    out_ref[:corners, :] = conn
    for d in range(3):
        total = jnp.zeros((corners, width), F32)
        for a in range(corners):
            total = total + jnp.where(conn == conn[a : a + 1, :], grads_ref[d, a : a + 1, :], 0.0)
        out_ref[(d + 1) * corners : (d + 2) * corners, :] = total
    out_ref[4 * corners :, :] = jnp.broadcast_to(modulus_ref[...], (corners, width))


def element_data(mark, conn, grads, modulus):
    corners, elems = conn.shape
    vmem = pl.BlockSpec(memory_space=pltpu.VMEM)
    return pl.pallas_call(
        element_data_kernel,
        out_shape=shaped((5 * corners, elems), F32),
        in_specs=[ANY, vmem, vmem, vmem],
        out_specs=vmem,
        compiler_params=params(8),
        cost_estimate=cost(),
        name="element_data",
    )(mark, conn, grads, modulus[None, :])


def split_ways(blocks, plus_ref, minus_ref, up_ref, down_ref, own_ref):
    half = up_ref.shape[-1]
    low = [b[..., :half] for b in blocks]
    high = [b[..., half:] for b in blocks]
    plus_ref[0, 0] = low[2]
    plus_ref[1, 0] = high[1]
    minus_ref[0, 0] = high[2]
    minus_ref[1, 0] = low[3]
    up_ref[0] = low[1]
    down_ref[0] = high[3]
    own_ref[0] = blocks[0]


def way_shapes(comps, rows, width):
    half = width // 2
    shapes = (
        (2, comps, rows, half),
        (2, comps, rows, half),
        (comps, rows, half),
        (comps, rows, half),
        (comps, rows, width),
    )
    specs = tuple(
        pl.BlockSpec((2, 1) + s[2:], lambda i: (0, i, 0, 0))
        if len(s) == 4
        else pl.BlockSpec((1,) + s[1:], lambda i: (i, 0, 0))
        for s in shapes
    )
    return tuple(shaped(s, BF16) for s in shapes), specs


def fetch_shapes(first, shapes_ref, held, sems):
    step = pl.program_id(0)
    cut = pl.ds(first, held.shape[2])

    @pl.when(step == 0)
    def _():
        for c in range(held.shape[0]):
            pltpu.make_async_copy(shapes_ref.at[c, :, cut], held.at[c], sems.at[c]).start()

    pltpu.make_async_copy(shapes_ref.at[step, :, cut], held.at[step], sems.at[step]).wait()
    return held[step]


def fetch_scratch(shapes, width):
    comps, modes, _ = shapes.shape
    return [pltpu.VMEM((comps, modes, width), BF16), pltpu.SemaphoreType.DMA((comps,))]


def z_first_kernel(first, mark_ref, resp_ref, shapes_ref, *refs):
    del mark_ref
    out_refs, (held, sems) = refs[:5], refs[5:]
    part = fetch_shapes(first, shapes_ref, held, sems)
    value = jnp.dot(resp_ref[...], part, preferred_element_type=F32).astype(BF16)
    rows = value.shape[0] // Z
    split_ways([value[j * rows : (j + 1) * rows, :] for j in range(Z)], *out_refs)


def z_first_terms(mark, resp, shapes, chunk, mib):
    first, width = chunk
    comps, modes, _ = shapes.shape
    cols = resp.shape[0]
    out_shape, out_specs = way_shapes(comps, cols // Z, width)
    return pl.pallas_call(
        functools.partial(z_first_kernel, first),
        out_shape=out_shape,
        grid=(comps,),
        in_specs=[ANY, pl.BlockSpec((cols, modes), lambda i: (0, 0)), HBM],
        out_specs=out_specs,
        scratch_shapes=fetch_scratch(shapes, width),
        compiler_params=params(mib),
        cost_estimate=cost(),
        name="z_first_terms",
    )(mark, resp, shapes)


def x_first_kernel(
    first, core_ref, mine_ref, theirs_ref, order_ref, shapes_ref, away_ref, keep_ref, turned_ref, resp, held, sems
):
    modes = shapes_ref.shape[1]
    part = fetch_shapes(first, shapes_ref, held, sems)

    @pl.when(pl.program_id(0) == 0)
    def _():
        core = core_ref[0]
        resp[pl.ds(core * HALF, HALF), :] = mine_ref[...]
        resp[pl.ds((1 - core) * HALF, HALF), :] = theirs_ref[...]
        turned = lax.dot_general(
            order_ref[...], resp[...], (((1,), (1,)), ((), ())), preferred_element_type=F32
        )
        turned_ref[...] = turned[:, :modes].astype(BF16)

    value = jnp.dot(turned_ref[...], part, preferred_element_type=F32).astype(BF16)
    rows = value.shape[0] // (Z * XLO)
    for j in range(Z):
        keep_ref[j, 0] = value[(2 * j) * rows : (2 * j + 1) * rows, :]
        away_ref[j, 0] = value[(2 * j + 1) * rows : (2 * j + 2) * rows, :]


def x_first_terms(core, mine, theirs, order, shapes, chunk, mib):
    first, width = chunk
    comps, modes, _ = shapes.shape
    cols = mine.shape[1]
    rows = cols // (Z * XLO)
    part = pl.BlockSpec((Z, 1, rows, width), lambda i: (0, i, 0, 0))
    whole = lambda i: (0, 0)
    return pl.pallas_call(
        functools.partial(x_first_kernel, first),
        out_shape=(
            shaped((Z, comps, rows, width), BF16),
            shaped((Z, comps, rows, width), BF16),
            shaped((cols, modes), BF16),
        ),
        grid=(comps,),
        in_specs=[
            SMEM,
            pl.BlockSpec((HALF, cols), whole),
            pl.BlockSpec((HALF, cols), whole),
            pl.BlockSpec((cols, cols), whole),
            HBM,
        ],
        out_specs=(part, part, pl.BlockSpec((cols, modes), whole)),
        scratch_shapes=[pltpu.VMEM((2 * HALF, cols), BF16)] + fetch_scratch(shapes, width),
        compiler_params=params(mib),
        cost_estimate=cost(),
        name="x_first_terms",
    )(core, mine, theirs, order, shapes)


def x_sum_kernel(mark_ref, keep_ref, got_ref, *out_refs):
    del mark_ref
    blocks = [(keep_ref[j, 0].astype(F32) + got_ref[j, 0].astype(F32)).astype(BF16) for j in range(Z)]
    split_ways(blocks, *out_refs)


def x_sum(mark, keep, got):
    _, comps, rows, width = keep.shape
    out_shape, out_specs = way_shapes(comps, rows, width)
    part = pl.BlockSpec((Z, 1, rows, width), lambda i: (0, i, 0, 0))
    return pl.pallas_call(
        x_sum_kernel,
        out_shape=out_shape,
        grid=(comps,),
        in_specs=[ANY, part, part],
        out_specs=out_specs,
        compiler_params=params(8),
        cost_estimate=cost(),
        name="x_sum",
    )(mark, keep, got)


def pass_on_kernel(mark_ref, up_ref, down_ref, plus_ref, minus_ref, up_out, down_out):
    del mark_ref
    up_out[...] = (up_ref[...].astype(F32) + plus_ref[0].astype(F32)).astype(BF16)
    down_out[...] = (down_ref[...].astype(F32) + minus_ref[0].astype(F32)).astype(BF16)


def pass_on(mark, up, down, plus, minus):
    comps, rows, half = up.shape
    one = pl.BlockSpec((1, rows, half), lambda i: (i, 0, 0))
    first = pl.BlockSpec((1, 1, rows, half), lambda i: (0, i, 0, 0))
    return pl.pallas_call(
        pass_on_kernel,
        out_shape=(shaped(up.shape, BF16), shaped(up.shape, BF16)),
        grid=(comps,),
        in_specs=[ANY, one, one, first, first],
        out_specs=(one, one),
        compiler_params=params(8),
        cost_estimate=cost(),
        name="pass_on",
    )(mark, up, down, plus, minus)


def ring_sum_kernel(mark_ref, own_ref, plus_ref, minus_ref, up_ref, down_ref, out_ref):
    del mark_ref
    half = up_ref.shape[2]
    low = own_ref[0, :, :half].astype(F32) + minus_ref[0, 0].astype(F32) + up_ref[0].astype(F32)
    high = own_ref[0, :, half:].astype(F32) + plus_ref[0, 0].astype(F32) + down_ref[0].astype(F32)
    out_ref[0, :, :half] = low.astype(BF16)
    out_ref[0, :, half:] = high.astype(BF16)


def ring_sum(mark, own, plus, minus, up, down):
    comps, rows, width = own.shape
    one = lambda n: pl.BlockSpec((1, rows, n), lambda i: (i, 0, 0))
    second = pl.BlockSpec((1, 1, rows, width // 2), lambda i: (1, i, 0, 0))
    return pl.pallas_call(
        ring_sum_kernel,
        out_shape=shaped(own.shape, BF16),
        grid=(comps,),
        in_specs=[ANY, one(width), second, second, one(width // 2), one(width // 2)],
        out_specs=one(width),
        compiler_params=params(8),
        cost_estimate=cost(),
        name="ring_sum",
    )(mark, own, plus, minus, up, down)


def half_sum_kernel(mark_ref, after_ref, own_ref, direct_ref, passed_ref, out_ref):
    del mark_ref, after_ref
    total = own_ref[...].astype(F32) + direct_ref[0].astype(F32) + passed_ref[...].astype(F32)
    out_ref[...] = total.astype(BF16)


def half_sum(mark, after, side, own, direct, passed):
    comps, rows, half = passed.shape
    one = pl.BlockSpec((1, rows, half), lambda i: (i, 0, 0))
    return pl.pallas_call(
        half_sum_kernel,
        out_shape=shaped(passed.shape, BF16),
        grid=(comps,),
        in_specs=[
            ANY,
            ANY,
            pl.BlockSpec((1, rows, half), lambda i: (i, 0, side)),
            pl.BlockSpec((1, 1, rows, half), lambda i: (1, i, 0, 0)),
            one,
        ],
        out_specs=one,
        compiler_params=params(8),
        cost_estimate=cost(),
        name="half_sum",
    )(mark, after, own, direct, passed)


def gather_rows_kernel(first, mark_ref, lists_ref, own_ref, got_ref, *refs):
    del mark_ref
    rim_in_ref, out_ref, rim_ref = refs if len(refs) == 3 else (None,) + refs
    rows = own_ref.shape[1]
    width = own_ref.shape[2]
    if rows == out_ref.shape[1]:
        half = rows // 2
        own = own_ref[0].astype(F32)
        got = got_ref[0].astype(F32)
        out_ref[0, :half, :] = (own[:half] + got[half:]).astype(BF16)
        out_ref[0, half:, :] = (own[half:] + got[:half]).astype(BF16)
    else:
        out_ref[0, :rows, :] = own_ref[0]
        out_ref[0, rows:, :] = got_ref[0]
    node = lax.broadcasted_iota(jnp.int32, (width, lists_ref.shape[1]), 0)
    pick = jnp.where(node == lists_ref[...] - first, 1.0, 0.0).astype(BF16)
    rim = jnp.dot(out_ref[0], pick, preferred_element_type=F32)
    if rim_in_ref is not None:
        rim = rim + rim_in_ref[0].astype(F32)
    rim_ref[0] = rim.astype(BF16)


def gather_rows(mark, lists, own, got, rim, first, full):
    comps, rows, width = own.shape
    count = lists.shape[1]
    one = lambda r, n: pl.BlockSpec((1, r, n), lambda i: (i, 0, 0))
    specs = [ANY, pl.BlockSpec((1, count), lambda i: (0, 0)), one(rows, width), one(rows, width)]
    args = [mark, lists, own, got]
    if rim is not None:
        specs.append(one(full, count))
        args.append(rim)
    return pl.pallas_call(
        functools.partial(gather_rows_kernel, first),
        out_shape=(shaped((comps, full, width), BF16), shaped((comps, full, count), BF16)),
        grid=(comps,),
        in_specs=specs,
        out_specs=(one(full, width), one(full, count)),
        compiler_params=params(8),
        cost_estimate=cost(),
        name="gather_rows",
    )(*args)


NODE_BLOCK = 256
WIDE = 256
ROWS = 16
LANES = 128


def build_tiles(first, nodes, conn, grads, store):
    corners = conn.shape[0]
    base = lax.broadcasted_iota(jnp.int32, (ROWS, LANES), 0).astype(F32).astype(BF16)
    zero = jnp.zeros((ROWS, LANES), BF16)
    grads = grads.astype(BF16)
    grad = [jnp.broadcast_to(grads[i : i + 1, :], (ROWS, LANES)) for i in range(3 * corners)]
    for at in range(0, nodes, NODE_BLOCK):
        keys = (conn - (first + at)).astype(BF16)
        key = [jnp.broadcast_to(keys[a : a + 1, :], (ROWS, LANES)) for a in range(corners)]
        for row in range(0, min(NODE_BLOCK, nodes - at), ROWS):
            node = base + BF16(row)
            sums = [zero] * 3
            for a in range(corners):
                hit = node == key[a]
                for d in range(3):
                    sums[d] = jnp.where(hit, grad[d * corners + a], sums[d])
            for d in range(3):
                store(d, at + row, sums[d])


def weights_kernel(first, mark_ref, conn_ref, grads_ref, out_ref):
    del mark_ref

    def piece(step, carry):
        cut = pl.ds(pl.multiple_of(step * LANES, LANES), LANES)

        def store(d, row, value):
            out_ref[d, pl.ds(row, ROWS), cut] = value

        build_tiles(first, out_ref.shape[1], conn_ref[:, cut], grads_ref[:, cut], store)
        return carry

    lax.fori_loop(0, conn_ref.shape[1] // LANES, piece, 0)


def all_weights_kernel(mark_ref, conn_ref, grads_ref, out_ref, made, sems):
    del mark_ref
    blocks, _, nodes, _ = out_ref.shape
    slots, _, count, wide = made.shape
    parts = nodes // count

    def copies(block, part, slot):
        rows = pl.ds(part * count, count)
        return [
            pltpu.make_async_copy(made.at[slot, d], out_ref.at[block, d, rows, :], sems.at[slot, d])
            for d in range(3)
        ]

    def block_of_elements(block, carry):
        for part in range(parts):
            slot = part % slots

            @pl.when(block > 0)
            def _():
                for copy in copies(block - 1, part, slot):
                    copy.wait()

            for lane in range(0, wide, LANES):
                cut = pl.ds(pl.multiple_of(block * wide + lane, LANES), LANES)

                def store(d, row, value):
                    made[slot, d, pl.ds(row, ROWS), pl.ds(lane, LANES)] = value

                build_tiles(float(part * count), count, conn_ref[:, cut], grads_ref[:, cut], store)
            for copy in copies(block, part, slot):
                copy.start()
        return carry

    lax.fori_loop(0, blocks, block_of_elements, 0)
    for part in range(parts):
        for copy in copies(blocks - 1, part, part):
            copy.wait()


def all_weights(mark, data, nodes):
    elems = data.shape[1]
    slots = 4
    count = nodes // slots
    return pl.pallas_call(
        all_weights_kernel,
        out_shape=shaped((elems // WIDE, 3, nodes, WIDE), BF16),
        in_specs=[ANY, VMEM, VMEM],
        out_specs=ANY,
        scratch_shapes=[pltpu.VMEM((slots, 3, count, WIDE), BF16), pltpu.SemaphoreType.DMA((slots, 3))],
        compiler_params=params(30),
        cost_estimate=cost(),
        name="all_weights",
    )(mark, data[:8], data[8:32])


def element_weights(mark, data, first, count):
    elems = data.shape[1]
    return pl.pallas_call(
        functools.partial(weights_kernel, float(first)),
        out_shape=shaped((3, count, elems), BF16),
        in_specs=[ANY, VMEM, VMEM],
        out_specs=VMEM,
        compiler_params=params(8),
        cost_estimate=cost(),
        name="element_weights",
    )(mark, data[:8], data[8:32])


def multiply_kernel(mark_ref, values_ref, weights_ref, *refs):
    del mark_ref
    acc_ref, out_ref = refs if len(refs) == 2 else (None,) + refs
    comps, rows, nodes = values_ref.shape
    values = values_ref[...].reshape(comps * rows, nodes)

    def piece(step, carry):
        cut = pl.ds(pl.multiple_of(step * WIDE, WIDE), WIDE)
        for d in range(3):
            term = jnp.dot(values, weights_ref[d, :, cut], preferred_element_type=F32)
            out_ref[d, :, cut] = term if acc_ref is None else term + acc_ref[d, :, cut]
        return carry

    lax.fori_loop(0, out_ref.shape[2] // WIDE, piece, 0)


def multiply(mark, values, weights, acc):
    comps, rows, _ = values.shape
    elems = weights.shape[2]
    args = [mark, values, weights] + ([] if acc is None else [acc])
    return pl.pallas_call(
        multiply_kernel,
        out_shape=shaped((3, comps * rows, elems), F32),
        in_specs=[ANY] + [VMEM] * (len(args) - 1),
        out_specs=VMEM,
        input_output_aliases={} if acc is None else {3: 0},
        compiler_params=params(8),
        cost_estimate=cost(),
        name="multiply",
    )(*args)


def fetch_multiply_kernel(mark_ref, values_ref, weights_ref, acc_ref, out_ref, held, sems):
    del mark_ref
    comps, rows, nodes = values_ref.shape
    values = values_ref[...].reshape(comps * rows, nodes)
    blocks = weights_ref.shape[0]

    def copy(block, slot):
        return pltpu.make_async_copy(weights_ref.at[block], held.at[slot], sems.at[slot])

    for slot in range(2):
        copy(slot, slot).start()

    def pair(twice, carry):
        for slot in range(2):
            block = twice * 2 + slot
            copy(block, slot).wait()
            cut = pl.ds(pl.multiple_of(block * WIDE, WIDE), WIDE)
            for d in range(3):
                term = jnp.dot(values, held[slot, d], preferred_element_type=F32)
                out_ref[d, :, cut] = term + acc_ref[d, :, cut]

            @pl.when(twice < blocks // 2 - 1)
            def _():
                copy(block + 2, slot).start()

        return carry

    lax.fori_loop(0, blocks // 2, pair, 0)


def fetch_multiply(mark, values, weights, acc):
    nodes = values.shape[2]
    return pl.pallas_call(
        fetch_multiply_kernel,
        out_shape=shaped(acc.shape, F32),
        in_specs=[ANY, VMEM, ANY, VMEM],
        out_specs=VMEM,
        input_output_aliases={3: 0},
        scratch_shapes=[pltpu.VMEM((2, 3, nodes, WIDE), BF16), pltpu.SemaphoreType.DMA((2,))],
        compiler_params=params(34),
        cost_estimate=cost(),
        name="fetch_multiply",
    )(mark, values, weights, acc)


def spectra_kernel(before_ref, after_ref, weights_ref, acc_ref, modulus_ref, out_ref, grads):
    comps, rows, rim = before_ref.shape
    half = rows // 4
    groups, _, count = out_ref.shape
    per = count // WIDE
    before = before_ref[...].reshape(comps * rows, rim)
    after = after_ref[...].reshape(comps * rows, rim)

    def finish(group, place, lanes_at, modulus):
        lame = modulus * (POISSON / ((1.0 + POISSON) * (1.0 - 2.0 * POISSON)))
        shear = modulus * (1.0 / (2.0 * (1.0 + POISSON)))
        twice = 2.0 * shear
        lanes = pl.ds(lanes_at, LANES)

        def stress(top):
            def at(c, d):
                return grads[d, c * rows + top : c * rows + top + 8, lanes]

            volume = lame * (at(0, 0) + at(1, 1) + at(2, 2))
            return [
                volume + twice * at(0, 0),
                volume + twice * at(1, 1),
                volume + twice * at(2, 2),
                shear * (at(1, 2) + at(2, 1)),
                shear * (at(2, 0) + at(0, 2)),
                shear * (at(0, 1) + at(1, 0)),
            ]

        pairs = [(i, j, 0) for i in range(6) for j in range(i, 6)]
        pairs += [(i, j, 1) for i in range(6) for j in range(i + 1, 6)]
        totals = [None] * len(pairs)
        for top in [s * 2 * half + p for s in range(2) for p in range(0, half, 8)]:
            re = stress(top)
            im = stress(top + half)
            for n, (i, j, turned) in enumerate(pairs):
                if turned:
                    term = im[i] * re[j] - re[i] * im[j]
                else:
                    term = re[i] * re[j] + im[i] * im[j]
                totals[n] = term if totals[n] is None else totals[n] + term
        for n in range(len(pairs)):
            out_ref[group, pl.ds(n, 1), pl.ds(place, LANES)] = jnp.sum(totals[n], axis=0, keepdims=True)

    def piece(step, carry):
        cut = pl.ds(pl.multiple_of(step * WIDE, WIDE), WIDE)
        for d in range(3):
            grads[d] = (
                acc_ref[d, :, cut]
                + jnp.dot(before, weights_ref[d, :rim, cut], preferred_element_type=F32)
                + jnp.dot(after, weights_ref[d, rim:, cut], preferred_element_type=F32)
            )
        group = step // per
        start = (step % per) * WIDE
        for at in range(0, WIDE, LANES):
            here = pl.ds(pl.multiple_of(step * WIDE + at, LANES), LANES)
            finish(group, pl.multiple_of(start + at, LANES), at, modulus_ref[:1, here])
        return carry

    lax.fori_loop(0, groups * per, piece, 0)


def element_spectra(before, after, weights, acc, modulus):
    comps, rows, rim = before.shape
    elems = weights.shape[2]
    return pl.pallas_call(
        spectra_kernel,
        out_shape=shaped((Z, 36, elems // Z), F32),
        in_specs=[VMEM] * 5,
        out_specs=VMEM,
        scratch_shapes=[pltpu.VMEM((3, comps * rows, WIDE), F32)],
        compiler_params=params(8),
        cost_estimate=cost(),
        name="element_spectra",
    )(before, after, weights, acc, modulus)


def collect_kernel(place_ref, a_ref, b_ref, c_ref, d_ref, out_ref):
    for j, ref in enumerate((a_ref, b_ref, c_ref, d_ref)):
        out_ref[pl.ds((place_ref[0] + Z - j) % Z, 1)] = ref[...][None]


def collect(place, blocks):
    return pl.pallas_call(
        collect_kernel,
        out_shape=shaped((Z,) + blocks[0].shape, F32),
        in_specs=[SMEM] + [VMEM] * Z,
        out_specs=VMEM,
        compiler_params=params(8),
        cost_estimate=cost(),
        name="collect",
    )(place, *blocks)


def local(
    mode_shapes,
    load_nodal,
    mode_freq,
    damping,
    drive_freq,
    send_lists,
    connectivity,
    shape_grads,
    modulus,
):
    modes, _, nodes = mode_shapes.shape
    cols = load_nodal.shape[2]
    bound = send_lists.shape[1]
    freqs = drive_freq.shape[0]
    rows = cols // (Z * XLO)
    mode_at = lax.axis_index("mode")
    z_at, x_at = mode_at // XLO, mode_at % XLO
    core = (lax.axis_index("mesh") % CORE).astype(jnp.int32)
    core_arg = core.reshape(1)
    shapes = jnp.transpose(mode_shapes, (1, 0, 2))
    lists = send_lists.reshape(1, -1)

    pad = 2 * HALF - modes
    natural = jnp.pad(mode_freq, (0, pad), constant_values=1.0)[:, None]
    loss = jnp.pad(damping, (0, pad), constant_values=0.5)[:, None]
    natural = lax.dynamic_slice_in_dim(natural, core * HALF, HALF)
    loss = lax.dynamic_slice_in_dim(loss, core * HALF, HALF)
    forcing = jnp.repeat(drive_freq, cols // freqs)[None, :]
    gap = natural * natural - forcing * forcing
    damp = 2.0 * loss * natural * forcing
    size = gap * gap + damp * damp
    sign = jnp.where(jnp.arange(cols) % 2 == 0, 1.0, -1.0).astype(F32)[None, :]
    direct = gap / size
    cross = sign * (damp / size)

    spot = jnp.arange(cols)
    block, inside = spot // rows, spot % rows
    block = mode_index(z_at + block // XLO, x_at ^ (block % XLO))
    source = block * rows + 2 * (inside % (rows // 2)) + inside // (rows // 2)
    order = (source[:, None] == spot[None, :]).astype(BF16)

    mine, theirs = partial_loads(core_arg, shapes, load_nodal)
    got = lax.ppermute(theirs, "mesh", mesh_perm(0, 0, 1))
    chip = (mine + got.astype(F32)).astype(BF16)
    got = lax.ppermute(chip, "mesh", mesh_perm(0, 1, 0))
    pair = (chip.astype(F32) + got.astype(F32)).astype(BF16)
    ring = [pair] + [lax.ppermute(pair, "mesh", mesh_perm(dy)) for dy in range(1, Y)]

    data = element_data(chip, connectivity, shape_grads, modulus)
    data = jnp.concatenate(
        [data] + [lax.ppermute(data, "mode", mode_perm(-j)) for j in range(1, Z)], axis=1
    )
    up_perm, down_perm, side_perm = mode_perm(1), mode_perm(-1), mode_perm(0, 1)
    up = lambda v: lax.ppermute(v, "mode", up_perm)
    down = lambda v: lax.ppermute(v, "mode", down_perm)
    side = lambda v: lax.ppermute(v, "mode", side_perm)
    full = 2 * rows

    w_0 = nodes * 7 // 16
    w_1 = nodes - w_0
    c_0, c_1 = (0, w_0), (w_0, w_1)
    middle = w_0 + w_1 // 2

    resp_mine = half_response(data, ring, direct, cross)
    resp_theirs = lax.ppermute(resp_mine, "mesh", mesh_perm(0, 0, 1))
    away, keep, resp = x_first_terms(core_arg, resp_mine, resp_theirs, order, shapes, c_0, 43)
    got_0 = side(away)
    ways_1 = z_first_terms(keep, resp, shapes, c_1, 43)
    plus_1, minus_1 = up(ways_1[0]), down(ways_1[1])
    weights_0 = all_weights(ways_1[2], data, w_0)
    on_1 = pass_on(weights_0, ways_1[2], ways_1[3], plus_1, minus_1)
    up_1, down_1 = up(on_1[0]), down(on_1[1])
    ways_0 = x_sum(on_1[0], keep, got_0)
    plus_0, minus_0 = up(ways_0[0]), down(ways_0[1])
    weights_low = element_weights(ways_0[2], data, w_0, w_1 // 2)
    low_1 = half_sum(weights_low, weights_low, 0, ways_1[4], minus_1, up_1)
    side_low = side(low_1)
    high_1 = half_sum(low_1, low_1, 1, ways_1[4], plus_1, down_1)
    side_high = side(high_1)
    weights_high = element_weights(high_1, data, middle, w_1 // 2)
    on_0 = pass_on(weights_high, ways_0[2], ways_0[3], plus_0, minus_0)
    up_0, down_0 = up(on_0[0]), down(on_0[1])
    values_low, rim = gather_rows(on_0[0], lists, low_1, side_low, None, w_0, full)
    acc = multiply(rim, values_low, weights_low, None)
    own_0 = ring_sum(acc, ways_0[4], plus_0, minus_0, up_0, down_0)
    side_0 = side(own_0)
    rim_weights = element_weights(own_0, data, nodes, 2 * bound)
    values_high, rim = gather_rows(rim_weights, lists, high_1, side_high, rim, middle, full)
    acc = multiply(rim, values_high, weights_high, acc)
    values_0, rim = gather_rows(acc, lists, own_0, side_0, rim, 0, full)

    count = lax.axis_size("mesh")
    before = lax.ppermute(rim[..., bound:], "mesh", [(p, p + 1) for p in range(count - 1)])
    after = lax.ppermute(rim[..., :bound], "mesh", [(p + 1, p) for p in range(count - 1)])
    acc = fetch_multiply(rim, values_0, weights_0, acc)
    spectra = element_spectra(before, after, rim_weights, acc, data[32:40])
    back = [spectra[0]] + [lax.ppermute(spectra[j], "mode", mode_perm(j)) for j in range(1, Z)]
    return collect(z_at.astype(jnp.int32).reshape(1), back)


def solution(mesh):
    in_specs = (
        P("mode", None, "mesh"),
        P(None, "mesh", None),
        P("mode"),
        P("mode"),
        P(),
        P(None, "mesh"),
        P(None, ("mesh", "mode")),
        P(None, None, ("mesh", "mode")),
        P(("mesh", "mode")),
    )
    out_specs = P(None, None, ("mesh", "mode"))
    return jax.shard_map(local, mesh=mesh, in_specs=in_specs, out_specs=out_specs, check_vma=False)
```

```python
import functools

import jax
import jax.numpy as jnp
from jax import lax
from jax.experimental import pallas as pl
from jax.experimental.pallas import tpu as pltpu
from jax.sharding import PartitionSpec as P

POISSON = 0.3
F32 = jnp.float32
BF16 = jnp.bfloat16
MIB = 1024 * 1024
Z, XLO = 4, 2
Y, XHI, CORE = 4, 2, 2
HALF = 256
ANY = pl.BlockSpec(memory_space=pl.ANY)
VMEM = pl.BlockSpec(memory_space=pltpu.VMEM)
HBM = pl.BlockSpec(memory_space=pltpu.HBM)
SMEM = pl.BlockSpec(memory_space=pltpu.SMEM)


def params(mib):
    return pltpu.CompilerParams(vmem_limit_bytes=mib * MIB)


def cost(flops=1, moved=1):
    return pl.CostEstimate(flops=flops, bytes_accessed=moved, transcendentals=0)


def shaped(shape, kind):
    return jax.ShapeDtypeStruct(shape, kind)


def mode_index(z, x):
    return (z % Z) * XLO + x


def mesh_index(y, h, c):
    return ((y % Y) * XHI + h) * CORE + c


def mode_perm(dz, flip=0):
    return [(mode_index(z, x), mode_index(z + dz, x ^ flip)) for z in range(Z) for x in range(XLO)]


def mesh_perm(dy, flip_h=0, flip_c=0):
    return [
        (mesh_index(y, h, c), mesh_index(y + dy, h ^ flip_h, c ^ flip_c))
        for y in range(Y)
        for h in range(XHI)
        for c in range(CORE)
    ]


def loads_kernel(cuts, core_ref, shapes_ref, load_ref, mine_ref, theirs_ref, shapes, load, acc, shape_sems, load_sems):
    modes = shapes.shape[1]

    def copies(i):
        c, at, width = cuts[i]
        cut = pl.ds(at, width)
        return (
            pltpu.make_async_copy(shapes_ref.at[c, :, cut], shapes.at[c, :, cut], shape_sems.at[i]),
            pltpu.make_async_copy(load_ref.at[c, cut, :], load.at[c, cut, :], load_sems.at[i]),
        )

    for i in range(len(cuts)):
        for copy in copies(i):
            copy.start()
    acc[modes:, :] = jnp.zeros((acc.shape[0] - modes, acc.shape[1]), F32)
    for i, (c, at, width) in enumerate(cuts):
        for copy in copies(i):
            copy.wait()
        cut = pl.ds(at, width)
        term = jnp.dot(shapes[c, :, cut], load[c, cut, :], preferred_element_type=F32)
        acc[:modes, :] = term if i == 0 else acc[:modes, :] + term
    core = core_ref[0]
    mine_ref[...] = acc[pl.ds(core * HALF, HALF), :]
    theirs_ref[...] = acc[pl.ds((1 - core) * HALF, HALF), :].astype(BF16)


def partial_loads(core, shapes, load):
    comps, modes, nodes = shapes.shape
    cols = load.shape[2]
    block = 1024
    cuts = [(c, at, block) for c in range(comps) for at in range(0, nodes, block)]
    vmem = pl.BlockSpec(memory_space=pltpu.VMEM)
    return pl.pallas_call(
        functools.partial(loads_kernel, cuts),
        out_shape=(shaped((HALF, cols), F32), shaped((HALF, cols), BF16)),
        in_specs=[SMEM, HBM, HBM],
        out_specs=(vmem, vmem),
        scratch_shapes=[
            pltpu.VMEM(shapes.shape, BF16),
            pltpu.VMEM(load.shape, BF16),
            pltpu.VMEM((2 * HALF, cols), F32),
            pltpu.SemaphoreType.DMA((len(cuts),)),
            pltpu.SemaphoreType.DMA((len(cuts),)),
        ],
        compiler_params=params(56),
        cost_estimate=cost(),
        name="modal_loads",
    )(core, shapes, load)


def response_kernel(mark_ref, a_ref, b_ref, c_ref, d_ref, direct_ref, cross_ref, out_ref):
    del mark_ref
    total = (
        a_ref[...].astype(F32)
        + b_ref[...].astype(F32)
        + c_ref[...].astype(F32)
        + d_ref[...].astype(F32)
    )
    cols = total.shape[1]
    even = lax.broadcasted_iota(jnp.int32, total.shape, 1) % 2 == 0
    other = jnp.where(even, pltpu.roll(total, cols - 1, 1), pltpu.roll(total, 1, 1))
    out_ref[...] = (direct_ref[...] * total + cross_ref[...] * other).astype(BF16)


def half_response(mark, parts, direct, cross):
    vmem = pl.BlockSpec(memory_space=pltpu.VMEM)
    return pl.pallas_call(
        response_kernel,
        out_shape=shaped(direct.shape, BF16),
        in_specs=[ANY] + [vmem] * 6,
        out_specs=vmem,
        compiler_params=params(8),
        cost_estimate=cost(),
        name="modal_response",
    )(mark, *parts, direct, cross)


def element_data_kernel(mark_ref, conn_ref, grads_ref, modulus_ref, out_ref):
    del mark_ref
    corners, width = conn_ref.shape
    conn = conn_ref[...].astype(F32)
    out_ref[:corners, :] = conn
    for d in range(3):
        total = jnp.zeros((corners, width), F32)
        for a in range(corners):
            total = total + jnp.where(conn == conn[a : a + 1, :], grads_ref[d, a : a + 1, :], 0.0)
        out_ref[(d + 1) * corners : (d + 2) * corners, :] = total
    out_ref[4 * corners :, :] = jnp.broadcast_to(modulus_ref[...], (corners, width))


def element_data(mark, conn, grads, modulus):
    corners, elems = conn.shape
    vmem = pl.BlockSpec(memory_space=pltpu.VMEM)
    return pl.pallas_call(
        element_data_kernel,
        out_shape=shaped((5 * corners, elems), F32),
        in_specs=[ANY, vmem, vmem, vmem],
        out_specs=vmem,
        compiler_params=params(8),
        cost_estimate=cost(),
        name="element_data",
    )(mark, conn, grads, modulus[None, :])


def split_ways(blocks, plus_ref, minus_ref, up_ref, down_ref, own_ref):
    half = up_ref.shape[-1]
    low = [b[..., :half] for b in blocks]
    high = [b[..., half:] for b in blocks]
    plus_ref[0, 0] = low[2]
    plus_ref[1, 0] = high[1]
    minus_ref[0, 0] = high[2]
    minus_ref[1, 0] = low[3]
    up_ref[0] = low[1]
    down_ref[0] = high[3]
    own_ref[0] = blocks[0]


def way_shapes(comps, rows, width):
    half = width // 2
    shapes = (
        (2, comps, rows, half),
        (2, comps, rows, half),
        (comps, rows, half),
        (comps, rows, half),
        (comps, rows, width),
    )
    specs = tuple(
        pl.BlockSpec((2, 1) + s[2:], lambda i: (0, i, 0, 0))
        if len(s) == 4
        else pl.BlockSpec((1,) + s[1:], lambda i: (i, 0, 0))
        for s in shapes
    )
    return tuple(shaped(s, BF16) for s in shapes), specs


def fetch_shapes(first, shapes_ref, held, sems):
    step = pl.program_id(0)
    cut = pl.ds(first, held.shape[2])

    @pl.when(step == 0)
    def _():
        for c in range(held.shape[0]):
            pltpu.make_async_copy(shapes_ref.at[c, :, cut], held.at[c], sems.at[c]).start()

    pltpu.make_async_copy(shapes_ref.at[step, :, cut], held.at[step], sems.at[step]).wait()
    return held[step]


def fetch_scratch(shapes, width):
    comps, modes, _ = shapes.shape
    return [pltpu.VMEM((comps, modes, width), BF16), pltpu.SemaphoreType.DMA((comps,))]


def z_first_kernel(first, mark_ref, resp_ref, shapes_ref, *refs):
    del mark_ref
    out_refs, (held, sems) = refs[:5], refs[5:]
    part = fetch_shapes(first, shapes_ref, held, sems)
    value = jnp.dot(resp_ref[...], part, preferred_element_type=F32).astype(BF16)
    rows = value.shape[0] // Z
    split_ways([value[j * rows : (j + 1) * rows, :] for j in range(Z)], *out_refs)


def z_first_terms(mark, resp, shapes, chunk, mib):
    first, width = chunk
    comps, modes, _ = shapes.shape
    cols = resp.shape[0]
    out_shape, out_specs = way_shapes(comps, cols // Z, width)
    return pl.pallas_call(
        functools.partial(z_first_kernel, first),
        out_shape=out_shape,
        grid=(comps,),
        in_specs=[ANY, pl.BlockSpec((cols, modes), lambda i: (0, 0)), HBM],
        out_specs=out_specs,
        scratch_shapes=fetch_scratch(shapes, width),
        compiler_params=params(mib),
        cost_estimate=cost(),
        name="z_first_terms",
    )(mark, resp, shapes)


def x_first_kernel(
    first, core_ref, mine_ref, theirs_ref, order_ref, shapes_ref, away_ref, keep_ref, turned_ref, resp, held, sems
):
    modes = shapes_ref.shape[1]
    part = fetch_shapes(first, shapes_ref, held, sems)

    @pl.when(pl.program_id(0) == 0)
    def _():
        core = core_ref[0]
        resp[pl.ds(core * HALF, HALF), :] = mine_ref[...]
        resp[pl.ds((1 - core) * HALF, HALF), :] = theirs_ref[...]
        turned = lax.dot_general(
            order_ref[...], resp[...], (((1,), (1,)), ((), ())), preferred_element_type=F32
        )
        turned_ref[...] = turned[:, :modes].astype(BF16)

    value = jnp.dot(turned_ref[...], part, preferred_element_type=F32).astype(BF16)
    rows = value.shape[0] // (Z * XLO)
    for j in range(Z):
        keep_ref[j, 0] = value[(2 * j) * rows : (2 * j + 1) * rows, :]
        away_ref[j, 0] = value[(2 * j + 1) * rows : (2 * j + 2) * rows, :]


def x_first_terms(core, mine, theirs, order, shapes, chunk, mib):
    first, width = chunk
    comps, modes, _ = shapes.shape
    cols = mine.shape[1]
    rows = cols // (Z * XLO)
    part = pl.BlockSpec((Z, 1, rows, width), lambda i: (0, i, 0, 0))
    whole = lambda i: (0, 0)
    return pl.pallas_call(
        functools.partial(x_first_kernel, first),
        out_shape=(
            shaped((Z, comps, rows, width), BF16),
            shaped((Z, comps, rows, width), BF16),
            shaped((cols, modes), BF16),
        ),
        grid=(comps,),
        in_specs=[
            SMEM,
            pl.BlockSpec((HALF, cols), whole),
            pl.BlockSpec((HALF, cols), whole),
            pl.BlockSpec((cols, cols), whole),
            HBM,
        ],
        out_specs=(part, part, pl.BlockSpec((cols, modes), whole)),
        scratch_shapes=[pltpu.VMEM((2 * HALF, cols), BF16)] + fetch_scratch(shapes, width),
        compiler_params=params(mib),
        cost_estimate=cost(),
        name="x_first_terms",
    )(core, mine, theirs, order, shapes)


def x_sum_kernel(mark_ref, keep_ref, got_ref, *out_refs):
    del mark_ref
    blocks = [(keep_ref[j, 0].astype(F32) + got_ref[j, 0].astype(F32)).astype(BF16) for j in range(Z)]
    split_ways(blocks, *out_refs)


def x_sum(mark, keep, got):
    _, comps, rows, width = keep.shape
    out_shape, out_specs = way_shapes(comps, rows, width)
    part = pl.BlockSpec((Z, 1, rows, width), lambda i: (0, i, 0, 0))
    return pl.pallas_call(
        x_sum_kernel,
        out_shape=out_shape,
        grid=(comps,),
        in_specs=[ANY, part, part],
        out_specs=out_specs,
        compiler_params=params(8),
        cost_estimate=cost(),
        name="x_sum",
    )(mark, keep, got)


def pass_on_kernel(mark_ref, up_ref, down_ref, plus_ref, minus_ref, up_out, down_out):
    del mark_ref
    up_out[...] = (up_ref[...].astype(F32) + plus_ref[0].astype(F32)).astype(BF16)
    down_out[...] = (down_ref[...].astype(F32) + minus_ref[0].astype(F32)).astype(BF16)


def pass_on(mark, up, down, plus, minus):
    comps, rows, half = up.shape
    one = pl.BlockSpec((1, rows, half), lambda i: (i, 0, 0))
    first = pl.BlockSpec((1, 1, rows, half), lambda i: (0, i, 0, 0))
    return pl.pallas_call(
        pass_on_kernel,
        out_shape=(shaped(up.shape, BF16), shaped(up.shape, BF16)),
        grid=(comps,),
        in_specs=[ANY, one, one, first, first],
        out_specs=(one, one),
        compiler_params=params(8),
        cost_estimate=cost(),
        name="pass_on",
    )(mark, up, down, plus, minus)


def ring_sum_kernel(mark_ref, own_ref, plus_ref, minus_ref, up_ref, down_ref, out_ref):
    del mark_ref
    half = up_ref.shape[2]
    low = own_ref[0, :, :half].astype(F32) + minus_ref[0, 0].astype(F32) + up_ref[0].astype(F32)
    high = own_ref[0, :, half:].astype(F32) + plus_ref[0, 0].astype(F32) + down_ref[0].astype(F32)
    out_ref[0, :, :half] = low.astype(BF16)
    out_ref[0, :, half:] = high.astype(BF16)


def ring_sum(mark, own, plus, minus, up, down):
    comps, rows, width = own.shape
    one = lambda n: pl.BlockSpec((1, rows, n), lambda i: (i, 0, 0))
    second = pl.BlockSpec((1, 1, rows, width // 2), lambda i: (1, i, 0, 0))
    return pl.pallas_call(
        ring_sum_kernel,
        out_shape=shaped(own.shape, BF16),
        grid=(comps,),
        in_specs=[ANY, one(width), second, second, one(width // 2), one(width // 2)],
        out_specs=one(width),
        compiler_params=params(8),
        cost_estimate=cost(),
        name="ring_sum",
    )(mark, own, plus, minus, up, down)


def half_sum_kernel(mark_ref, after_ref, own_ref, direct_ref, passed_ref, out_ref):
    del mark_ref, after_ref
    total = own_ref[...].astype(F32) + direct_ref[0].astype(F32) + passed_ref[...].astype(F32)
    out_ref[...] = total.astype(BF16)


def half_sum(mark, after, side, own, direct, passed):
    comps, rows, half = passed.shape
    one = pl.BlockSpec((1, rows, half), lambda i: (i, 0, 0))
    return pl.pallas_call(
        half_sum_kernel,
        out_shape=shaped(passed.shape, BF16),
        grid=(comps,),
        in_specs=[
            ANY,
            ANY,
            pl.BlockSpec((1, rows, half), lambda i: (i, 0, side)),
            pl.BlockSpec((1, 1, rows, half), lambda i: (1, i, 0, 0)),
            one,
        ],
        out_specs=one,
        compiler_params=params(8),
        cost_estimate=cost(),
        name="half_sum",
    )(mark, after, own, direct, passed)


def gather_rows_kernel(first, mark_ref, lists_ref, own_ref, got_ref, *refs):
    del mark_ref
    rim_in_ref, out_ref, rim_ref = refs if len(refs) == 3 else (None,) + refs
    rows = own_ref.shape[1]
    width = own_ref.shape[2]
    if rows == out_ref.shape[1]:
        half = rows // 2
        own = own_ref[0].astype(F32)
        got = got_ref[0].astype(F32)
        out_ref[0, :half, :] = (own[:half] + got[half:]).astype(BF16)
        out_ref[0, half:, :] = (own[half:] + got[:half]).astype(BF16)
    else:
        out_ref[0, :rows, :] = own_ref[0]
        out_ref[0, rows:, :] = got_ref[0]
    node = lax.broadcasted_iota(jnp.int32, (width, lists_ref.shape[1]), 0)
    pick = jnp.where(node == lists_ref[...] - first, 1.0, 0.0).astype(BF16)
    rim = jnp.dot(out_ref[0], pick, preferred_element_type=F32)
    if rim_in_ref is not None:
        rim = rim + rim_in_ref[0].astype(F32)
    rim_ref[0] = rim.astype(BF16)


def gather_rows(mark, lists, own, got, rim, first, full):
    comps, rows, width = own.shape
    count = lists.shape[1]
    one = lambda r, n: pl.BlockSpec((1, r, n), lambda i: (i, 0, 0))
    specs = [ANY, pl.BlockSpec((1, count), lambda i: (0, 0)), one(rows, width), one(rows, width)]
    args = [mark, lists, own, got]
    if rim is not None:
        specs.append(one(full, count))
        args.append(rim)
    return pl.pallas_call(
        functools.partial(gather_rows_kernel, first),
        out_shape=(shaped((comps, full, width), BF16), shaped((comps, full, count), BF16)),
        grid=(comps,),
        in_specs=specs,
        out_specs=(one(full, width), one(full, count)),
        compiler_params=params(8),
        cost_estimate=cost(),
        name="gather_rows",
    )(*args)


NODE_BLOCK = 256
WIDE = 256
ROWS = 16
LANES = 128


def build_tiles(first, nodes, conn, grads, store):
    corners = conn.shape[0]
    base = lax.broadcasted_iota(jnp.int32, (ROWS, LANES), 0).astype(F32).astype(BF16)
    zero = jnp.zeros((ROWS, LANES), BF16)
    grads = grads.astype(BF16)
    grad = [jnp.broadcast_to(grads[i : i + 1, :], (ROWS, LANES)) for i in range(3 * corners)]
    for at in range(0, nodes, NODE_BLOCK):
        keys = (conn - (first + at)).astype(BF16)
        key = [jnp.broadcast_to(keys[a : a + 1, :], (ROWS, LANES)) for a in range(corners)]
        for row in range(0, min(NODE_BLOCK, nodes - at), ROWS):
            node = base + BF16(row)
            sums = [zero] * 3
            for a in range(corners):
                hit = node == key[a]
                for d in range(3):
                    sums[d] = jnp.where(hit, grad[d * corners + a], sums[d])
            for d in range(3):
                store(d, at + row, sums[d])


def weights_kernel(first, mark_ref, conn_ref, grads_ref, out_ref):
    del mark_ref

    def piece(step, carry):
        cut = pl.ds(pl.multiple_of(step * LANES, LANES), LANES)

        def store(d, row, value):
            out_ref[d, pl.ds(row, ROWS), cut] = value

        build_tiles(first, out_ref.shape[1], conn_ref[:, cut], grads_ref[:, cut], store)
        return carry

    lax.fori_loop(0, conn_ref.shape[1] // LANES, piece, 0)


def all_weights_kernel(mark_ref, conn_ref, grads_ref, out_ref, made, sems):
    del mark_ref
    blocks = out_ref.shape[0]
    slots, _, count, wide = made.shape
    parts = slots

    def copies(block, part, slot):
        rows = pl.ds(part * count, count)
        return [
            pltpu.make_async_copy(made.at[slot, d], out_ref.at[block, d, rows, :], sems.at[slot, d])
            for d in range(3)
        ]

    def block_of_elements(block, carry):
        for part in range(parts):
            slot = part % slots

            @pl.when(block > 0)
            def _():
                for copy in copies(block - 1, part, slot):
                    copy.wait()

            for lane in range(0, wide, LANES):
                cut = pl.ds(pl.multiple_of(block * wide + lane, LANES), LANES)

                def store(d, row, value):
                    made[slot, d, pl.ds(row, ROWS), pl.ds(lane, LANES)] = value

                build_tiles(float(part * count), count, conn_ref[:, cut], grads_ref[:, cut], store)
            for copy in copies(block, part, slot):
                copy.start()
        return carry

    lax.fori_loop(0, blocks, block_of_elements, 0)
    for part in range(parts):
        for copy in copies(blocks - 1, part, part):
            copy.wait()


def all_weights(mark, data, nodes, room):
    elems = data.shape[1]
    slots = 4
    count = nodes // slots
    return pl.pallas_call(
        all_weights_kernel,
        out_shape=shaped((elems // WIDE, 3, room, WIDE), BF16),
        in_specs=[ANY, VMEM, VMEM],
        out_specs=ANY,
        scratch_shapes=[pltpu.VMEM((slots, 3, count, WIDE), BF16), pltpu.SemaphoreType.DMA((slots, 3))],
        compiler_params=params(16),
        cost_estimate=cost(),
        name="all_weights",
    )(mark, data[:8], data[8:32])


def element_weights(mark, data, first, count):
    elems = data.shape[1]
    return pl.pallas_call(
        functools.partial(weights_kernel, float(first)),
        out_shape=shaped((3, count, elems), BF16),
        in_specs=[ANY, VMEM, VMEM],
        out_specs=VMEM,
        compiler_params=params(8),
        cost_estimate=cost(),
        name="element_weights",
    )(mark, data[:8], data[8:32])


def multiply_kernel(mark_ref, values_ref, weights_ref, *refs):
    del mark_ref
    acc_ref, out_ref = refs if len(refs) == 2 else (None,) + refs
    comps, rows, nodes = values_ref.shape
    values = values_ref[...].reshape(comps * rows, nodes)

    def piece(step, carry):
        cut = pl.ds(pl.multiple_of(step * WIDE, WIDE), WIDE)
        for d in range(3):
            term = jnp.dot(values, weights_ref[d, :, cut], preferred_element_type=F32)
            out_ref[d, :, cut] = term if acc_ref is None else term + acc_ref[d, :, cut]
        return carry

    lax.fori_loop(0, out_ref.shape[2] // WIDE, piece, 0)


def multiply(mark, values, weights, acc):
    comps, rows, _ = values.shape
    elems = weights.shape[2]
    args = [mark, values, weights] + ([] if acc is None else [acc])
    return pl.pallas_call(
        multiply_kernel,
        out_shape=shaped((3, comps * rows, elems), F32),
        in_specs=[ANY] + [VMEM] * (len(args) - 1),
        out_specs=VMEM,
        input_output_aliases={} if acc is None else {3: 0},
        compiler_params=params(8),
        cost_estimate=cost(),
        name="multiply",
    )(*args)


def fetch_multiply_kernel(mark_ref, values_ref, weights_ref, acc_ref, out_ref, held, sems):
    del mark_ref
    comps, rows, nodes = values_ref.shape
    values = values_ref[...].reshape(comps * rows, nodes)
    blocks = weights_ref.shape[0]

    def copy(block, slot):
        rows = pl.ds(0, nodes)
        return pltpu.make_async_copy(weights_ref.at[block, :, rows, :], held.at[slot], sems.at[slot])

    for slot in range(2):
        copy(slot, slot).start()

    def pair(twice, carry):
        for slot in range(2):
            block = twice * 2 + slot
            copy(block, slot).wait()
            cut = pl.ds(pl.multiple_of(block * WIDE, WIDE), WIDE)
            for d in range(3):
                term = jnp.dot(values, held[slot, d], preferred_element_type=F32)
                out_ref[d, :, cut] = term + acc_ref[d, :, cut]

            @pl.when(twice < blocks // 2 - 1)
            def _():
                copy(block + 2, slot).start()

        return carry

    lax.fori_loop(0, blocks // 2, pair, 0)


def fetch_multiply(mark, values, weights, acc):
    nodes = values.shape[2]
    return pl.pallas_call(
        fetch_multiply_kernel,
        out_shape=shaped(acc.shape, F32),
        in_specs=[ANY, VMEM, ANY, VMEM],
        out_specs=VMEM,
        input_output_aliases={3: 0},
        scratch_shapes=[pltpu.VMEM((2, 3, nodes, WIDE), BF16), pltpu.SemaphoreType.DMA((2,))],
        compiler_params=params(20),
        cost_estimate=cost(),
        name="fetch_multiply",
    )(mark, values, weights, acc)


def spectra_kernel(before_ref, after_ref, weights_ref, acc_ref, modulus_ref, out_ref, grads):
    comps, rows, rim = before_ref.shape
    half = rows // 4
    groups, _, count = out_ref.shape
    per = count // WIDE
    before = before_ref[...].reshape(comps * rows, rim)
    after = after_ref[...].reshape(comps * rows, rim)

    def finish(group, place, lanes_at, modulus):
        lame = modulus * (POISSON / ((1.0 + POISSON) * (1.0 - 2.0 * POISSON)))
        shear = modulus * (1.0 / (2.0 * (1.0 + POISSON)))
        twice = 2.0 * shear
        lanes = pl.ds(lanes_at, LANES)

        def stress(top):
            def at(c, d):
                return grads[d, c * rows + top : c * rows + top + 8, lanes]

            volume = lame * (at(0, 0) + at(1, 1) + at(2, 2))
            return [
                volume + twice * at(0, 0),
                volume + twice * at(1, 1),
                volume + twice * at(2, 2),
                shear * (at(1, 2) + at(2, 1)),
                shear * (at(2, 0) + at(0, 2)),
                shear * (at(0, 1) + at(1, 0)),
            ]

        pairs = [(i, j, 0) for i in range(6) for j in range(i, 6)]
        pairs += [(i, j, 1) for i in range(6) for j in range(i + 1, 6)]
        totals = [None] * len(pairs)
        for top in [s * 2 * half + p for s in range(2) for p in range(0, half, 8)]:
            re = stress(top)
            im = stress(top + half)
            for n, (i, j, turned) in enumerate(pairs):
                if turned:
                    term = im[i] * re[j] - re[i] * im[j]
                else:
                    term = re[i] * re[j] + im[i] * im[j]
                totals[n] = term if totals[n] is None else totals[n] + term
        for n in range(len(pairs)):
            out_ref[group, pl.ds(n, 1), pl.ds(place, LANES)] = jnp.sum(totals[n], axis=0, keepdims=True)

    def piece(step, carry):
        cut = pl.ds(pl.multiple_of(step * WIDE, WIDE), WIDE)
        for d in range(3):
            grads[d] = (
                acc_ref[d, :, cut]
                + jnp.dot(before, weights_ref[d, :rim, cut], preferred_element_type=F32)
                + jnp.dot(after, weights_ref[d, rim:, cut], preferred_element_type=F32)
            )
        group = step // per
        start = (step % per) * WIDE
        for at in range(0, WIDE, LANES):
            here = pl.ds(pl.multiple_of(step * WIDE + at, LANES), LANES)
            finish(group, pl.multiple_of(start + at, LANES), at, modulus_ref[:1, here])
        return carry

    lax.fori_loop(0, groups * per, piece, 0)


def element_spectra(before, after, weights, acc, modulus):
    comps, rows, rim = before.shape
    elems = weights.shape[2]
    return pl.pallas_call(
        spectra_kernel,
        out_shape=shaped((Z, 36, elems // Z), F32),
        in_specs=[VMEM] * 5,
        out_specs=VMEM,
        scratch_shapes=[pltpu.VMEM((3, comps * rows, WIDE), F32)],
        compiler_params=params(8),
        cost_estimate=cost(),
        name="element_spectra",
    )(before, after, weights, acc, modulus)


def collect_kernel(place_ref, a_ref, b_ref, c_ref, d_ref, out_ref):
    for j, ref in enumerate((a_ref, b_ref, c_ref, d_ref)):
        out_ref[pl.ds((place_ref[0] + Z - j) % Z, 1)] = ref[...][None]


def collect(place, blocks):
    return pl.pallas_call(
        collect_kernel,
        out_shape=shaped((Z,) + blocks[0].shape, F32),
        in_specs=[SMEM] + [VMEM] * Z,
        out_specs=VMEM,
        compiler_params=params(8),
        cost_estimate=cost(),
        name="collect",
    )(place, *blocks)


def local(
    mode_shapes,
    load_nodal,
    mode_freq,
    damping,
    drive_freq,
    send_lists,
    connectivity,
    shape_grads,
    modulus,
):
    modes, _, nodes = mode_shapes.shape
    cols = load_nodal.shape[2]
    bound = send_lists.shape[1]
    freqs = drive_freq.shape[0]
    rows = cols // (Z * XLO)
    mode_at = lax.axis_index("mode")
    z_at, x_at = mode_at // XLO, mode_at % XLO
    core = (lax.axis_index("mesh") % CORE).astype(jnp.int32)
    core_arg = core.reshape(1)
    shapes = jnp.transpose(mode_shapes, (1, 0, 2))
    lists = send_lists.reshape(1, -1)

    pad = 2 * HALF - modes
    natural = jnp.pad(mode_freq, (0, pad), constant_values=1.0)[:, None]
    loss = jnp.pad(damping, (0, pad), constant_values=0.5)[:, None]
    natural = lax.dynamic_slice_in_dim(natural, core * HALF, HALF)
    loss = lax.dynamic_slice_in_dim(loss, core * HALF, HALF)
    forcing = jnp.repeat(drive_freq, cols // freqs)[None, :]
    gap = natural * natural - forcing * forcing
    damp = 2.0 * loss * natural * forcing
    size = gap * gap + damp * damp
    sign = jnp.where(jnp.arange(cols) % 2 == 0, 1.0, -1.0).astype(F32)[None, :]
    direct = gap / size
    cross = sign * (damp / size)

    spot = jnp.arange(cols)
    block, inside = spot // rows, spot % rows
    block = mode_index(z_at + block // XLO, x_at ^ (block % XLO))
    source = block * rows + 2 * (inside % (rows // 2)) + inside // (rows // 2)
    order = (source[:, None] == spot[None, :]).astype(BF16)

    mine, theirs = partial_loads(core_arg, shapes, load_nodal)
    got = lax.ppermute(theirs, "mesh", mesh_perm(0, 0, 1))
    chip = (mine + got.astype(F32)).astype(BF16)
    got = lax.ppermute(chip, "mesh", mesh_perm(0, 1, 0))
    pair = (chip.astype(F32) + got.astype(F32)).astype(BF16)
    ring = [pair] + [lax.ppermute(pair, "mesh", mesh_perm(dy)) for dy in range(1, Y)]

    data = element_data(chip, connectivity, shape_grads, modulus)
    data = jnp.concatenate(
        [data] + [lax.ppermute(data, "mode", mode_perm(-j)) for j in range(1, Z)], axis=1
    )
    up_perm, down_perm, side_perm = mode_perm(1), mode_perm(-1), mode_perm(0, 1)
    up = lambda v: lax.ppermute(v, "mode", up_perm)
    down = lambda v: lax.ppermute(v, "mode", down_perm)
    side = lambda v: lax.ppermute(v, "mode", side_perm)
    full = 2 * rows

    w_0 = nodes * 7 // 16
    w_1 = nodes - w_0
    c_0, c_1 = (0, w_0), (w_0, w_1)
    middle = w_0 + w_1 // 2

    resp_mine = half_response(data, ring, direct, cross)
    resp_theirs = lax.ppermute(resp_mine, "mesh", mesh_perm(0, 0, 1))
    away, keep, resp = x_first_terms(core_arg, resp_mine, resp_theirs, order, shapes, c_0, 43)
    got_0 = side(away)
    ways_1 = z_first_terms(keep, resp, shapes, c_1, 43)
    plus_1, minus_1 = up(ways_1[0]), down(ways_1[1])
    weights_0 = all_weights(ways_1[2], data, w_0, nodes)
    on_1 = pass_on(weights_0, ways_1[2], ways_1[3], plus_1, minus_1)
    up_1, down_1 = up(on_1[0]), down(on_1[1])
    ways_0 = x_sum(on_1[0], keep, got_0)
    plus_0, minus_0 = up(ways_0[0]), down(ways_0[1])
    weights_low = element_weights(ways_0[2], data, w_0, w_1 // 2)
    low_1 = half_sum(weights_low, weights_low, 0, ways_1[4], minus_1, up_1)
    side_low = side(low_1)
    high_1 = half_sum(low_1, low_1, 1, ways_1[4], plus_1, down_1)
    side_high = side(high_1)
    weights_high = element_weights(high_1, data, middle, w_1 // 2)
    on_0 = pass_on(weights_high, ways_0[2], ways_0[3], plus_0, minus_0)
    up_0, down_0 = up(on_0[0]), down(on_0[1])
    values_low, rim = gather_rows(on_0[0], lists, low_1, side_low, None, w_0, full)
    acc = multiply(rim, values_low, weights_low, None)
    own_0 = ring_sum(acc, ways_0[4], plus_0, minus_0, up_0, down_0)
    side_0 = side(own_0)
    rim_weights = element_weights(own_0, data, nodes, 2 * bound)
    values_high, rim = gather_rows(rim_weights, lists, high_1, side_high, rim, middle, full)
    acc = multiply(rim, values_high, weights_high, acc)
    values_0, rim = gather_rows(acc, lists, own_0, side_0, rim, 0, full)

    count = lax.axis_size("mesh")
    before = lax.ppermute(rim[..., bound:], "mesh", [(p, p + 1) for p in range(count - 1)])
    after = lax.ppermute(rim[..., :bound], "mesh", [(p + 1, p) for p in range(count - 1)])
    acc = fetch_multiply(rim, values_0, weights_0, acc)
    spectra = element_spectra(before, after, rim_weights, acc, data[32:40])
    back = [spectra[0]] + [lax.ppermute(spectra[j], "mode", mode_perm(j)) for j in range(1, Z)]
    return collect(z_at.astype(jnp.int32).reshape(1), back)


def solution(mesh):
    in_specs = (
        P("mode", None, "mesh"),
        P(None, "mesh", None),
        P("mode"),
        P("mode"),
        P(),
        P(None, "mesh"),
        P(None, ("mesh", "mode")),
        P(None, None, ("mesh", "mode")),
        P(("mesh", "mode")),
    )
    out_specs = P(None, None, ("mesh", "mode"))
    return jax.shard_map(local, mesh=mesh, in_specs=in_specs, out_specs=out_specs, check_vma=False)
```
